32 devices in a mesh: dp: 8 (over z, x), grp: 4 (over y, core).
Axes of the slice: x: 2, y: 2, z: 4, core: 2. Of those that a mesh axis runs over, the one named last changes fastest.
Arguments:
- tokens: bfloat16 [8, 1024, 960], P('dp', 'grp'), may hold values from -6 to 6
- cotangent: bfloat16 [8, 1024, 960], P('dp', 'grp')
- segments: int32 [8, 1024], P('dp'), may hold values from 0 to 2, as said below
- positions: int32 [8, 1024], P('dp', 'grp'), may hold values from 0 to 1923, as said below
- w_qkv: float32 [960, 1600], P('grp', 'dp'), may hold values from -0.1875 to 0.1875
- m_qkv: float32 [960, 1600], P('grp', 'dp'), may hold values from -192 to 192
- v_qkv: float32 [960, 1600], P('grp', 'dp'), may hold values from 3850.24 to 15564.8
- w_out: float32 [960, 960], P('grp', 'dp'), may hold values from -1.5 to 1.5
- m_out: float32 [960, 960], P('grp', 'dp'), may hold values from -32 to 32
- v_out: float32 [960, 960], P('grp', 'dp'), may hold values from 155.648 to 622.592
- w_in: float32 [2, 960, 2560], P(None, 'grp', 'dp'), may hold values from -0.1875 to 0.1875
- m_in: float32 [2, 960, 2560], P(None, 'grp', 'dp'), may hold values from -64 to 64
- v_in: float32 [2, 960, 2560], P(None, 'grp', 'dp'), may hold values from 622.592 to 2457.6
- w_down: float32 [2560, 960], P('grp', 'dp'), may hold values from -0.125 to 0.125
- m_down: float32 [2560, 960], P('grp', 'dp'), may hold values from -128 to 128
- v_down: float32 [2560, 960], P('grp', 'dp'), may hold values from 1720.32 to 6881.28
- gains: float32 [2, 960], replicated, may hold values from 0.5 to 1.5
- m_gains: float32 [2, 960], replicated, may hold values from -256 to 256
- v_gains: float32 [2, 960], replicated, may hold values from 6881.28 to 27852.8
Outputs:
- layer_out: float32 [8, 1024, 960], P('dp', 'grp')
- tokens_grad: float32 [8, 1024, 960], P('dp', 'grp')
- new_qkv: float32 [960, 1600], P('grp', 'dp')
- mom_qkv: float32 [960, 1600], P('grp', 'dp')
- sq_qkv: float32 [960, 1600], P('grp', 'dp')
- new_out: float32 [960, 960], P('grp', 'dp')
- mom_out: float32 [960, 960], P('grp', 'dp')
- sq_out: float32 [960, 960], P('grp', 'dp')
- new_in: float32 [2, 960, 2560], P(None, 'grp', 'dp')
- mom_in: float32 [2, 960, 2560], P(None, 'grp', 'dp')
- sq_in: float32 [2, 960, 2560], P(None, 'grp', 'dp')
- new_down: float32 [2560, 960], P('grp', 'dp')
- mom_down: float32 [2560, 960], P('grp', 'dp')
- sq_down: float32 [2560, 960], P('grp', 'dp')
- new_gains: float32 [2, 960], replicated
- mom_gains: float32 [2, 960], replicated
- sq_gains: float32 [2, 960], replicated
The draws below stay inside these ranges and needn't reach their ends.
Inputs may be any that keep to these rules, and one draw needn't show every extreme that they name: `segments`: in each sequence the numbers never fall and are 0, 1, 2 in turn; document 1 begins within the first 256 tokens and ends within the last 256 tokens, so it reaches every piece of the sequence. Within a document positions rise by one from token to token; documents 1 and 2 begin at position 0; document 0 continues from an earlier position, and its last token stands at position 1923.
All inputs are finite; a program needn't handle non-finite values.
Results may differ from the reference program's by a relative error of at most 0.013.
Values may be sent and summed in bfloat16 or wider, within the bound.
No kernel may reach another device: no remote copies, remote signals or barrier semaphores. Data moves between devices by JAX's collectives and lax.ppermute only.
A program may use at most 384 MiB of HBM per device.

```python
import math
from functools import partial
import jax
import jax.numpy as jnp
from jax import lax

D = 960
QUERY_HEADS = 15
KEY_VALUE_HEADS = 5
HEAD_SIZE = 64
FF = 2560
STEP = 10
SEQ = 1024
TOK_DEV = 256
SEQS = 8
QKV = 1600


def document_bounds(key):
    starts = jax.random.randint(jax.random.fold_in(key, 11), (SEQS,), 1, TOK_DEV)
    finish = jax.random.randint(jax.random.fold_in(key, 12), (SEQS,), SEQ - TOK_DEV + 1, SEQ)
    places = jnp.arange(SEQ, dtype=jnp.int32)[None, :]
    segment = (places >= starts[:, None]).astype(jnp.int32) + (places >= finish[:, None]).astype(jnp.int32)
    return (segment, places, starts, finish)


def draw_segments(key, part):
    segment = document_bounds(key)[0]
    return segment.astype(jnp.int32)


def draw_positions(key, part):
    segment, places, starts, finish = document_bounds(key)
    first_begin = starts[:, None] - 1 - (SEQ + 899)
    begins = jnp.where(segment == 0, first_begin, jnp.where(segment == 1, starts[:, None], finish[:, None]))
    return (places - begins).astype(jnp.int32)


def draw_cotangent(key, part):
    key = jax.random.fold_in(key, 5)
    position_ramp = jnp.arange(SEQS * SEQ, dtype=jnp.float32).reshape(SEQS, SEQ, 1) / (SEQS * SEQ - 1)
    values_drawn = jax.random.normal(key, (SEQS, SEQ, D), jnp.float32)
    scaling = 1.0 + 2.0 * position_ramp
    return (values_drawn * scaling).astype(jnp.bfloat16)


def block_scale(own_key, dims, shards, least, top_value):
    def one(axis_at, blocks):
        steps = jax.random.uniform(jax.random.fold_in(jax.random.fold_in(own_key, 6), axis_at), (blocks,), jnp.float32, least / len(shards), top_value / len(shards))
        return jnp.repeat(jnp.exp(steps), dims[axis_at] // blocks).reshape((-1,) + (1,) * (len(dims) - axis_at - 1))

    level = one(*shards[0])
    for cut in shards[1:]:
        level = level * one(*cut)
    return level


def noise(key, shape, scale, limit, shards=(), held_as=jnp.bfloat16):
    drawn = jax.random.normal(key, shape, jnp.float32) * scale
    if len(shards) > 0:
        drawn = block_scale(key, shape, shards, -0.22, 0.18) * drawn
    return jnp.clip(drawn, min=-limit, max=limit).astype(held_as)


def setup_inputs(seed: int = 0) -> dict:
    splits = jax.random.split(jax.random.key(seed), 20)
    tokens = noise(splits[0], (SEQS, SEQ, D), 1.0, 6.0, ((0, 8), (1, 4)))
    cotangent = draw_cotangent(jax.random.fold_in(splits[19], 71), 0)
    segments = draw_segments(jax.random.fold_in(splits[19], 71), 0)
    positions = draw_positions(jax.random.fold_in(splits[19], 71), 0)
    w_qkv = noise(splits[4], (D, QKV), D ** -0.5, 0.1875, ((0, 4), (1, 8)), jnp.float32)
    m_qkv = noise(splits[5], (D, QKV), (0.333 * (SEQS * SEQ) ** 0.5), 192.0, ((0, 4), (1, 8)), jnp.float32)
    v_qkv = jnp.clip(jnp.exp(math.log(15564.8) - 1.3968765 * jax.random.uniform(splits[6], (D, QKV), jnp.float32) ** block_scale(splits[6], (D, QKV), ((0, 4), (1, 8)), -0.2, 0.2)), 3850.24, 15564.8)
    w_out = noise(splits[7], (QUERY_HEADS * HEAD_SIZE, D), (max(D // 64, 4)) ** -0.5, 1.5, ((0, 4), (1, 8)), jnp.float32)
    m_out = noise(splits[8], (QUERY_HEADS * HEAD_SIZE, D), (0.067 * (SEQS * SEQ) ** 0.5), 32.0, ((0, 4), (1, 8)), jnp.float32)
    v_out = jnp.clip(jnp.exp(math.log(622.592) - 1.3862944 * jax.random.uniform(splits[9], (QUERY_HEADS * HEAD_SIZE, D), jnp.float32) ** block_scale(splits[9], (QUERY_HEADS * HEAD_SIZE, D), ((0, 4), (1, 8)), -0.2, 0.2)), 155.648, 622.592)
    w_in = noise(splits[10], (2, D, FF), D ** -0.5, 0.1875, ((1, 4), (2, 8)), jnp.float32)
    m_in = noise(splits[11], (2, D, FF), (0.133 * (SEQS * SEQ) ** 0.5), 64.0, ((1, 4), (2, 8)), jnp.float32)
    v_in = jnp.clip(jnp.exp(math.log(2457.6) - 1.3730492 * jax.random.uniform(splits[12], (2, D, FF), jnp.float32) ** block_scale(splits[12], (2, D, FF), ((1, 4), (2, 8)), -0.2, 0.2)), 622.592, 2457.6)
    w_down = noise(splits[13], (FF, D), FF ** -0.5, 0.125, ((0, 4), (1, 8)), jnp.float32)
    m_down = noise(splits[14], (FF, D), (0.222 * (SEQS * SEQ) ** 0.5), 128.0, ((0, 4), (1, 8)), jnp.float32)
    v_down = jnp.clip(jnp.exp(math.log(6881.28) - 1.3862944 * jax.random.uniform(splits[15], (FF, D), jnp.float32) ** block_scale(splits[15], (FF, D), ((0, 4), (1, 8)), -0.2, 0.2)), 1720.32, 6881.28)
    gains = jnp.clip(1.0 + 0.1 * jax.random.normal(splits[16], (2, D), jnp.float32), 0.5, 1.5)
    m_gains = noise(splits[17], (2, D), (0.444 * (SEQS * SEQ) ** 0.5), 256.0, (), jnp.float32)
    v_gains = jnp.clip(jnp.exp(jax.random.uniform(splits[18], (2, D), jnp.float32, math.log(6881.28), math.log(27852.8))), 6881.28, 27852.8)
    return {"tokens": tokens, "cotangent": cotangent, "segments": segments, "positions": positions, "w_qkv": w_qkv, "m_qkv": m_qkv, "v_qkv": v_qkv, "w_out": w_out, "m_out": m_out, "v_out": v_out, "w_in": w_in, "m_in": m_in, "v_in": v_in, "w_down": w_down, "m_down": m_down, "v_down": v_down, "gains": gains, "m_gains": m_gains, "v_gains": v_gains}


NORM_EPS = 1e-05
ROPE_BASE = 10000.0
MASKED = -1e+30
BETA_FIRST = 0.9
BETA_SECOND = 0.95
ADAM_EPS = 1e-08
WEIGHT_DECAY = 0.1
RATE_MATRIX = 0.05
RATE_GAIN = 0.3
HIGHEST = lax.Precision.HIGHEST

@jax.custom_vjp
def reduced_precision(v):
    return lax.optimization_barrier(v.astype(jnp.bfloat16)).astype(jnp.float32)

@jax.custom_vjp
def low_back(v):
    return v

def low_keep(v):
    return (reduced_precision(v), None)

def low_pass(kept, grad):
    return (grad,)

def back_keep(v):
    return (v, None)

def back_low(kept, grad):
    return (reduced_precision(grad),)
reduced_precision.defvjp(low_keep, low_pass)
low_back.defvjp(back_keep, back_low)

def rms_norm(hidden, gain_row):
    factor = lax.rsqrt(lax.optimization_barrier(jnp.mean(hidden * hidden, axis=-1, keepdims=True)) + NORM_EPS)
    return hidden * factor * gain_row

def rotation(places_in_doc):
    frequency = ROPE_BASE ** (-(jnp.arange(HEAD_SIZE // 2).astype(jnp.float32) * 2.0 / HEAD_SIZE))
    angles = places_in_doc.astype(jnp.float32)[:, None] * frequency[None, :]
    return (jnp.cos(angles)[:, None, :], jnp.sin(angles)[:, None, :])

def apply_rotary(head_rows, rotary_cosine, rotary_sine):
    half_width = head_rows.shape[-1] // 2
    front_half = head_rows[..., :half_width]
    back_half = head_rows[..., half_width:]
    return jnp.concatenate([front_half * rotary_cosine - back_half * rotary_sine, back_half * rotary_cosine + front_half * rotary_sine], axis=-1)

def head_block(allowed, operands):
    query_block, key_block, value_block = operands
    raw_scores = jnp.einsum('rtd,sd->rts', query_block, key_block, precision=HIGHEST) * HEAD_SIZE ** (-0.5)
    raw_scores = low_back(raw_scores)
    masked = jnp.where(allowed[None], raw_scores, MASKED)
    probability = reduced_precision(jax.nn.softmax(masked, axis=-1))
    return jnp.einsum('rts,sd->rtd', probability, value_block, precision=HIGHEST)

def block_forward(inputs, weight_qkv, weight_out, weight_in, weight_down, gain_pair, seq_segments, seq_positions):
    token_length = inputs.shape[0]
    group_count = QUERY_HEADS // KEY_VALUE_HEADS
    rotary_cosine, rotary_sine = rotation(seq_positions)
    places = jnp.arange(token_length)
    allowed = (places[None, :] <= places[:, None]) & (seq_segments[None, :] == seq_segments[:, None])
    normed = reduced_precision(rms_norm(inputs, gain_pair[0]))
    blended_rows = low_back(jnp.einsum('tc,cq->tq', normed, reduced_precision(weight_qkv), precision=HIGHEST))
    query_rows = reduced_precision(apply_rotary(blended_rows[:, :QUERY_HEADS * HEAD_SIZE].reshape(token_length, QUERY_HEADS, HEAD_SIZE), rotary_cosine, rotary_sine))
    rows_of_keys = reduced_precision(apply_rotary(blended_rows[:, QUERY_HEADS * HEAD_SIZE:(QUERY_HEADS + KEY_VALUE_HEADS) * HEAD_SIZE].reshape(token_length, KEY_VALUE_HEADS, HEAD_SIZE), rotary_cosine, rotary_sine))
    rows_of_values = reduced_precision(blended_rows[:, (QUERY_HEADS + KEY_VALUE_HEADS) * HEAD_SIZE:].reshape(token_length, KEY_VALUE_HEADS, HEAD_SIZE))
    grouped_heads = query_rows.reshape(token_length, KEY_VALUE_HEADS, group_count, HEAD_SIZE).transpose(1, 2, 0, 3)
    attended = lax.map(jax.checkpoint(partial(head_block, allowed)), (grouped_heads, rows_of_keys.transpose(1, 0, 2), rows_of_values.transpose(1, 0, 2)))
    attended = attended.transpose(2, 0, 1, 3).reshape(token_length, QUERY_HEADS * HEAD_SIZE)
    attended = low_back(reduced_precision(attended))
    branch = low_back(jnp.einsum('ta,ad->td', attended, reduced_precision(weight_out), precision=HIGHEST))
    middle = inputs + branch
    normed_two = reduced_precision(rms_norm(middle, gain_pair[1]))
    weights_low = reduced_precision(weight_in)
    gate_pre = low_back(jnp.einsum('tc,cf->tf', normed_two, weights_low[0], precision=HIGHEST))
    up_proj = low_back(jnp.einsum('tc,cf->tf', normed_two, weights_low[1], precision=HIGHEST))
    hidden = reduced_precision(jax.nn.silu(gate_pre) * up_proj)
    output = low_back(jnp.einsum('tf,fd->td', hidden, reduced_precision(weight_down), precision=HIGHEST))
    return middle + output

def adamw_update(weight, moment_one, moment_two, gradient, step_rate, decay_rate):
    first_new = BETA_FIRST * moment_one + (1.0 - BETA_FIRST) * gradient
    second_new = BETA_SECOND * moment_two + (1.0 - BETA_SECOND) * gradient * gradient
    first_hat = first_new / (1.0 - BETA_FIRST ** STEP)
    second_hat = second_new / (1.0 - BETA_SECOND ** STEP)
    weight_new = weight - step_rate * (first_hat / (jnp.sqrt(second_hat) + ADAM_EPS) + decay_rate * weight)
    return (weight_new, first_new, second_new)

def reference(tokens, cotangent, segments, positions, w_qkv, m_qkv, v_qkv, w_out, m_out, v_out, w_in, m_in, v_in, w_down, m_down, v_down, gains, m_gains, v_gains):
    params = (w_qkv, w_out, w_in, w_down, gains)

    def one_sequence(totals, operands):
        seq_tokens, seq_cot, seq_segments, seq_positions = operands

        def forward(inputs, weight_qkv, weight_out, weight_in, weight_down, gain_pair):
            return block_forward(inputs, weight_qkv, weight_out, weight_in, weight_down, gain_pair, seq_segments, seq_positions)
        result, pullback = jax.vjp(forward, seq_tokens.astype(jnp.float32), *params)
        gradients = pullback(seq_cot.astype(jnp.float32))
        totals = tuple((total + gradient for total, gradient in zip(totals, gradients[1:])))
        return (totals, (result, gradients[0]))
    initial = tuple((jnp.zeros_like(param) for param in params))
    totals, (layer_out, tokens_grad) = lax.scan(one_sequence, initial, (tokens, cotangent, segments, positions))
    new_qkv, mom_qkv, sq_qkv = adamw_update(w_qkv, m_qkv, v_qkv, totals[0], RATE_MATRIX, WEIGHT_DECAY)
    new_out, mom_out, sq_out = adamw_update(w_out, m_out, v_out, totals[1], RATE_MATRIX, WEIGHT_DECAY)
    new_in, mom_in, sq_in = adamw_update(w_in, m_in, v_in, totals[2], RATE_MATRIX, WEIGHT_DECAY)
    new_down, mom_down, sq_down = adamw_update(w_down, m_down, v_down, totals[3], RATE_MATRIX, WEIGHT_DECAY)
    new_gains, mom_gains, sq_gains = adamw_update(gains, m_gains, v_gains, totals[4], RATE_GAIN, 0.0)
    return (layer_out, tokens_grad, new_qkv, mom_qkv, sq_qkv, new_out, mom_out, sq_out, new_in, mom_in, sq_in, new_down, mom_down, sq_down, new_gains, mom_gains, sq_gains)
```

```python
from functools import partial

import jax
import jax.numpy as jnp
from jax import lax
from jax.sharding import PartitionSpec as P

QUERY_HEADS = 15
KEY_VALUE_HEADS = 5
HEAD_SIZE = 64
STEP = 10


NORM_EPS = 1e-05
ROPE_BASE = 10000.0
MASKED = -1e30
BETA_FIRST = 0.9
BETA_SECOND = 0.95
ADAM_EPS = 1e-08
WEIGHT_DECAY = 0.1
RATE_MATRIX = 0.05
RATE_GAIN = 0.3


def rotation(places_in_doc):
    frequency = ROPE_BASE ** (-(jnp.arange(HEAD_SIZE // 2).astype(jnp.float32) * 2.0 / HEAD_SIZE))
    angles = places_in_doc.astype(jnp.float32)[:, None] * frequency[None, :]
    return (jnp.cos(angles)[:, None, :], jnp.sin(angles)[:, None, :])


def apply_rotary(head_rows, rotary_cosine, rotary_sine):
    half_width = head_rows.shape[-1] // 2
    front_half = head_rows[..., :half_width]
    back_half = head_rows[..., half_width:]
    return jnp.concatenate(
        [
            front_half * rotary_cosine - back_half * rotary_sine,
            back_half * rotary_cosine + front_half * rotary_sine,
        ],
        axis=-1,
    )


def inverse_rotary(grad_rows, rotary_cosine, rotary_sine):
    half_width = grad_rows.shape[-1] // 2
    front_half = grad_rows[..., :half_width]
    back_half = grad_rows[..., half_width:]
    return jnp.concatenate(
        [
            front_half * rotary_cosine + back_half * rotary_sine,
            back_half * rotary_cosine - front_half * rotary_sine,
        ],
        axis=-1,
    )


def norm_back(grad_output, plain_rows, factor, gain_row):
    scaled = grad_output * gain_row
    grad_input = factor * (
        scaled - plain_rows * jnp.mean(scaled * plain_rows, axis=-1, keepdims=True)
    )
    gain_gradient = jnp.sum(grad_output * plain_rows, axis=0)
    return (grad_input, gain_gradient)


def adamw_update(weight, moment_one, moment_two, gradient, step_rate, decay_rate):
    first_new = BETA_FIRST * moment_one + (1.0 - BETA_FIRST) * gradient
    second_new = BETA_SECOND * moment_two + (1.0 - BETA_SECOND) * gradient * gradient
    first_hat = first_new / (1.0 - BETA_FIRST**STEP)
    second_hat = second_new / (1.0 - BETA_SECOND**STEP)
    weight_new = weight - step_rate * (
        first_hat / (jnp.sqrt(second_hat) + ADAM_EPS) + decay_rate * weight
    )
    return (weight_new, first_new, second_new)


def bits_of(count):
    return count.bit_length() - 1


def swap(array, axis, size, mask):
    return lax.ppermute(array, axis, [(k, k ^ mask) for k in range(size)])


class Slice:
    def __init__(self, dp_size, grp_size):
        self.dp_size = dp_size
        self.grp_size = grp_size
        dp_bits = bits_of(dp_size)
        grp_bits = bits_of(grp_size)
        x_bits = min(max(grp_bits - 1, 0), dp_bits)
        self.z_bits = list(range(dp_bits - 1, x_bits - 1, -1))
        self.x_bits = list(range(x_bits - 1, -1, -1))
        self.y_bits = list(range(1, grp_bits))

    def dp_bit(self, bit):
        return (lax.axis_index("dp") >> bit) & 1

    def gather_dp(self, pieces, bit):
        own = self.dp_bit(bit)
        gathered = {}
        for mask, piece in pieces.items():
            other = swap(piece, "dp", self.dp_size, 1 << bit)
            low = jnp.where(own == 0, piece, other)
            high = jnp.where(own == 0, other, piece)
            joined = jnp.stack([low, high], axis=-3)
            gathered[mask] = joined.reshape(
                joined.shape[:-4] + (joined.shape[-4] * 2,) + joined.shape[-2:]
            )
        return gathered

    def gather_grp(self, pieces, bit):
        gathered = dict(pieces)
        for mask, piece in pieces.items():
            gathered[mask ^ (1 << bit)] = swap(piece, "grp", self.grp_size, 1 << bit)
        return gathered

    def gather(self, block, x_first):
        pieces = {0: block}
        for bit in self.z_bits:
            pieces = self.gather_dp(pieces, bit)
        for axis in ("xy" if x_first else "yx"):
            if axis == "x":
                for bit in self.x_bits:
                    pieces = self.gather_dp(pieces, bit)
            else:
                for bit in self.y_bits:
                    pieces = self.gather_grp(pieces, bit)
        return self.gather_grp(pieces, 0)

    def reduce_dp(self, pieces, bit):
        own = self.dp_bit(bit)
        reduced = {}
        for mask, piece in pieces.items():
            paired = piece.reshape(
                piece.shape[:-3] + (piece.shape[-3] // 2, 2) + piece.shape[-2:]
            )
            axis = paired.ndim - 3
            kept = lax.dynamic_index_in_dim(paired, own, axis, keepdims=False)
            sent = lax.dynamic_index_in_dim(paired, 1 - own, axis, keepdims=False)
            came = swap(sent.astype(jnp.bfloat16), "dp", self.dp_size, 1 << bit)
            reduced[mask] = kept.astype(jnp.float32) + came.astype(jnp.float32)
        return reduced

    def reduce_grp(self, pieces, bit):
        reduced = {}
        for mask, piece in pieces.items():
            if mask & (1 << bit) == 0:
                came = swap(
                    pieces[mask | (1 << bit)].astype(jnp.bfloat16),
                    "grp",
                    self.grp_size,
                    1 << bit,
                )
                reduced[mask] = piece.astype(jnp.float32) + came.astype(jnp.float32)
        return reduced

    def scatter_sum(self, pieces, x_first):
        for axis in ("xy" if x_first else "yx"):
            if axis == "x":
                for bit in reversed(self.x_bits):
                    pieces = self.reduce_dp(pieces, bit)
            else:
                for bit in reversed(self.y_bits):
                    pieces = self.reduce_grp(pieces, bit)
        for bit in reversed(self.z_bits):
            pieces = self.reduce_dp(pieces, bit)
        return pieces[0]

    def to_masks(self, rows):
        width = rows.shape[1] // self.grp_size
        blocks = jnp.stack([rows[:, k * width : (k + 1) * width] for k in range(self.grp_size)])
        own = lax.axis_index("grp")
        return {
            m: lax.dynamic_index_in_dim(blocks, own ^ m, 0, keepdims=False)
            for m in range(self.grp_size)
        }

    def from_masks(self, blocks):
        stacked = jnp.stack([blocks[m] for m in range(self.grp_size)])
        own = lax.axis_index("grp")
        return jnp.concatenate(
            [
                lax.dynamic_index_in_dim(stacked, own ^ k, 0, keepdims=False)
                for k in range(self.grp_size)
            ],
            axis=1,
        )

    def pair(self, array):
        return jnp.concatenate([array, swap(array, "grp", self.grp_size, 1)], axis=0)

    def pair_blocks(self, blocks):
        own = [m for m in range(self.grp_size) if m & 1 == 0]
        came = swap(jnp.stack([blocks[m ^ 1] for m in own]), "grp", self.grp_size, 1)
        return {m: jnp.concatenate([blocks[m], came[n]], axis=0) for n, m in enumerate(own)}


def rows_of(piece):
    return piece.reshape(-1, piece.shape[-1])


def forward_product(blocks, pieces):
    total = None
    for mask, block in blocks.items():
        term = lax.dot_general(
            block,
            rows_of(pieces[mask]),
            (((1,), (1,)), ((), ())),
            preferred_element_type=jnp.float32,
        )
        total = term if total is None else total + term
    return total


def backward_product(grad_rows, pieces):
    return {
        mask: jnp.dot(grad_rows, rows_of(piece), preferred_element_type=jnp.float32)
        for mask, piece in pieces.items()
    }


def weight_gradient(grad_rows, blocks, lead):
    return {
        mask: lax.dot_general(
            grad_rows, block, (((0,), (0,)), ((), ())), preferred_element_type=jnp.float32
        ).reshape(lead + (-1, block.shape[1]))
        for mask, block in blocks.items()
    }


def local(
    dp_size,
    grp_size,
    tokens,
    cotangent,
    segments,
    positions,
    w_qkv,
    m_qkv,
    v_qkv,
    w_out,
    m_out,
    v_out,
    w_in,
    m_in,
    v_in,
    w_down,
    m_down,
    v_down,
    gains,
    m_gains,
    v_gains,
):
    net = Slice(dp_size, grp_size)
    low = jnp.bfloat16
    full_qkv = net.gather(w_qkv.astype(low).T[None], True)
    full_out = net.gather(w_out.astype(low).T[None], True)
    full_in = net.gather(w_in.astype(low).transpose(0, 2, 1)[:, None], False)
    full_down = net.gather(w_down.astype(low).T[None], True)

    inputs = tokens[0].astype(jnp.float32)
    token_length = inputs.shape[0]
    group_count = QUERY_HEADS // KEY_VALUE_HEADS
    query_width = QUERY_HEADS * HEAD_SIZE
    key_width = KEY_VALUE_HEADS * HEAD_SIZE
    scale_factor = HEAD_SIZE ** (-0.5)
    own_piece = lax.axis_index("grp")
    query_places = own_piece * token_length + jnp.arange(token_length)
    segment_pieces = segments[0].reshape(grp_size, token_length)
    own_segments = lax.dynamic_index_in_dim(segment_pieces, own_piece, 0, keepdims=False)
    key_masks = [0]
    for bit in net.y_bits + [0]:
        key_masks = key_masks + [m ^ (1 << bit) for m in key_masks]
    key_segments = jnp.concatenate(
        [
            lax.dynamic_index_in_dim(segment_pieces, own_piece ^ m, 0, keepdims=False)
            for m in key_masks
        ]
    )
    key_places = jnp.concatenate(
        [(own_piece ^ m) * token_length + jnp.arange(token_length) for m in key_masks]
    )
    allowed = (key_places[None, :] <= query_places[:, None]) & (
        key_segments[None, :] == own_segments[:, None]
    )
    rotary_cosine, rotary_sine = rotation(positions[0])
    factor_one = lax.rsqrt(jnp.mean(inputs * inputs, axis=-1, keepdims=True) + NORM_EPS)
    plain_one = inputs * factor_one
    normed = (plain_one * gains[0]).astype(low)
    normed_blocks = net.to_masks(normed)
    blended_rows = forward_product(normed_blocks, full_qkv)
    query_rows = apply_rotary(
        blended_rows[:, :query_width].reshape(token_length, QUERY_HEADS, HEAD_SIZE),
        rotary_cosine,
        rotary_sine,
    ).astype(low)
    own_keys = apply_rotary(
        blended_rows[:, query_width : query_width + key_width].reshape(
            token_length, KEY_VALUE_HEADS, HEAD_SIZE
        ),
        rotary_cosine,
        rotary_sine,
    )
    own_keys = own_keys.astype(low).reshape(token_length, key_width)
    own_values = blended_rows[:, query_width + key_width :].astype(low)
    keys_values = jnp.concatenate([own_keys, own_values], axis=1)
    for bit in net.y_bits + [0]:
        keys_values = jnp.concatenate(
            [keys_values, swap(keys_values, "grp", grp_size, 1 << bit)], axis=0
        )
    rows_of_keys = keys_values[:, :key_width]
    rows_of_values = keys_values[:, key_width:]
    grouped_heads = query_rows.reshape(token_length, KEY_VALUE_HEADS, group_count, HEAD_SIZE)

    def scores_of(group_of_head, key_all):
        key_block = key_all[:, group_of_head * HEAD_SIZE : (group_of_head + 1) * HEAD_SIZE]
        raw_scores = (
            jnp.einsum(
                "trd,sd->rts",
                grouped_heads[:, group_of_head],
                key_block,
                preferred_element_type=jnp.float32,
            )
            * scale_factor
        )
        return jnp.where(allowed[None], raw_scores, MASKED)

    outputs = []
    log_totals = []
    for group_of_head in range(KEY_VALUE_HEADS):
        masked = scores_of(group_of_head, rows_of_keys)
        row_peak = jnp.max(masked, axis=-1, keepdims=True)
        exponent = jnp.exp(masked - row_peak)
        row_total = jnp.sum(exponent, axis=-1, keepdims=True)
        probability = exponent / row_total
        log_totals.append(row_peak + jnp.log(row_total))
        value_block = rows_of_values[:, group_of_head * HEAD_SIZE : (group_of_head + 1) * HEAD_SIZE]
        outputs.append(
            jnp.einsum(
                "rts,sd->trd",
                probability.astype(low),
                value_block,
                preferred_element_type=jnp.float32,
            )
        )
    attended_low = jnp.concatenate(outputs, axis=1).reshape(token_length, query_width).astype(low)
    attended_blocks = net.to_masks(attended_low)
    middle = inputs + forward_product(attended_blocks, full_out)
    factor_two = lax.rsqrt(jnp.mean(middle * middle, axis=-1, keepdims=True) + NORM_EPS)
    plain_two = middle * factor_two
    normed_two = (plain_two * gains[1]).astype(low)
    normed_two_blocks = net.to_masks(normed_two)
    gate_up = forward_product(normed_two_blocks, full_in)
    ff_width = gate_up.shape[1] // 2
    gate_pre = gate_up[:, :ff_width]
    up_proj = gate_up[:, ff_width:]
    sigmoid_gate = jax.nn.sigmoid(gate_pre)
    activated = gate_pre * sigmoid_gate
    hidden = (activated * up_proj).astype(low)
    hidden_blocks = net.to_masks(hidden)
    layer_out = middle + forward_product(hidden_blocks, full_down)

    upstream = cotangent[0].astype(jnp.float32)
    upstream_low = cotangent[0]
    grad_down = weight_gradient(
        net.pair(upstream_low), net.pair_blocks(hidden_blocks), (dp_size,)
    )
    owned_down = net.scatter_sum(grad_down, True)[0]
    grad_hidden = net.from_masks(backward_product(upstream_low, full_down))
    grad_gate = (
        grad_hidden * up_proj * sigmoid_gate * (1.0 + gate_pre * (1.0 - sigmoid_gate))
    ).astype(low)
    grad_up = (grad_hidden * activated).astype(low)
    grad_gate_up = jnp.concatenate([grad_gate, grad_up], axis=1)
    grad_in = weight_gradient(
        net.pair(grad_gate_up), net.pair_blocks(normed_two_blocks), (2, dp_size)
    )
    owned_in = net.scatter_sum(grad_in, False)[:, 0]
    grad_normed_two = net.from_masks(backward_product(grad_gate_up, full_in))
    back_two, gain_two = norm_back(grad_normed_two, plain_two, factor_two, gains[1])
    grad_middle = upstream + back_two
    middle_low = grad_middle.astype(low)
    grad_out = weight_gradient(
        net.pair(middle_low), net.pair_blocks(attended_blocks), (dp_size,)
    )
    owned_out = net.scatter_sum(grad_out, True)[0]
    attended_gradient = net.from_masks(backward_product(middle_low, full_out))
    attended_gradient = attended_gradient.astype(low).reshape(
        token_length, KEY_VALUE_HEADS, group_count, HEAD_SIZE
    )
    grads_query = []
    grads_key = []
    grads_value = []
    for group_of_head in range(KEY_VALUE_HEADS):
        masked = scores_of(group_of_head, rows_of_keys)
        probability = jnp.exp(masked - log_totals[group_of_head])
        key_block = rows_of_keys[:, group_of_head * HEAD_SIZE : (group_of_head + 1) * HEAD_SIZE]
        value_block = rows_of_values[:, group_of_head * HEAD_SIZE : (group_of_head + 1) * HEAD_SIZE]
        grad_block = attended_gradient[:, group_of_head]
        grad_probs = jnp.einsum(
            "trd,sd->rts", grad_block, value_block, preferred_element_type=jnp.float32
        )
        grads_value.append(
            jnp.einsum(
                "rts,trd->sd",
                probability.astype(low),
                grad_block,
                preferred_element_type=jnp.float32,
            )
        )
        grad_scores = probability * (
            grad_probs - jnp.sum(probability * grad_probs, axis=-1, keepdims=True)
        )
        grad_scores = grad_scores.astype(low)
        grads_query.append(
            jnp.einsum("rts,sd->trd", grad_scores, key_block, preferred_element_type=jnp.float32)
            * scale_factor
        )
        grads_key.append(
            jnp.einsum(
                "rts,trd->sd",
                grad_scores,
                grouped_heads[:, group_of_head],
                preferred_element_type=jnp.float32,
            )
            * scale_factor
        )
    grad_keys_values = jnp.concatenate(grads_key + grads_value, axis=1)
    for bit in [0] + net.y_bits[::-1]:
        half = grad_keys_values.shape[0] // 2
        came = swap(grad_keys_values[half:].astype(low), "grp", grp_size, 1 << bit)
        grad_keys_values = grad_keys_values[:half] + came.astype(jnp.float32)
    grad_queries = jnp.concatenate(grads_query, axis=1)
    grad_mixed = jnp.concatenate(
        [
            inverse_rotary(grad_queries, rotary_cosine, rotary_sine).reshape(
                token_length, query_width
            ),
            inverse_rotary(
                grad_keys_values[:, :key_width].reshape(token_length, KEY_VALUE_HEADS, HEAD_SIZE),
                rotary_cosine,
                rotary_sine,
            ).reshape(token_length, key_width),
            grad_keys_values[:, key_width:],
        ],
        axis=1,
    ).astype(low)
    grad_qkv = weight_gradient(net.pair(grad_mixed), net.pair_blocks(normed_blocks), (dp_size,))
    owned_qkv = net.scatter_sum(grad_qkv, True)[0]
    grad_normed = net.from_masks(backward_product(grad_mixed, full_qkv))
    back_one, gain_one = norm_back(grad_normed, plain_one, factor_one, gains[0])
    tokens_grad = grad_middle + back_one
    gain_grads = jnp.stack([gain_one, gain_two])
    for bit in range(bits_of(grp_size)):
        gain_grads = gain_grads + swap(gain_grads, "grp", grp_size, 1 << bit)
    for bit in range(bits_of(dp_size)):
        gain_grads = gain_grads + swap(gain_grads, "dp", dp_size, 1 << bit)
    new_qkv, mom_qkv, sq_qkv = adamw_update(
        w_qkv, m_qkv, v_qkv, owned_qkv.T, RATE_MATRIX, WEIGHT_DECAY
    )
    new_out, mom_out, sq_out = adamw_update(
        w_out, m_out, v_out, owned_out.T, RATE_MATRIX, WEIGHT_DECAY
    )
    new_in, mom_in, sq_in = adamw_update(
        w_in, m_in, v_in, owned_in.transpose(0, 2, 1), RATE_MATRIX, WEIGHT_DECAY
    )
    new_down, mom_down, sq_down = adamw_update(
        w_down, m_down, v_down, owned_down.T, RATE_MATRIX, WEIGHT_DECAY
    )
    new_gains, mom_gains, sq_gains = adamw_update(
        gains, m_gains, v_gains, gain_grads, RATE_GAIN, 0.0
    )
    return (
        layer_out[None],
        tokens_grad[None],
        new_qkv,
        mom_qkv,
        sq_qkv,
        new_out,
        mom_out,
        sq_out,
        new_in,
        mom_in,
        sq_in,
        new_down,
        mom_down,
        sq_down,
        new_gains,
        mom_gains,
        sq_gains,
    )


def solution(mesh):
    return jax.shard_map(
        partial(local, mesh.shape["dp"], mesh.shape["grp"]),
        mesh=mesh,
        in_specs=(
            P("dp", "grp", None),
            P("dp", "grp", None),
            P("dp", None),
            P("dp", "grp"),
            P("grp", "dp"),
            P("grp", "dp"),
            P("grp", "dp"),
            P("grp", "dp"),
            P("grp", "dp"),
            P("grp", "dp"),
            P(None, "grp", "dp"),
            P(None, "grp", "dp"),
            P(None, "grp", "dp"),
            P("grp", "dp"),
            P("grp", "dp"),
            P("grp", "dp"),
            P(),
            P(),
            P(),
        ),
        out_specs=(
            P("dp", "grp", None),
            P("dp", "grp", None),
            P("grp", "dp"),
            P("grp", "dp"),
            P("grp", "dp"),
            P("grp", "dp"),
            P("grp", "dp"),
            P("grp", "dp"),
            P(None, "grp", "dp"),
            P(None, "grp", "dp"),
            P(None, "grp", "dp"),
            P("grp", "dp"),
            P("grp", "dp"),
            P("grp", "dp"),
            P(),
            P(),
            P(),
        ),
        check_vma=False,
    )
```

```python
from functools import partial

import jax
import jax.numpy as jnp
from jax import lax
from jax.sharding import PartitionSpec as P

QUERY_HEADS = 15
KEY_VALUE_HEADS = 5
HEAD_SIZE = 64
STEP = 10


NORM_EPS = 1e-05
ROPE_BASE = 10000.0
MASKED = -1e30
BETA_FIRST = 0.9
BETA_SECOND = 0.95
ADAM_EPS = 1e-08
WEIGHT_DECAY = 0.1
RATE_MATRIX = 0.05
RATE_GAIN = 0.3


def rotation(places_in_doc):
    frequency = ROPE_BASE ** (-(jnp.arange(HEAD_SIZE // 2).astype(jnp.float32) * 2.0 / HEAD_SIZE))
    angles = places_in_doc.astype(jnp.float32)[:, None] * frequency[None, :]
    return (jnp.cos(angles)[:, None, :], jnp.sin(angles)[:, None, :])


def apply_rotary(head_rows, rotary_cosine, rotary_sine):
    half_width = head_rows.shape[-1] // 2
    front_half = head_rows[..., :half_width]
    back_half = head_rows[..., half_width:]
    return jnp.concatenate(
        [
            front_half * rotary_cosine - back_half * rotary_sine,
            back_half * rotary_cosine + front_half * rotary_sine,
        ],
        axis=-1,
    )


def inverse_rotary(grad_rows, rotary_cosine, rotary_sine):
    half_width = grad_rows.shape[-1] // 2
    front_half = grad_rows[..., :half_width]
    back_half = grad_rows[..., half_width:]
    return jnp.concatenate(
        [
            front_half * rotary_cosine + back_half * rotary_sine,
            back_half * rotary_cosine - front_half * rotary_sine,
        ],
        axis=-1,
    )


def norm_back(grad_output, plain_rows, factor, gain_row):
    scaled = grad_output * gain_row
    grad_input = factor * (
        scaled - plain_rows * jnp.mean(scaled * plain_rows, axis=-1, keepdims=True)
    )
    gain_gradient = jnp.sum(grad_output * plain_rows, axis=0)
    return (grad_input, gain_gradient)


def adamw_update(weight, moment_one, moment_two, gradient, step_rate, decay_rate):
    first_new = BETA_FIRST * moment_one + (1.0 - BETA_FIRST) * gradient
    second_new = BETA_SECOND * moment_two + (1.0 - BETA_SECOND) * gradient * gradient
    first_hat = first_new / (1.0 - BETA_FIRST**STEP)
    second_hat = second_new / (1.0 - BETA_SECOND**STEP)
    weight_new = weight - step_rate * (
        first_hat / (jnp.sqrt(second_hat) + ADAM_EPS) + decay_rate * weight
    )
    return (weight_new, first_new, second_new)


def bits_of(count):
    return count.bit_length() - 1


def tie(value, *others):
    return lax.optimization_barrier((value, others))[0]


class Slice:

    def __init__(self, dp_size, grp_size):
        self.dp_size = dp_size
        self.grp_size = grp_size
        dp_bits = bits_of(dp_size)
        grp_bits = bits_of(grp_size)
        x_count = min(max(grp_bits - 1, 0), dp_bits)
        self.x_bits = [("dp", bit) for bit in range(x_count - 1, -1, -1)]
        z_bits = [("dp", bit) for bit in range(dp_bits - 1, x_count - 1, -1)]
        self.far_bits = z_bits[:1]
        self.near_bits = z_bits[1:]
        self.y_bits = [("grp", bit) for bit in range(1, grp_bits)]
        self.core_bits = [("grp", 0)]

    def size(self, axis):
        return self.dp_size if axis == "dp" else self.grp_size

    def own(self, axis, bit):
        return (lax.axis_index(axis) >> bit) & 1

    def swap(self, array, step):
        axis, bit = step
        size = self.size(axis)
        return lax.ppermute(array, axis, [(k, k ^ (1 << bit)) for k in range(size)])

    def gather(self, pieces, steps):
        for step in steps:
            axis, bit = step
            came = {mask: self.swap(piece, step) for mask, piece in pieces.items()}
            if axis == "grp":
                pieces = dict(pieces)
                for mask, piece in came.items():
                    pieces[mask ^ (1 << bit)] = piece
            else:
                own = self.own(axis, bit)
                joined = {}
                for mask, piece in pieces.items():
                    low = jnp.where(own == 0, piece, came[mask])
                    high = jnp.where(own == 0, came[mask], piece)
                    pair = jnp.stack([low, high], axis=1)
                    joined[mask] = pair.reshape((-1,) + piece.shape[1:])
                pieces = joined
        return pieces

    def reduce(self, pieces, steps):
        for axis, bit in reversed(steps):
            reduced = {}
            if axis == "grp":
                for mask, piece in pieces.items():
                    if mask & (1 << bit) == 0:
                        sent = pieces[mask | (1 << bit)].astype(jnp.bfloat16)
                        came = self.swap(sent, (axis, bit))
                        reduced[mask] = piece.astype(jnp.float32) + came.astype(jnp.float32)
            else:
                own = self.own(axis, bit)
                for mask, piece in pieces.items():
                    paired = piece.reshape((piece.shape[0] // 2, 2) + piece.shape[1:])
                    kept = jnp.where(own == 0, paired[:, 0], paired[:, 1])
                    sent = jnp.where(own == 0, paired[:, 1], paired[:, 0])
                    came = self.swap(sent.astype(jnp.bfloat16), (axis, bit))
                    reduced[mask] = kept.astype(jnp.float32) + came.astype(jnp.float32)
            pieces = reduced
        return pieces

    def by_mask(self, blocks):
        blocks = list(blocks)
        for bit in range(bits_of(self.grp_size)):
            own = self.own("grp", bit)
            blocks = [
                jnp.where(own == 0, block, blocks[k ^ (1 << bit)]) for k, block in enumerate(blocks)
            ]
        return blocks

    def to_masks(self, rows):
        width = rows.shape[1] // self.grp_size
        return self.by_mask([rows[:, k * width : (k + 1) * width] for k in range(self.grp_size)])

    def from_masks(self, blocks):
        return jnp.concatenate(self.by_mask(blocks), axis=1)

    def pair(self, array):
        return jnp.concatenate([array, self.swap(array, self.core_bits[0])], axis=0)

    def pair_blocks(self, blocks):
        own = range(0, self.grp_size, 2)
        came = self.swap(jnp.stack([blocks[m ^ 1] for m in own]), self.core_bits[0])
        return {m: jnp.concatenate([blocks[m], came[n]], axis=0) for n, m in enumerate(own)}


def rows_of(piece):
    return piece.reshape(-1, piece.shape[-1])


def forward_product(blocks, pieces):
    total = None
    for mask in pieces:
        block = blocks[mask]
        term = lax.dot_general(
            block,
            rows_of(pieces[mask]),
            (((1,), (1,)), ((), ())),
            preferred_element_type=jnp.float32,
        )
        total = term if total is None else total + term
    return total


def backward_product(grad_rows, pieces):
    return [
        jnp.dot(grad_rows, rows_of(pieces[mask]), preferred_element_type=jnp.float32)
        for mask in sorted(pieces)
    ]


def weight_gradient(grad_rows, blocks, dp_size):
    return {
        mask: lax.dot_general(
            grad_rows, block, (((0,), (0,)), ((), ())), preferred_element_type=jnp.float32
        ).reshape((dp_size, -1, block.shape[1]))
        for mask, block in blocks.items()
    }


def local(
    dp_size,
    grp_size,
    tokens,
    cotangent,
    segments,
    positions,
    w_qkv,
    m_qkv,
    v_qkv,
    w_out,
    m_out,
    v_out,
    w_in,
    m_in,
    v_in,
    w_down,
    m_down,
    v_down,
    gains,
    m_gains,
    v_gains,
):
    net = Slice(dp_size, grp_size)
    low = jnp.bfloat16
    x_then_y = net.x_bits + net.y_bits
    y_then_x = net.y_bits + net.x_bits
    down_low = w_down.astype(low).T
    down_cut = down_low.shape[1] * 3 // 5
    down_orders = (x_then_y, y_then_x)
    in_low = w_in.astype(low)
    far_qkv = net.gather({0: w_qkv.astype(low).T[None]}, net.far_bits)
    far_out = net.gather({0: w_out.astype(low).T[None]}, net.far_bits)
    near_qkv = net.gather(far_qkv, net.near_bits)
    near_out = net.gather(far_out, net.near_bits)
    far_down = [
        net.gather({0: tie(half[None], far_qkv)}, net.far_bits)
        for half in (down_low[:, :down_cut], down_low[:, down_cut:])
    ]
    third_qkv = net.gather(near_qkv, x_then_y[:1])
    third_out = net.gather(near_out, y_then_x[:1])
    near_down = [net.gather(tie(part, near_qkv), net.near_bits) for part in far_down]
    part_gate, part_up = [
        net.gather({0: tie(in_low[n].T[None], far_down, near_qkv)}, net.far_bits)
        for n in range(2)
    ]
    full_qkv = net.gather(third_qkv, x_then_y[1:] + net.core_bits)
    full_out = net.gather(third_out, y_then_x[1:] + net.core_bits)
    half_down = [
        net.gather(tie(part, third_qkv), order + net.core_bits)
        for part, order in zip(near_down, down_orders)
    ]
    part_gate = net.gather(tie(part_gate, near_down, third_qkv), net.near_bits + net.x_bits)
    part_up = net.gather(tie(part_up, near_down, third_qkv), net.near_bits + net.y_bits)

    inputs = tokens[0].astype(jnp.float32)
    token_length = inputs.shape[0]
    group_count = QUERY_HEADS // KEY_VALUE_HEADS
    query_width = QUERY_HEADS * HEAD_SIZE
    key_width = KEY_VALUE_HEADS * HEAD_SIZE
    scale_factor = HEAD_SIZE ** (-0.5)
    own_piece = lax.axis_index("grp")
    query_places = own_piece * token_length + jnp.arange(token_length)
    segment_pieces = segments[0].reshape(grp_size, token_length)
    own_segments = lax.dynamic_index_in_dim(segment_pieces, own_piece, 0, keepdims=False)
    key_masks = [0]
    for axis, bit in net.y_bits + net.core_bits:
        key_masks = key_masks + [m ^ (1 << bit) for m in key_masks]
    key_segments = jnp.concatenate(
        [
            lax.dynamic_index_in_dim(segment_pieces, own_piece ^ m, 0, keepdims=False)
            for m in key_masks
        ]
    )
    key_places = jnp.concatenate(
        [(own_piece ^ m) * token_length + jnp.arange(token_length) for m in key_masks]
    )
    allowed = (key_places[None, :] <= query_places[:, None]) & (
        key_segments[None, :] == own_segments[:, None]
    )
    rotary_cosine, rotary_sine = rotation(positions[0])
    factor_one = lax.rsqrt(jnp.mean(inputs * inputs, axis=-1, keepdims=True) + NORM_EPS)
    plain_one = inputs * factor_one
    normed = (plain_one * gains[0]).astype(low)
    normed_blocks = net.to_masks(normed)
    blended_rows = forward_product(normed_blocks, full_qkv)
    query_rows = apply_rotary(
        blended_rows[:, :query_width].reshape(token_length, QUERY_HEADS, HEAD_SIZE),
        rotary_cosine,
        rotary_sine,
    ).astype(low)
    own_keys = apply_rotary(
        blended_rows[:, query_width : query_width + key_width].reshape(
            token_length, KEY_VALUE_HEADS, HEAD_SIZE
        ),
        rotary_cosine,
        rotary_sine,
    )
    own_keys = own_keys.astype(low).reshape(token_length, key_width)
    own_values = blended_rows[:, query_width + key_width :].astype(low)
    keys_values = jnp.concatenate([own_keys, own_values], axis=1)
    part_gate = net.gather(tie(part_gate, keys_values), net.y_bits + net.core_bits)
    part_up = net.gather(tie(part_up, keys_values), net.x_bits + net.core_bits)
    for step in net.y_bits + net.core_bits:
        keys_values = jnp.concatenate([keys_values, net.swap(keys_values, step)], axis=0)
    rows_of_keys = keys_values[:, :key_width]
    rows_of_values = keys_values[:, key_width:]
    grouped_heads = query_rows.reshape(token_length, KEY_VALUE_HEADS, group_count, HEAD_SIZE)

    def scores_of(group_of_head, key_all):
        key_block = key_all[:, group_of_head * HEAD_SIZE : (group_of_head + 1) * HEAD_SIZE]
        raw_scores = (
            jnp.einsum(
                "trd,sd->rts",
                grouped_heads[:, group_of_head],
                key_block,
                preferred_element_type=jnp.float32,
            )
            * scale_factor
        )
        return jnp.where(allowed[None], raw_scores, MASKED)

    outputs = []
    log_totals = []
    for group_of_head in range(KEY_VALUE_HEADS):
        masked = scores_of(group_of_head, rows_of_keys)
        row_peak = jnp.max(masked, axis=-1, keepdims=True)
        exponent = jnp.exp(masked - row_peak)
        row_total = jnp.sum(exponent, axis=-1, keepdims=True)
        probability = exponent / row_total
        log_totals.append(row_peak + jnp.log(row_total))
        value_block = rows_of_values[:, group_of_head * HEAD_SIZE : (group_of_head + 1) * HEAD_SIZE]
        outputs.append(
            jnp.einsum(
                "rts,sd->trd",
                probability.astype(low),
                value_block,
                preferred_element_type=jnp.float32,
            )
        )
    attended_low = jnp.concatenate(outputs, axis=1).reshape(token_length, query_width).astype(low)
    attended_blocks = net.to_masks(attended_low)
    middle = inputs + forward_product(attended_blocks, full_out)
    factor_two = lax.rsqrt(jnp.mean(middle * middle, axis=-1, keepdims=True) + NORM_EPS)
    plain_two = middle * factor_two
    normed_two = (plain_two * gains[1]).astype(low)
    normed_two_blocks = net.to_masks(normed_two)
    gate_pre = forward_product(normed_two_blocks, part_gate)
    up_proj = forward_product(normed_two_blocks, part_up)
    sigmoid_gate = jax.nn.sigmoid(gate_pre)
    activated = gate_pre * sigmoid_gate
    hidden = (activated * up_proj).astype(low)
    hidden_blocks = net.to_masks(hidden)
    hidden_halves = (
        [block[:, :down_cut] for block in hidden_blocks],
        [block[:, down_cut:] for block in hidden_blocks],
    )
    layer_out = middle + (
        forward_product(hidden_halves[0], half_down[0])
        + forward_product(hidden_halves[1], half_down[1])
    )

    upstream = cotangent[0].astype(jnp.float32)
    upstream_low = cotangent[0]
    upstream_pair = net.pair(upstream_low)
    grad_down = [
        weight_gradient(upstream_pair, blocks, dp_size)
        for blocks in (net.pair_blocks(hidden_halves[0]), net.pair_blocks(hidden_halves[1]))
    ]
    grad_hidden = net.from_masks(
        [
            jnp.concatenate(halves, axis=1)
            for halves in zip(
                backward_product(upstream_low, half_down[0]),
                backward_product(upstream_low, half_down[1]),
            )
        ]
    )
    grad_gate = (
        grad_hidden * up_proj * sigmoid_gate * (1.0 + gate_pre * (1.0 - sigmoid_gate))
    ).astype(low)
    grad_up = (grad_hidden * activated).astype(low)
    normed_two_pair = net.pair_blocks(normed_two_blocks)
    grad_in_gate = weight_gradient(net.pair(grad_gate), normed_two_pair, dp_size)
    grad_in_up = weight_gradient(net.pair(grad_up), normed_two_pair, dp_size)
    grad_normed_two = net.from_masks(
        [
            one + two
            for one, two in zip(
                backward_product(grad_gate, part_gate), backward_product(grad_up, part_up)
            )
        ]
    )
    back_two, gain_two = norm_back(grad_normed_two, plain_two, factor_two, gains[1])
    grad_middle = upstream + back_two
    middle_low = grad_middle.astype(low)
    grad_out = weight_gradient(net.pair(middle_low), net.pair_blocks(attended_blocks), dp_size)
    attended_gradient = net.from_masks(backward_product(middle_low, full_out))
    attended_gradient = attended_gradient.astype(low).reshape(
        token_length, KEY_VALUE_HEADS, group_count, HEAD_SIZE
    )
    first_down = [net.reduce(grad, order[-1:]) for grad, order in zip(grad_down, down_orders)]
    first_gate = net.reduce(grad_in_gate, x_then_y[-1:])
    first_up = net.reduce(grad_in_up, y_then_x[-1:])
    second_down = [net.reduce(grad, order[:-1]) for grad, order in zip(first_down, down_orders)]
    beside = [grad_down, (grad_in_gate, grad_in_up), None, first_down, None]
    grads_query = []
    grads_key = []
    grads_value = []
    for group_of_head in range(KEY_VALUE_HEADS):
        masked = scores_of(group_of_head, rows_of_keys)
        probability = jnp.exp(masked - log_totals[group_of_head])
        key_block = rows_of_keys[:, group_of_head * HEAD_SIZE : (group_of_head + 1) * HEAD_SIZE]
        value_block = rows_of_values[:, group_of_head * HEAD_SIZE : (group_of_head + 1) * HEAD_SIZE]
        grad_block = tie(attended_gradient[:, group_of_head], beside[group_of_head])
        grad_probs = jnp.einsum(
            "trd,sd->rts", grad_block, value_block, preferred_element_type=jnp.float32
        )
        grads_value.append(
            jnp.einsum(
                "rts,trd->sd",
                probability.astype(low),
                grad_block,
                preferred_element_type=jnp.float32,
            )
        )
        grad_scores = probability * (
            grad_probs - jnp.sum(probability * grad_probs, axis=-1, keepdims=True)
        )
        grad_scores = grad_scores.astype(low)
        grads_query.append(
            jnp.einsum("rts,sd->trd", grad_scores, key_block, preferred_element_type=jnp.float32)
            * scale_factor
        )
        grads_key.append(
            jnp.einsum(
                "rts,trd->sd",
                grad_scores,
                grouped_heads[:, group_of_head],
                preferred_element_type=jnp.float32,
            )
            * scale_factor
        )
    grad_keys_values = jnp.concatenate(grads_key + grads_value, axis=1)
    for step in net.core_bits + net.y_bits[::-1]:
        half = grad_keys_values.shape[0] // 2
        came = net.swap(grad_keys_values[half:].astype(low), step)
        grad_keys_values = grad_keys_values[:half] + came.astype(jnp.float32)
    grad_queries = jnp.concatenate(grads_query, axis=1)
    grad_mixed = jnp.concatenate(
        [
            inverse_rotary(grad_queries, rotary_cosine, rotary_sine).reshape(
                token_length, query_width
            ),
            inverse_rotary(
                grad_keys_values[:, :key_width].reshape(token_length, KEY_VALUE_HEADS, HEAD_SIZE),
                rotary_cosine,
                rotary_sine,
            ).reshape(token_length, key_width),
            grad_keys_values[:, key_width:],
        ],
        axis=1,
    ).astype(low)
    grad_qkv = weight_gradient(net.pair(grad_mixed), net.pair_blocks(normed_blocks), dp_size)
    grad_normed = net.from_masks(backward_product(grad_mixed, full_qkv))
    back_one, gain_one = norm_back(grad_normed, plain_one, factor_one, gains[0])
    tokens_grad = grad_middle + back_one
    gain_grads = jnp.stack([gain_one, gain_two])
    for step in net.core_bits + net.y_bits + net.x_bits + net.near_bits + net.far_bits:
        gain_grads = gain_grads + net.swap(gain_grads, step)
    z_bits = net.far_bits + net.near_bits
    owned_down = jnp.concatenate([net.reduce(grad, z_bits)[0][0] for grad in second_down], axis=1)
    owned_in = jnp.stack(
        [
            net.reduce(first_gate, z_bits + x_then_y[:-1])[0][0],
            net.reduce(first_up, z_bits + y_then_x[:-1])[0][0],
        ]
    )
    owned_out = net.reduce(grad_out, z_bits + y_then_x)[0][0]
    owned_qkv = net.reduce(grad_qkv, z_bits + x_then_y)[0][0]
    new_qkv, mom_qkv, sq_qkv = adamw_update(
        w_qkv, m_qkv, v_qkv, owned_qkv.T, RATE_MATRIX, WEIGHT_DECAY
    )
    new_out, mom_out, sq_out = adamw_update(
        w_out, m_out, v_out, owned_out.T, RATE_MATRIX, WEIGHT_DECAY
    )
    new_in, mom_in, sq_in = adamw_update(
        w_in, m_in, v_in, owned_in.transpose(0, 2, 1), RATE_MATRIX, WEIGHT_DECAY
    )
    new_down, mom_down, sq_down = adamw_update(
        w_down, m_down, v_down, owned_down.T, RATE_MATRIX, WEIGHT_DECAY
    )
    new_gains, mom_gains, sq_gains = adamw_update(
        gains, m_gains, v_gains, gain_grads, RATE_GAIN, 0.0
    )
    return (
        layer_out[None],
        tokens_grad[None],
        new_qkv,
        mom_qkv,
        sq_qkv,
        new_out,
        mom_out,
        sq_out,
        new_in,
        mom_in,
        sq_in,
        new_down,
        mom_down,
        sq_down,
        new_gains,
        mom_gains,
        sq_gains,
    )


def solution(mesh):
    return jax.shard_map(
        partial(local, mesh.shape["dp"], mesh.shape["grp"]),
        mesh=mesh,
        in_specs=(
            P("dp", "grp", None),
            P("dp", "grp", None),
            P("dp", None),
            P("dp", "grp"),
            P("grp", "dp"),
            P("grp", "dp"),
            P("grp", "dp"),
            P("grp", "dp"),
            P("grp", "dp"),
            P("grp", "dp"),
            P(None, "grp", "dp"),
            P(None, "grp", "dp"),
            P(None, "grp", "dp"),
            P("grp", "dp"),
            P("grp", "dp"),
            P("grp", "dp"),
            P(),
            P(),
            P(),
        ),
        out_specs=(
            P("dp", "grp", None),
            P("dp", "grp", None),
            P("grp", "dp"),
            P("grp", "dp"),
            P("grp", "dp"),
            P("grp", "dp"),
            P("grp", "dp"),
            P("grp", "dp"),
            P(None, "grp", "dp"),
            P(None, "grp", "dp"),
            P(None, "grp", "dp"),
            P("grp", "dp"),
            P("grp", "dp"),
            P("grp", "dp"),
            P(),
            P(),
            P(),
        ),
        check_vma=False,
    )
```

```python
from functools import partial

import jax
import jax.numpy as jnp
from jax import lax
from jax.sharding import PartitionSpec as P

QUERY_HEADS = 15
KEY_VALUE_HEADS = 5
HEAD_SIZE = 64
STEP = 10


NORM_EPS = 1e-05
ROPE_BASE = 10000.0
MASKED = -1e30
BETA_FIRST = 0.9
BETA_SECOND = 0.95
ADAM_EPS = 1e-08
WEIGHT_DECAY = 0.1
RATE_MATRIX = 0.05
RATE_GAIN = 0.3


def rotation(places_in_doc):
    frequency = ROPE_BASE ** (-(jnp.arange(HEAD_SIZE // 2).astype(jnp.float32) * 2.0 / HEAD_SIZE))
    angles = places_in_doc.astype(jnp.float32)[:, None] * frequency[None, :]
    return (jnp.cos(angles)[:, None, :], jnp.sin(angles)[:, None, :])


def apply_rotary(head_rows, rotary_cosine, rotary_sine):
    half_width = head_rows.shape[-1] // 2
    front_half = head_rows[..., :half_width]
    back_half = head_rows[..., half_width:]
    return jnp.concatenate(
        [
            front_half * rotary_cosine - back_half * rotary_sine,
            back_half * rotary_cosine + front_half * rotary_sine,
        ],
        axis=-1,
    )


def inverse_rotary(grad_rows, rotary_cosine, rotary_sine):
    half_width = grad_rows.shape[-1] // 2
    front_half = grad_rows[..., :half_width]
    back_half = grad_rows[..., half_width:]
    return jnp.concatenate(
        [
            front_half * rotary_cosine + back_half * rotary_sine,
            back_half * rotary_cosine - front_half * rotary_sine,
        ],
        axis=-1,
    )


def norm_back(grad_output, plain_rows, factor, gain_row):
    scaled = grad_output * gain_row
    grad_input = factor * (
        scaled - plain_rows * jnp.mean(scaled * plain_rows, axis=-1, keepdims=True)
    )
    gain_gradient = jnp.sum(grad_output * plain_rows, axis=0)
    return (grad_input, gain_gradient)


def adamw_update(weight, moment_one, moment_two, gradient, step_rate, decay_rate):
    first_new = BETA_FIRST * moment_one + (1.0 - BETA_FIRST) * gradient
    second_new = BETA_SECOND * moment_two + (1.0 - BETA_SECOND) * gradient * gradient
    first_hat = first_new / (1.0 - BETA_FIRST**STEP)
    second_hat = second_new / (1.0 - BETA_SECOND**STEP)
    weight_new = weight - step_rate * (
        first_hat / (jnp.sqrt(second_hat) + ADAM_EPS) + decay_rate * weight
    )
    return (weight_new, first_new, second_new)


def bits_of(count):
    return count.bit_length() - 1


def tie(value, *others):
    return lax.optimization_barrier((value, others))[0]


class Slice:

    def __init__(self, dp_size, grp_size):
        self.dp_size = dp_size
        self.grp_size = grp_size
        dp_bits = bits_of(dp_size)
        grp_bits = bits_of(grp_size)
        x_count = min(max(grp_bits - 1, 0), dp_bits)
        z_bits = [("dp", bit) for bit in range(dp_bits - 1, x_count - 1, -1)]
        self.far = z_bits[:1]
        self.near = z_bits[1:]
        self.x = [("dp", bit) for bit in range(x_count - 1, -1, -1)]
        self.y = [("grp", bit) for bit in range(1, grp_bits)]
        self.core = [("grp", 0)]
        self.clock = None

    def size(self, axis):
        return self.dp_size if axis == "dp" else self.grp_size

    def own(self, axis, bit):
        return (lax.axis_index(axis) >> bit) & 1

    def swap(self, array, step):
        axis, bit = step
        size = self.size(axis)
        return lax.ppermute(array, axis, [(k, k ^ (1 << bit)) for k in range(size)])

    def in_turn(self, value):
        if self.clock is None:
            return value
        return tie(value, self.clock)

    def by_mask(self, blocks):
        blocks = list(blocks)
        for bit in range(bits_of(self.grp_size)):
            own = self.own("grp", bit)
            blocks = [
                jnp.where(own == 0, block, blocks[k ^ (1 << bit)]) for k, block in enumerate(blocks)
            ]
        return blocks

    def to_masks(self, rows):
        width = rows.shape[1] // self.grp_size
        return self.by_mask([rows[:, k * width : (k + 1) * width] for k in range(self.grp_size)])

    def from_masks(self, blocks):
        return jnp.concatenate(self.by_mask(blocks), axis=1)

    def pair(self, array):
        return jnp.concatenate([array, self.swap(array, self.core[0])], axis=0)

    def pair_blocks(self, blocks):
        own = range(0, self.grp_size, 2)
        came = self.swap(jnp.stack([blocks[m ^ 1] for m in own]), self.core[0])
        return {m: jnp.concatenate([blocks[m], came[n]], axis=0) for n, m in enumerate(own)}


class Gather:

    def __init__(self, net, chunks, bits=()):
        self.net = net
        self.chunks = chunks
        self.bits = list(bits)
        self.sent = None

    def send(self, steps):
        for step in steps:
            self.land()
            self.sent = (step, [self.net.swap(array, step) for _, array in self.chunks])
        return self

    def land(self, join=True, in_turn=False):
        if self.sent is None:
            return self
        (axis, bit), came = self.sent
        self.sent = None
        if in_turn:
            came = self.net.in_turn(came)
        chunks = []
        if axis == "grp":
            for (masks, array), other in zip(self.chunks, came):
                other_masks = [m ^ (1 << bit) for m in masks]
                if join:
                    chunks.append((masks + other_masks, jnp.concatenate([array, other])))
                else:
                    chunks += [(masks, array), (other_masks, other)]
        else:
            own = self.net.own(axis, bit)
            self.bits = sorted(self.bits + [bit], reverse=True)
            place = 1 + self.bits.index(bit)
            for (masks, array), other in zip(self.chunks, came):
                low = jnp.where(own == 0, array, other)
                high = jnp.where(own == 0, other, array)
                chunks.append((masks, jnp.stack([low, high], axis=place)))
        self.chunks = chunks
        if in_turn:
            self.net.clock = came if axis == "grp" and not join else [a for _, a in chunks]
        return self

    def land_next(self, steps, join=True):
        return self.land(join, True).send(steps)

    def rows(self, low, high):
        chunks = [(masks, array[..., low:high, :]) for masks, array in self.chunks]
        return Gather(self.net, chunks, self.bits)

    def pieces(self):
        return {
            mask: array[n].reshape(-1, array.shape[-1])
            for masks, array in self.chunks
            for n, mask in enumerate(masks)
        }


class Sum:

    def __init__(self, net, pieces, low=0, high=None):
        self.net = net
        self.bits = list(range(bits_of(net.dp_size) - 1, -1, -1))
        self.pieces = {
            mask: piece.reshape((2,) * len(self.bits) + (-1, piece.shape[1]))[..., low:high, :]
            for mask, piece in pieces.items()
        }
        self.sent = None
        self.outgoing = None

    def send(self, steps):
        for step in steps[::-1]:
            self.land()
            axis, bit = step
            kept, sent = {}, {}
            if axis == "grp":
                for mask, piece in self.pieces.items():
                    if mask & (1 << bit):
                        sent[mask ^ (1 << bit)] = piece
                    else:
                        kept[mask] = piece
            else:
                own = self.net.own(axis, bit)
                place = self.bits.index(bit)
                self.bits = self.bits[:place] + self.bits[place + 1 :]
                for mask, piece in self.pieces.items():
                    low = lax.index_in_dim(piece, 0, place, keepdims=False)
                    high = lax.index_in_dim(piece, 1, place, keepdims=False)
                    kept[mask] = jnp.where(own == 0, low, high)
                    sent[mask] = jnp.where(own == 0, high, low)
            self.outgoing = {mask: piece.astype(jnp.bfloat16) for mask, piece in sent.items()}
            came = {mask: self.net.swap(piece, step) for mask, piece in self.outgoing.items()}
            self.sent = (kept, came)
        return self

    def land(self, in_turn=False):
        if self.sent is None:
            return self
        kept, came = self.sent
        self.sent = None
        if in_turn:
            came = self.net.in_turn(came)
        self.pieces = {
            mask: kept[mask].astype(jnp.float32) + came[mask].astype(jnp.float32) for mask in kept
        }
        if in_turn:
            self.net.clock = self.pieces
        return self

    def land_next(self, steps):
        return self.land(True).send(steps)

    def owned(self):
        return self.land().pieces[0]


def forward_product(blocks, pieces):
    total = None
    for mask, piece in pieces.items():
        term = lax.dot_general(
            blocks[mask], piece, (((1,), (1,)), ((), ())), preferred_element_type=jnp.float32
        )
        total = term if total is None else total + term
    return total


def backward_product(grad_rows, pieces):
    return [
        jnp.dot(grad_rows, pieces[mask], preferred_element_type=jnp.float32)
        for mask in sorted(pieces)
    ]


def weight_gradient(grad_rows, blocks):
    return {
        mask: lax.dot_general(
            grad_rows, block, (((0,), (0,)), ((), ())), preferred_element_type=jnp.float32
        )
        for mask, block in blocks.items()
    }


def local(
    dp_size,
    grp_size,
    tokens,
    cotangent,
    segments,
    positions,
    w_qkv,
    m_qkv,
    v_qkv,
    w_out,
    m_out,
    v_out,
    w_in,
    m_in,
    v_in,
    w_down,
    m_down,
    v_down,
    gains,
    m_gains,
    v_gains,
):
    net = Slice(dp_size, grp_size)
    low = jnp.bfloat16
    qkv_width = w_qkv.shape[1]
    qkv_out = jnp.concatenate([w_qkv.astype(low).T, w_out.astype(low).T])
    qkv_out = Gather(net, [([0], qkv_out[None])]).send(net.far)
    gate = Gather(net, [([0], w_in[0].astype(low).T[None])]).send(net.y)
    up = Gather(net, [([0], w_in[1].astype(low).T[None])]).send(net.x)
    down = Gather(net, [([0], w_down.astype(low).T[None])]).send(net.far)
    gate.land_next(net.far)
    up.land_next(net.far)
    qkv_out.land_next(net.near)
    down.land_next(net.near)
    qkv_out.land(True, True)
    qkv = qkv_out.rows(0, qkv_width).send(net.x)
    out = qkv_out.rows(qkv_width, None).send(net.y)
    down.land(True, True)
    out.land_next(net.x)
    qkv.land_next(net.y)
    down.chunks = [(masks, net.in_turn(array)) for masks, array in down.chunks]
    down.send(net.y)
    gate.land_next(net.near)
    out.land_next(net.core, False)
    up.land_next(net.near)
    gate.land_next(net.x)
    qkv.land_next(net.core, False)
    qkv.land(False)

    inputs = tokens[0].astype(jnp.float32)
    token_length = inputs.shape[0]
    group_count = QUERY_HEADS // KEY_VALUE_HEADS
    query_width = QUERY_HEADS * HEAD_SIZE
    key_width = KEY_VALUE_HEADS * HEAD_SIZE
    scale_factor = HEAD_SIZE ** (-0.5)
    own_piece = lax.axis_index("grp")
    query_places = own_piece * token_length + jnp.arange(token_length)
    segment_pieces = segments[0].reshape(grp_size, token_length)
    own_segments = lax.dynamic_index_in_dim(segment_pieces, own_piece, 0, keepdims=False)
    key_masks = [0]
    for axis, bit in net.y + net.core:
        key_masks = key_masks + [m ^ (1 << bit) for m in key_masks]
    key_segments = jnp.concatenate(
        [
            lax.dynamic_index_in_dim(segment_pieces, own_piece ^ m, 0, keepdims=False)
            for m in key_masks
        ]
    )
    key_places = jnp.concatenate(
        [(own_piece ^ m) * token_length + jnp.arange(token_length) for m in key_masks]
    )
    allowed = (key_places[None, :] <= query_places[:, None]) & (
        key_segments[None, :] == own_segments[:, None]
    )
    rotary_cosine, rotary_sine = rotation(positions[0])
    factor_one = lax.rsqrt(jnp.mean(inputs * inputs, axis=-1, keepdims=True) + NORM_EPS)
    plain_one = inputs * factor_one
    normed = (plain_one * gains[0]).astype(low)
    normed_blocks = net.to_masks(normed)
    blended_rows = forward_product(normed_blocks, qkv.pieces())
    query_rows = apply_rotary(
        blended_rows[:, :query_width].reshape(token_length, QUERY_HEADS, HEAD_SIZE),
        rotary_cosine,
        rotary_sine,
    ).astype(low)
    own_keys = apply_rotary(
        blended_rows[:, query_width : query_width + key_width].reshape(
            token_length, KEY_VALUE_HEADS, HEAD_SIZE
        ),
        rotary_cosine,
        rotary_sine,
    )
    own_keys = own_keys.astype(low).reshape(token_length, key_width)
    own_values = blended_rows[:, query_width + key_width :].astype(low)
    keys_values = jnp.concatenate([own_keys, own_values], axis=1)
    up.land(True, True)
    up.chunks = [(masks, tie(array, keys_values)) for masks, array in up.chunks]
    up.send(net.y)
    for step in net.y + net.core:
        keys_values = jnp.concatenate([keys_values, net.swap(keys_values, step)], axis=0)
    down.land_next(net.x)
    rows_of_keys = keys_values[:, :key_width]
    rows_of_values = keys_values[:, key_width:]
    grouped_heads = query_rows.reshape(token_length, KEY_VALUE_HEADS, group_count, HEAD_SIZE)

    def scores_of(group_of_head, key_all):
        key_block = key_all[:, group_of_head * HEAD_SIZE : (group_of_head + 1) * HEAD_SIZE]
        raw_scores = (
            jnp.einsum(
                "trd,sd->rts",
                grouped_heads[:, group_of_head],
                key_block,
                preferred_element_type=jnp.float32,
            )
            * scale_factor
        )
        return jnp.where(allowed[None], raw_scores, MASKED)

    outputs = []
    log_totals = []
    for group_of_head in range(KEY_VALUE_HEADS):
        masked = scores_of(group_of_head, rows_of_keys)
        row_peak = jnp.max(masked, axis=-1, keepdims=True)
        exponent = jnp.exp(masked - row_peak)
        row_total = jnp.sum(exponent, axis=-1, keepdims=True)
        probability = exponent / row_total
        log_totals.append(row_peak + jnp.log(row_total))
        value_block = rows_of_values[:, group_of_head * HEAD_SIZE : (group_of_head + 1) * HEAD_SIZE]
        outputs.append(
            jnp.einsum(
                "rts,sd->trd",
                probability.astype(low),
                value_block,
                preferred_element_type=jnp.float32,
            )
        )
    attended_low = jnp.concatenate(outputs, axis=1).reshape(token_length, query_width).astype(low)
    attended_blocks = net.to_masks(attended_low)
    net.clock = attended_low
    gate.land_next(net.core)
    up.land_next(net.core, False)
    down.land_next(net.core)
    gate, up, down, out = [part.land(False).pieces() for part in (gate, up, down, out)]
    middle = inputs + forward_product(attended_blocks, out)
    factor_two = lax.rsqrt(jnp.mean(middle * middle, axis=-1, keepdims=True) + NORM_EPS)
    plain_two = middle * factor_two
    normed_two = (plain_two * gains[1]).astype(low)
    normed_two_blocks = net.to_masks(normed_two)
    gate_pre = forward_product(normed_two_blocks, gate)
    up_proj = forward_product(normed_two_blocks, up)
    sigmoid_gate = jax.nn.sigmoid(gate_pre)
    activated = gate_pre * sigmoid_gate
    hidden = (activated * up_proj).astype(low)
    hidden_blocks = net.to_masks(hidden)
    layer_out = middle + forward_product(hidden_blocks, down)

    upstream = cotangent[0].astype(jnp.float32)
    upstream_low = cotangent[0]
    upstream_pair = net.pair(upstream_low)
    grad_down = Sum(net, weight_gradient(upstream_pair, net.pair_blocks(hidden_blocks)))
    grad_hidden = net.from_masks(backward_product(upstream_low, down))
    grad_gate = (
        grad_hidden * up_proj * sigmoid_gate * (1.0 + gate_pre * (1.0 - sigmoid_gate))
    ).astype(low)
    grad_up = (grad_hidden * activated).astype(low)
    normed_two_pair = net.pair_blocks(normed_two_blocks)
    grad_in_gate = Sum(net, weight_gradient(net.pair(grad_gate), normed_two_pair))
    grad_in_up = Sum(net, weight_gradient(net.pair(grad_up), normed_two_pair))
    grad_normed_two = net.from_masks(
        [
            one + two
            for one, two in zip(
                backward_product(grad_gate, gate), backward_product(grad_up, up)
            )
        ]
    )
    back_two, gain_two = norm_back(grad_normed_two, plain_two, factor_two, gains[1])
    grad_middle = upstream + back_two
    middle_low = grad_middle.astype(low)
    grad_out = Sum(
        net, weight_gradient(net.pair(middle_low), net.pair_blocks(attended_blocks))
    )
    attended_gradient = net.from_masks(backward_product(middle_low, out))
    attended_gradient = attended_gradient.astype(low).reshape(
        token_length, KEY_VALUE_HEADS, group_count, HEAD_SIZE
    )
    grad_down.send(net.x)
    grad_in_up.send(net.y)
    grad_in_gate.send(net.x)
    grad_out.send(net.x)
    beside = {
        0: grad_down.outgoing,
        1: (grad_in_up.outgoing, grad_in_gate.outgoing),
        2: grad_out.outgoing,
    }
    grads_query = []
    grads_key = []
    grads_value = []
    for group_of_head in range(KEY_VALUE_HEADS):
        masked = scores_of(group_of_head, rows_of_keys)
        probability = jnp.exp(masked - log_totals[group_of_head])
        key_block = rows_of_keys[:, group_of_head * HEAD_SIZE : (group_of_head + 1) * HEAD_SIZE]
        value_block = rows_of_values[:, group_of_head * HEAD_SIZE : (group_of_head + 1) * HEAD_SIZE]
        if group_of_head == 3:
            net.clock = grads_query[-1]
            beside[3] = grad_down.land_next(net.near).outgoing
        grad_block = attended_gradient[:, group_of_head]
        if group_of_head in beside:
            grad_block = tie(grad_block, beside[group_of_head])
        grad_probs = jnp.einsum(
            "trd,sd->rts", grad_block, value_block, preferred_element_type=jnp.float32
        )
        grads_value.append(
            jnp.einsum(
                "rts,trd->sd",
                probability.astype(low),
                grad_block,
                preferred_element_type=jnp.float32,
            )
        )
        grad_scores = probability * (
            grad_probs - jnp.sum(probability * grad_probs, axis=-1, keepdims=True)
        )
        grad_scores = grad_scores.astype(low)
        grads_query.append(
            jnp.einsum("rts,sd->trd", grad_scores, key_block, preferred_element_type=jnp.float32)
            * scale_factor
        )
        grads_key.append(
            jnp.einsum(
                "rts,trd->sd",
                grad_scores,
                grouped_heads[:, group_of_head],
                preferred_element_type=jnp.float32,
            )
            * scale_factor
        )
    grad_keys_values = jnp.concatenate(grads_key + grads_value, axis=1)
    net.clock = grad_keys_values
    for step in net.core + net.y[::-1]:
        half = grad_keys_values.shape[0] // 2
        came = net.swap(grad_keys_values[half:].astype(low), step)
        if step == net.core[0]:
            grad_down.land_next(net.far)
            came = net.in_turn(came)
        else:
            if step == net.y[-1]:
                grad_in_up.land_next(net.near)
                grad_in_gate.land_next(net.y)
            came = net.in_turn(came)
        grad_keys_values = grad_keys_values[:half] + came.astype(jnp.float32)
        net.clock = grad_keys_values
    grad_queries = jnp.concatenate(grads_query, axis=1)
    grad_mixed = jnp.concatenate(
        [
            inverse_rotary(grad_queries, rotary_cosine, rotary_sine).reshape(
                token_length, query_width
            ),
            inverse_rotary(
                grad_keys_values[:, :key_width].reshape(token_length, KEY_VALUE_HEADS, HEAD_SIZE),
                rotary_cosine,
                rotary_sine,
            ).reshape(token_length, key_width),
            grad_keys_values[:, key_width:],
        ],
        axis=1,
    ).astype(low)
    mixed_pair = net.pair(grad_mixed)
    net.clock = grad_mixed
    grad_down.land_next(net.y)
    grad_qkv = weight_gradient(tie(mixed_pair, net.clock), net.pair_blocks(normed_blocks))
    cut = qkv_width // 16 * 8
    first_qkv = Sum(net, grad_qkv, 0, cut).send(net.y)
    second_qkv = Sum(net, grad_qkv, cut).send(net.x)
    net.clock = (first_qkv.outgoing, second_qkv.outgoing)
    grad_in_up.land_next(net.far)
    grad_out.land_next(net.y)
    grad_in_gate.land_next(net.near)
    first_qkv.land_next(net.x)
    second_qkv.land_next(net.y)
    grad_normed = net.from_masks(backward_product(grad_mixed, qkv.pieces()))
    back_one, gain_one = norm_back(grad_normed, plain_one, factor_one, gains[0])
    tokens_grad = grad_middle + back_one
    gain_grads = jnp.stack([gain_one, gain_two])
    for step in net.core + net.y + net.x + net.near + net.far:
        gain_grads = gain_grads + net.swap(gain_grads, step)
    grad_in_up.land_next(net.x)
    grad_out.land_next(net.near)
    grad_in_gate.land_next(net.far)
    first_qkv.land_next(net.near)
    second_qkv.land_next(net.near)
    grad_out.land_next(net.far)
    first_qkv.land_next(net.far)
    second_qkv.land_next(net.far)
    owned_down = grad_down.owned()
    owned_in = jnp.stack([grad_in_gate.owned(), grad_in_up.owned()])
    owned_out = grad_out.owned()
    owned_qkv = jnp.concatenate([first_qkv.owned(), second_qkv.owned()])
    new_qkv, mom_qkv, sq_qkv = adamw_update(
        w_qkv, m_qkv, v_qkv, owned_qkv.T, RATE_MATRIX, WEIGHT_DECAY
    )
    new_out, mom_out, sq_out = adamw_update(
        w_out, m_out, v_out, owned_out.T, RATE_MATRIX, WEIGHT_DECAY
    )
    new_in, mom_in, sq_in = adamw_update(
        w_in, m_in, v_in, owned_in.transpose(0, 2, 1), RATE_MATRIX, WEIGHT_DECAY
    )
    new_down, mom_down, sq_down = adamw_update(
        w_down, m_down, v_down, owned_down.T, RATE_MATRIX, WEIGHT_DECAY
    )
    new_gains, mom_gains, sq_gains = adamw_update(
        gains, m_gains, v_gains, gain_grads, RATE_GAIN, 0.0
    )
    return (
        layer_out[None],
        tokens_grad[None],
        new_qkv,
        mom_qkv,
        sq_qkv,
        new_out,
        mom_out,
        sq_out,
        new_in,
        mom_in,
        sq_in,
        new_down,
        mom_down,
        sq_down,
        new_gains,
        mom_gains,
        sq_gains,
    )


def solution(mesh):
    return jax.shard_map(
        partial(local, mesh.shape["dp"], mesh.shape["grp"]),
        mesh=mesh,
        in_specs=(
            P("dp", "grp", None),
            P("dp", "grp", None),
            P("dp", None),
            P("dp", "grp"),
            P("grp", "dp"),
            P("grp", "dp"),
            P("grp", "dp"),
            P("grp", "dp"),
            P("grp", "dp"),
            P("grp", "dp"),
            P(None, "grp", "dp"),
            P(None, "grp", "dp"),
            P(None, "grp", "dp"),
            P("grp", "dp"),
            P("grp", "dp"),
            P("grp", "dp"),
            P(),
            P(),
            P(),
        ),
        out_specs=(
            P("dp", "grp", None),
            P("dp", "grp", None),
            P("grp", "dp"),
            P("grp", "dp"),
            P("grp", "dp"),
            P("grp", "dp"),
            P("grp", "dp"),
            P("grp", "dp"),
            P(None, "grp", "dp"),
            P(None, "grp", "dp"),
            P(None, "grp", "dp"),
            P("grp", "dp"),
            P("grp", "dp"),
            P("grp", "dp"),
            P(),
            P(),
            P(),
        ),
        check_vma=False,
    )
```

```python
import math
from functools import partial

import jax
import jax.numpy as jnp
from jax import lax
from jax.experimental import pallas as pl
from jax.experimental.pallas import tpu as pltpu
from jax.sharding import PartitionSpec as P

QUERY_HEADS = 15
KEY_VALUE_HEADS = 5
HEAD_SIZE = 64
STEP = 10


NORM_EPS = 1e-05
ROPE_BASE = 10000.0
MASKED = -1e30
BETA_FIRST = 0.9
BETA_SECOND = 0.95
ADAM_EPS = 1e-08
WEIGHT_DECAY = 0.1
RATE_MATRIX = 0.05
RATE_GAIN = 0.3


def rotation(places_in_doc):
    frequency = ROPE_BASE ** (-(jnp.arange(HEAD_SIZE // 2).astype(jnp.float32) * 2.0 / HEAD_SIZE))
    angles = places_in_doc.astype(jnp.float32)[:, None] * frequency[None, :]
    return (jnp.cos(angles)[:, None, :], jnp.sin(angles)[:, None, :])


def apply_rotary(head_rows, rotary_cosine, rotary_sine):
    half_width = head_rows.shape[-1] // 2
    front_half = head_rows[..., :half_width]
    back_half = head_rows[..., half_width:]
    return jnp.concatenate(
        [
            front_half * rotary_cosine - back_half * rotary_sine,
            back_half * rotary_cosine + front_half * rotary_sine,
        ],
        axis=-1,
    )


def inverse_rotary(grad_rows, rotary_cosine, rotary_sine):
    half_width = grad_rows.shape[-1] // 2
    front_half = grad_rows[..., :half_width]
    back_half = grad_rows[..., half_width:]
    return jnp.concatenate(
        [
            front_half * rotary_cosine + back_half * rotary_sine,
            back_half * rotary_cosine - front_half * rotary_sine,
        ],
        axis=-1,
    )


def norm_back(grad_output, plain_rows, factor, gain_row):
    scaled = grad_output * gain_row
    grad_input = factor * (
        scaled - plain_rows * jnp.mean(scaled * plain_rows, axis=-1, keepdims=True)
    )
    gain_gradient = jnp.sum(grad_output * plain_rows, axis=0)
    return (grad_input, gain_gradient)


def adamw_update(weight, moment_one, moment_two, gradient, step_rate, decay_rate):
    first_new = BETA_FIRST * moment_one + (1.0 - BETA_FIRST) * gradient
    second_new = BETA_SECOND * moment_two + (1.0 - BETA_SECOND) * gradient * gradient
    first_hat = first_new / (1.0 - BETA_FIRST**STEP)
    second_hat = second_new / (1.0 - BETA_SECOND**STEP)
    weight_new = weight - step_rate * (
        first_hat / (jnp.sqrt(second_hat) + ADAM_EPS) + decay_rate * weight
    )
    return (weight_new, first_new, second_new)


def bits_of(count):
    return count.bit_length() - 1


def tie(value, *others):
    return lax.optimization_barrier((value, others))[0]


TRANSPOSED = (((1,), (1,)), ((), ()))
FLAT = (((1,), (0,)), ((), ()))


def product(left, right, dims):
    return lax.dot_general(left, right, dims, preferred_element_type=jnp.float32)


def attend_kernel(query_ref, key_ref, value_ref, bias_ref, out_ref, total_ref):
    keys = key_ref[0]
    values_across = value_ref[0].T
    for head in range(query_ref.shape[1]):
        scores = product(keys, query_ref[0, head], TRANSPOSED) * HEAD_SIZE ** (-0.5) + bias_ref[...]
        peak = jnp.max(scores, axis=0, keepdims=True)
        exponent = jnp.exp(scores - peak)
        total = jnp.sum(exponent, axis=0, keepdims=True)
        probability = exponent * (1.0 / total)
        attended = product(values_across, probability.astype(jnp.bfloat16), FLAT)
        out_ref[0, head] = attended.T.astype(jnp.bfloat16)
        total_ref[0, head : head + 1] = peak + jnp.log(total)


def attend_back_kernel(
    query_ref, key_ref, value_ref, bias_ref, total_ref, grad_ref, query_grad, key_grad, value_grad
):
    keys = key_ref[0]
    values = value_ref[0]
    keys_across = keys.T
    for head in range(query_ref.shape[1]):
        queries = query_ref[0, head]
        grads = grad_ref[0, head]
        scores = product(keys, queries, TRANSPOSED) * HEAD_SIZE ** (-0.5) + bias_ref[...]
        probability = jnp.exp(scores - total_ref[0, head : head + 1])
        grad_probs = product(values, grads, TRANSPOSED)
        from_values = product(probability.astype(jnp.bfloat16), grads, FLAT)
        weighted = probability * grad_probs
        grad_scores = weighted - probability * jnp.sum(weighted, axis=0, keepdims=True)
        grad_scores = grad_scores.astype(jnp.bfloat16)
        from_queries = product(grad_scores, queries, FLAT) * HEAD_SIZE ** (-0.5)
        query_grad[0, head] = (product(keys_across, grad_scores, FLAT) * HEAD_SIZE ** (-0.5)).T
        if head == 0:
            key_grad[0] = from_queries
            value_grad[0] = from_values
        else:
            key_grad[0] += from_queries
            value_grad[0] += from_values


def group_block(array):
    zeros = (0,) * (array.ndim - 1)
    return pl.BlockSpec((1,) + array.shape[1:], lambda g: (g,) + zeros)


def whole_block(array):
    zeros = (0,) * array.ndim
    return pl.BlockSpec(array.shape, lambda g: zeros)


def attend(queries, keys, values, bias):
    groups, heads, length, _ = queries.shape
    work = queries.size * keys.shape[1]
    totals = jax.ShapeDtypeStruct((groups, heads, length), jnp.float32)
    return pl.pallas_call(
        attend_kernel,
        grid=(groups,),
        in_specs=[group_block(a) for a in (queries, keys, values)] + [whole_block(bias)],
        out_specs=[group_block(queries), group_block(totals)],
        out_shape=[jax.ShapeDtypeStruct(queries.shape, queries.dtype), totals],
        compiler_params=pltpu.CompilerParams(vmem_limit_bytes=40 << 20),
        cost_estimate=pl.CostEstimate(
            flops=work, bytes_accessed=1 << 20, transcendentals=0
        ),
    )(queries, keys, values, bias)


def attend_back(queries, keys, values, bias, totals, grads):
    work = queries.size * keys.shape[1]
    args = (queries, keys, values, bias, totals, grads)
    shapes = [jax.ShapeDtypeStruct(a.shape, jnp.float32) for a in (queries, keys, values)]
    specs = [group_block(a) for a in args]
    specs[3] = whole_block(bias)
    return pl.pallas_call(
        attend_back_kernel,
        grid=(queries.shape[0],),
        in_specs=specs,
        out_specs=[group_block(a) for a in shapes],
        out_shape=shapes,
        compiler_params=pltpu.CompilerParams(vmem_limit_bytes=40 << 20),
        cost_estimate=pl.CostEstimate(
            flops=work, bytes_accessed=1 << 20, transcendentals=0
        ),
    )(*args)


class Slice:

    def __init__(self, dp_size, grp_size):
        self.dp_size = dp_size
        self.grp_size = grp_size
        dp_bits = bits_of(dp_size)
        grp_bits = bits_of(grp_size)
        x_count = min(max(grp_bits - 1, 0), dp_bits)
        z_bits = [("dp", bit) for bit in range(dp_bits - 1, x_count - 1, -1)]
        self.far = z_bits[:1]
        self.near = z_bits[1:]
        self.x = [("dp", bit) for bit in range(x_count - 1, -1, -1)]
        self.y = [("grp", bit) for bit in range(1, grp_bits)]
        self.core = [("grp", 0)]
        self.clock = None

    def size(self, axis):
        return self.dp_size if axis == "dp" else self.grp_size

    def own(self, axis, bit):
        return (lax.axis_index(axis) >> bit) & 1

    def swap(self, array, step):
        axis, bit = step
        size = self.size(axis)
        return lax.ppermute(array, axis, [(k, k ^ (1 << bit)) for k in range(size)])

    def in_turn(self, value):
        if self.clock is None:
            return value
        return tie(value, self.clock)

    def by_mask(self, blocks):
        blocks = list(blocks)
        for bit in range(bits_of(self.grp_size)):
            own = self.own("grp", bit)
            blocks = [
                jnp.where(own == 0, block, blocks[k ^ (1 << bit)]) for k, block in enumerate(blocks)
            ]
        return blocks

    def to_masks(self, rows):
        width = rows.shape[1] // self.grp_size
        return self.by_mask([rows[:, k * width : (k + 1) * width] for k in range(self.grp_size)])

    def from_masks(self, blocks):
        return jnp.concatenate(self.by_mask(blocks), axis=1)

    def pair(self, array):
        return jnp.concatenate([array, self.swap(array, self.core[0])], axis=0)

    def pair_blocks(self, blocks):
        own = range(0, self.grp_size, 2)
        came = self.swap(jnp.stack([blocks[m ^ 1] for m in own]), self.core[0])
        return {m: jnp.concatenate([blocks[m], came[n]], axis=0) for n, m in enumerate(own)}


class Gather:

    def __init__(self, net, chunks, bits=()):
        self.net = net
        self.chunks = chunks
        self.bits = list(bits)
        self.sent = None

    def send(self, steps):
        for step in steps:
            self.land()
            self.sent = (step, [self.net.swap(array, step) for _, array in self.chunks])
        return self

    def land(self, join=True, in_turn=False):
        if self.sent is None:
            return self
        (axis, bit), came = self.sent
        self.sent = None
        if in_turn:
            came = self.net.in_turn(came)
        chunks = []
        if axis == "grp":
            for (masks, array), other in zip(self.chunks, came):
                other_masks = [m ^ (1 << bit) for m in masks]
                if join:
                    chunks.append((masks + other_masks, jnp.concatenate([array, other])))
                else:
                    chunks += [(masks, array), (other_masks, other)]
        else:
            own = self.net.own(axis, bit)
            self.bits = sorted(self.bits + [bit], reverse=True)
            place = 1 + self.bits.index(bit)
            for (masks, array), other in zip(self.chunks, came):
                low = jnp.where(own == 0, array, other)
                high = jnp.where(own == 0, other, array)
                chunks.append((masks, jnp.stack([low, high], axis=place)))
        self.chunks = chunks
        if in_turn:
            self.net.clock = came if axis == "grp" and not join else [a for _, a in chunks]
        return self

    def land_next(self, steps, join=True):
        return self.land(join, True).send(steps)

    def rows(self, low, high):
        chunks = [(masks, array[..., low:high, :]) for masks, array in self.chunks]
        return Gather(self.net, chunks, self.bits)

    def pieces(self):
        return {
            mask: array[n].reshape(-1, array.shape[-1])
            for masks, array in self.chunks
            for n, mask in enumerate(masks)
        }


class Sum:

    def __init__(self, net, pieces, low=0, high=None):
        self.net = net
        self.bits = list(range(bits_of(net.dp_size) - 1, -1, -1))
        self.pieces = {
            mask: piece.reshape((2,) * len(self.bits) + (-1, piece.shape[1]))[..., low:high, :]
            for mask, piece in pieces.items()
        }

    def split(self, step):
        axis, bit = step
        kept, sent = {}, {}
        if axis == "grp":
            for mask, piece in self.pieces.items():
                if mask & (1 << bit):
                    sent[mask ^ (1 << bit)] = piece
                else:
                    kept[mask] = piece
        else:
            own = self.net.own(axis, bit)
            place = self.bits.index(bit)
            self.bits = self.bits[:place] + self.bits[place + 1 :]
            for mask, piece in self.pieces.items():
                low = lax.index_in_dim(piece, 0, place, keepdims=False)
                high = lax.index_in_dim(piece, 1, place, keepdims=False)
                kept[mask] = jnp.where(own == 0, low, high)
                sent[mask] = jnp.where(own == 0, high, low)
        self.pieces = kept
        return sent

    def owned(self):
        return self.pieces[0]


class Bundle:

    def __init__(self, net, *sums):
        self.net = net
        self.sums = sums
        self.sent = None

    def send(self, steps):
        for step in steps[::-1]:
            self.land()
            places, packed = [], []
            for part in self.sums:
                for mask, piece in part.split(step).items():
                    places.append((part, mask, piece.shape))
                    packed.append(piece.astype(jnp.bfloat16).reshape(-1, piece.shape[-1]))
            self.outgoing = jnp.concatenate(packed)
            self.sent = (places, self.net.swap(self.outgoing, step))
        return self

    def land(self, in_turn=False):
        if self.sent is None:
            return self
        places, came = self.sent
        self.sent = None
        if in_turn:
            came = self.net.in_turn(came)
        at = 0
        for part, mask, shape in places:
            rows = came[at : at + math.prod(shape[:-1])]
            at += rows.shape[0]
            part.pieces[mask] = part.pieces[mask].astype(jnp.float32) + rows.reshape(
                shape
            ).astype(jnp.float32)
        if in_turn:
            self.net.clock = [part.pieces for part in self.sums]
        return self

    def land_next(self, steps):
        return self.land(True).send(steps)


def forward_product(blocks, pieces):
    total = None
    for mask, piece in pieces.items():
        term = lax.dot_general(
            blocks[mask], piece, (((1,), (1,)), ((), ())), preferred_element_type=jnp.float32
        )
        total = term if total is None else total + term
    return total


def backward_product(grad_rows, pieces):
    return [
        jnp.dot(grad_rows, pieces[mask], preferred_element_type=jnp.float32)
        for mask in sorted(pieces)
    ]


def weight_gradient(grad_rows, blocks):
    return {
        mask: lax.dot_general(
            grad_rows, block, (((0,), (0,)), ((), ())), preferred_element_type=jnp.float32
        )
        for mask, block in blocks.items()
    }


def local(
    dp_size,
    grp_size,
    tokens,
    cotangent,
    segments,
    positions,
    w_qkv,
    m_qkv,
    v_qkv,
    w_out,
    m_out,
    v_out,
    w_in,
    m_in,
    v_in,
    w_down,
    m_down,
    v_down,
    gains,
    m_gains,
    v_gains,
):
    net = Slice(dp_size, grp_size)
    low = jnp.bfloat16
    qkv_width = w_qkv.shape[1]
    qkv_out = jnp.concatenate([w_qkv.astype(low).T, w_out.astype(low).T])
    qkv_out = Gather(net, [([0], qkv_out[None])]).send(net.far)
    gate = Gather(net, [([0], w_in[0].astype(low).T[None])]).send(net.y)
    up = Gather(net, [([0], w_in[1].astype(low).T[None])]).send(net.x)
    down_low = w_down.astype(low).T[None]
    upstream_low = cotangent[0]
    upstream_pair = net.pair(upstream_low)
    qkv_out.land_next(net.near)
    down = Gather(net, [([0], net.in_turn(down_low))]).send(net.far)
    upstream_pair = net.in_turn(upstream_pair)
    net.clock = upstream_pair
    qkv_out.land(True, True)
    qkv = qkv_out.rows(0, qkv_width).send(net.x)
    out = qkv_out.rows(qkv_width, None).send(net.y)
    gate.land_next(net.far)
    down.land_next(net.near)
    out.land_next(net.x)
    down.land_next(net.y)
    qkv.land_next(net.y)
    up.land_next(net.far)
    gate.land_next(net.near)
    out.land_next(net.core)
    up.land_next(net.near)
    gate.land_next(net.x)
    qkv.land_next(net.core)
    qkv.land(False)
    down.land_next(net.x)

    inputs = tokens[0].astype(jnp.float32)
    token_length = inputs.shape[0]
    group_count = QUERY_HEADS // KEY_VALUE_HEADS
    query_width = QUERY_HEADS * HEAD_SIZE
    key_width = KEY_VALUE_HEADS * HEAD_SIZE
    scale_factor = HEAD_SIZE ** (-0.5)
    own_piece = lax.axis_index("grp")
    query_places = own_piece * token_length + jnp.arange(token_length)
    segment_pieces = segments[0].reshape(grp_size, token_length)
    own_segments = lax.dynamic_index_in_dim(segment_pieces, own_piece, 0, keepdims=False)
    key_masks = [0]
    for axis, bit in net.y + net.core:
        key_masks = key_masks + [m ^ (1 << bit) for m in key_masks]
    key_segments = jnp.concatenate(
        [
            lax.dynamic_index_in_dim(segment_pieces, own_piece ^ m, 0, keepdims=False)
            for m in key_masks
        ]
    )
    key_places = jnp.concatenate(
        [(own_piece ^ m) * token_length + jnp.arange(token_length) for m in key_masks]
    )
    allowed = (key_places[:, None] <= query_places[None, :]) & (
        key_segments[:, None] == own_segments[None, :]
    )
    bias = jnp.where(allowed, 0.0, MASKED)
    rotary_cosine, rotary_sine = rotation(positions[0])
    factor_one = lax.rsqrt(jnp.mean(inputs * inputs, axis=-1, keepdims=True) + NORM_EPS)
    plain_one = inputs * factor_one
    normed = (plain_one * gains[0]).astype(low)
    normed_blocks = net.to_masks(normed)
    normed_pair = net.pair_blocks(normed_blocks)
    blended_rows = forward_product(normed_blocks, qkv.pieces())
    query_rows = apply_rotary(
        blended_rows[:, :query_width].reshape(token_length, QUERY_HEADS, HEAD_SIZE),
        rotary_cosine,
        rotary_sine,
    ).astype(low)
    own_keys = apply_rotary(
        blended_rows[:, query_width : query_width + key_width].reshape(
            token_length, KEY_VALUE_HEADS, HEAD_SIZE
        ),
        rotary_cosine,
        rotary_sine,
    )
    own_keys = own_keys.astype(low).reshape(token_length, key_width)
    own_values = blended_rows[:, query_width + key_width :].astype(low)
    keys_values = jnp.concatenate([own_keys, own_values], axis=1)
    up.land(True, True)
    up.chunks = [(masks, tie(array, keys_values)) for masks, array in up.chunks]
    up.send(net.y)
    for step in net.y + net.core:
        keys_values = jnp.concatenate([keys_values, net.swap(keys_values, step)], axis=0)

    def by_group(rows):
        return rows.reshape(rows.shape[0], KEY_VALUE_HEADS, -1, HEAD_SIZE).transpose(1, 2, 0, 3)

    def by_row(groups):
        return groups.transpose(2, 0, 1, 3).reshape(groups.shape[2], -1)

    group_keys = by_group(keys_values[:, :key_width])[:, 0]
    group_values = by_group(keys_values[:, key_width:])[:, 0]
    group_queries = by_group(query_rows.reshape(token_length, query_width))
    attended, log_totals = attend(group_queries, group_keys, group_values, bias)
    attended_low = by_row(attended)
    attended_blocks = net.to_masks(attended_low)
    net.clock = attended_low
    gate.land_next(net.core)
    up.land_next(net.core, False)
    down.land_next(net.core)
    gate, up, down, out = [part.land(False).pieces() for part in (gate, up, down, out)]
    middle = inputs + forward_product(attended_blocks, out)
    factor_two = lax.rsqrt(jnp.mean(middle * middle, axis=-1, keepdims=True) + NORM_EPS)
    plain_two = middle * factor_two
    normed_two = (plain_two * gains[1]).astype(low)
    normed_two_blocks = net.to_masks(normed_two)
    gate_pre = forward_product(normed_two_blocks, gate)
    up_proj = forward_product(normed_two_blocks, up)
    sigmoid_gate = jax.nn.sigmoid(gate_pre)
    activated = gate_pre * sigmoid_gate
    hidden = (activated * up_proj).astype(low)
    hidden_blocks = net.to_masks(hidden)
    layer_out = middle + forward_product(hidden_blocks, down)

    upstream = cotangent[0].astype(jnp.float32)
    grad_down = weight_gradient(upstream_pair, net.pair_blocks(hidden_blocks))
    down_cut = w_down.shape[1] // 16 * 8
    sum_down = (Sum(net, grad_down, 0, down_cut), Sum(net, grad_down, down_cut))
    first_down = Bundle(net, sum_down[0]).send(net.x)
    second_down = Bundle(net, sum_down[1]).send(net.y)
    grad_hidden = net.from_masks(backward_product(upstream_low, down))
    grad_gate = (
        grad_hidden * up_proj * sigmoid_gate * (1.0 + gate_pre * (1.0 - sigmoid_gate))
    ).astype(low)
    grad_up = (grad_hidden * activated).astype(low)
    normed_two_pair = net.pair_blocks(normed_two_blocks)
    sum_gate = Sum(net, weight_gradient(net.pair(grad_gate), normed_two_pair))
    sum_up = Sum(net, weight_gradient(net.pair(grad_up), normed_two_pair))
    grad_in_gate = Bundle(net, sum_gate).send(net.x)
    grad_in_up = Bundle(net, sum_up).send(net.y)
    grad_normed_two = net.from_masks(
        [
            one + two
            for one, two in zip(
                backward_product(grad_gate, gate), backward_product(grad_up, up)
            )
        ]
    )
    back_two, gain_two = norm_back(grad_normed_two, plain_two, factor_two, gains[1])
    grad_middle = upstream + back_two
    middle_low = grad_middle.astype(low)
    attended_gradient = net.from_masks(backward_product(middle_low, out))
    outgoing = [part.outgoing for part in (first_down, second_down, grad_in_up, grad_in_gate)]
    grad_queries, grad_keys, grad_values = attend_back(
        group_queries,
        group_keys,
        group_values,
        bias,
        log_totals,
        tie(by_group(attended_gradient.astype(low)), outgoing),
    )
    grad_keys_values = jnp.concatenate(
        [by_row(grad_keys[:, None]), by_row(grad_values[:, None])], axis=1
    )
    grad_queries = by_row(grad_queries).reshape(token_length, QUERY_HEADS, HEAD_SIZE)
    net.clock = grad_keys_values
    for step in net.core + net.y[::-1]:
        half = grad_keys_values.shape[0] // 2
        came = net.swap(grad_keys_values[half:].astype(low), step)
        if step == net.y[-1]:
            first_down.land(True)
            second_down.land(True)
            both_down = Bundle(net, *sum_down).send(net.near)
            middle_pair = tie(net.pair(middle_low), net.clock)
            attended_pair = net.pair_blocks(attended_blocks)
            sum_out = Sum(net, weight_gradient(middle_pair, attended_pair))
            grad_out = Bundle(net, sum_out).send(net.x)
            grad_in_up.land_next(net.x)
            grad_in_gate.land_next(net.y)
        came = net.in_turn(came)
        grad_keys_values = grad_keys_values[:half] + came.astype(jnp.float32)
        net.clock = grad_keys_values
    grad_mixed = jnp.concatenate(
        [
            inverse_rotary(grad_queries, rotary_cosine, rotary_sine).reshape(
                token_length, query_width
            ),
            inverse_rotary(
                grad_keys_values[:, :key_width].reshape(token_length, KEY_VALUE_HEADS, HEAD_SIZE),
                rotary_cosine,
                rotary_sine,
            ).reshape(token_length, key_width),
            grad_keys_values[:, key_width:],
        ],
        axis=1,
    ).astype(low)
    net.clock = grad_mixed
    both_down.land_next(net.far)
    grad_out.land(True)
    mixed_pair = net.in_turn(net.pair(grad_mixed))
    grad_qkv = weight_gradient(mixed_pair, normed_pair)
    cut = qkv_width // 16 * 8
    sum_qkv = (Sum(net, grad_qkv, 0, cut), Sum(net, grad_qkv, cut))
    first_qkv = Bundle(net, sum_qkv[0]).send(net.y)
    second_qkv = Bundle(net, sum_qkv[1]).send(net.x)
    net.clock = (first_qkv.outgoing, second_qkv.outgoing)
    grad_normed = net.from_masks(backward_product(tie(grad_mixed, net.clock), qkv.pieces()))
    back_one, gain_one = norm_back(grad_normed, plain_one, factor_one, gains[0])
    tokens_grad = grad_middle + back_one
    gain_grads = jnp.stack([gain_one, gain_two])

    def gain_steps(gain_grads, steps):
        for step in steps:
            gain_grads = gain_grads + net.in_turn(net.swap(gain_grads, step))
            net.clock = gain_grads
        return gain_grads

    grad_in_up.land(True)
    grad_in_gate.land(True)
    both_in = Bundle(net, sum_up, sum_gate).send(net.near)
    grad_out.send(net.y)
    gain_grads = gain_steps(gain_grads, net.core)
    first_qkv.land_next(net.x)
    second_qkv.land_next(net.y)
    gain_grads = gain_steps(gain_grads, net.y)
    both_down.land(True)
    first_down.send(net.y)
    second_down.send(net.x)
    grad_out.land(True)
    gain_grads = gain_steps(gain_grads, net.x)
    both_in.land_next(net.far)
    first_qkv.land(True)
    second_qkv.land(True)
    rest = Bundle(net, sum_out, *sum_qkv).send(net.near)
    gain_grads = gain_steps(gain_grads, net.near)
    first_down.land(True)
    second_down.land(True)
    both_in.land(True)
    rest.land_next(net.far)
    gain_grads = gain_steps(gain_grads, net.far)
    rest.land(True)
    owned_down = jnp.concatenate([part.owned() for part in sum_down])
    owned_in = jnp.stack([sum_gate.owned(), sum_up.owned()])
    owned_out = sum_out.owned()
    owned_qkv = jnp.concatenate([part.owned() for part in sum_qkv])
    new_qkv, mom_qkv, sq_qkv = adamw_update(
        w_qkv, m_qkv, v_qkv, owned_qkv.T, RATE_MATRIX, WEIGHT_DECAY
    )
    new_out, mom_out, sq_out = adamw_update(
        w_out, m_out, v_out, owned_out.T, RATE_MATRIX, WEIGHT_DECAY
    )
    new_in, mom_in, sq_in = adamw_update(
        w_in, m_in, v_in, owned_in.transpose(0, 2, 1), RATE_MATRIX, WEIGHT_DECAY
    )
    new_down, mom_down, sq_down = adamw_update(
        w_down, m_down, v_down, owned_down.T, RATE_MATRIX, WEIGHT_DECAY
    )
    new_gains, mom_gains, sq_gains = adamw_update(
        gains, m_gains, v_gains, gain_grads, RATE_GAIN, 0.0
    )
    return (
        layer_out[None],
        tokens_grad[None],
        new_qkv,
        mom_qkv,
        sq_qkv,
        new_out,
        mom_out,
        sq_out,
        new_in,
        mom_in,
        sq_in,
        new_down,
        mom_down,
        sq_down,
        new_gains,
        mom_gains,
        sq_gains,
    )


def solution(mesh):
    return jax.shard_map(
        partial(local, mesh.shape["dp"], mesh.shape["grp"]),
        mesh=mesh,
        in_specs=(
            P("dp", "grp", None),
            P("dp", "grp", None),
            P("dp", None),
            P("dp", "grp"),
            P("grp", "dp"),
            P("grp", "dp"),
            P("grp", "dp"),
            P("grp", "dp"),
            P("grp", "dp"),
            P("grp", "dp"),
            P(None, "grp", "dp"),
            P(None, "grp", "dp"),
            P(None, "grp", "dp"),
            P("grp", "dp"),
            P("grp", "dp"),
            P("grp", "dp"),
            P(),
            P(),
            P(),
        ),
        out_specs=(
            P("dp", "grp", None),
            P("dp", "grp", None),
            P("grp", "dp"),
            P("grp", "dp"),
            P("grp", "dp"),
            P("grp", "dp"),
            P("grp", "dp"),
            P("grp", "dp"),
            P(None, "grp", "dp"),
            P(None, "grp", "dp"),
            P(None, "grp", "dp"),
            P("grp", "dp"),
            P("grp", "dp"),
            P("grp", "dp"),
            P(),
            P(),
            P(),
        ),
        check_vma=False,
    )
```

```python
import math
from functools import partial

import jax
import jax.numpy as jnp
from jax import lax
from jax.experimental import pallas as pl
from jax.experimental.pallas import tpu as pltpu
from jax.sharding import PartitionSpec as P

QUERY_HEADS = 15
KEY_VALUE_HEADS = 5
HEAD_SIZE = 64
STEP = 10


NORM_EPS = 1e-05
ROPE_BASE = 10000.0
MASKED = -1e30
BETA_FIRST = 0.9
BETA_SECOND = 0.95
ADAM_EPS = 1e-08
WEIGHT_DECAY = 0.1
RATE_MATRIX = 0.05
RATE_GAIN = 0.3


def rotation(places_in_doc):
    frequency = ROPE_BASE ** (-(jnp.arange(HEAD_SIZE // 2).astype(jnp.float32) * 2.0 / HEAD_SIZE))
    angles = frequency[:, None] * places_in_doc.astype(jnp.float32)[None, :]
    return (jnp.cos(angles), jnp.sin(angles))


def halves_of(head_rows):
    halves = head_rows.reshape(-1, 2, HEAD_SIZE // 2, head_rows.shape[-1])
    return halves[:, 0], halves[:, 1]


def apply_rotary(head_rows, rotary_cosine, rotary_sine):
    front_half, back_half = halves_of(head_rows)
    return jnp.stack(
        [
            front_half * rotary_cosine - back_half * rotary_sine,
            back_half * rotary_cosine + front_half * rotary_sine,
        ],
        axis=1,
    ).reshape(-1, head_rows.shape[-1])


def inverse_rotary(grad_rows, rotary_cosine, rotary_sine):
    return apply_rotary(grad_rows, rotary_cosine, -rotary_sine)


def norm_back(grad_output, plain_rows, factor, gain_row):
    scaled = grad_output * gain_row[:, None]
    grad_input = factor * (
        scaled - plain_rows * jnp.mean(scaled * plain_rows, axis=0, keepdims=True)
    )
    gain_gradient = jnp.sum(grad_output * plain_rows, axis=1)
    return (grad_input, gain_gradient)


def adamw_update(weight, moment_one, moment_two, gradient, step_rate, decay_rate):
    first_new = BETA_FIRST * moment_one + (1.0 - BETA_FIRST) * gradient
    second_new = BETA_SECOND * moment_two + (1.0 - BETA_SECOND) * gradient * gradient
    first_hat = first_new / (1.0 - BETA_FIRST**STEP)
    second_hat = second_new / (1.0 - BETA_SECOND**STEP)
    weight_new = weight - step_rate * (
        first_hat / (jnp.sqrt(second_hat) + ADAM_EPS) + decay_rate * weight
    )
    return (weight_new, first_new, second_new)


def bits_of(count):
    return count.bit_length() - 1


def tie(value, *others):
    return lax.optimization_barrier((value, others))[0]


TRANSPOSED = (((1,), (1,)), ((), ()))
FLAT = (((1,), (0,)), ((), ()))


def product(left, right, dims=FLAT):
    return lax.dot_general(left, right, dims, preferred_element_type=jnp.float32)


def upright(pieces_ref):
    return jnp.concatenate([pieces_ref[m, 0].T for m in range(pieces_ref.shape[0])], axis=0)


def attend_kernel(query_ref, key_ref, value_ref, bias_ref, out_ref, total_ref):
    keys = upright(key_ref)
    length = key_ref.shape[3]
    for head in range(query_ref.shape[1]):
        scores = product(keys, query_ref[0, head]) * HEAD_SIZE ** (-0.5) + bias_ref[...]
        peak = jnp.max(scores, axis=0, keepdims=True)
        exponent = jnp.exp(scores - peak)
        total = jnp.sum(exponent, axis=0, keepdims=True)
        probability = (exponent * (1.0 / total)).astype(jnp.bfloat16)
        attended = 0.0
        for m in range(key_ref.shape[0]):
            attended += product(value_ref[m, 0], probability[m * length : (m + 1) * length])
        out_ref[0, head] = attended.astype(jnp.bfloat16)
        total_ref[0, head : head + 1] = peak + jnp.log(total)


def attend_back_kernel(
    query_ref, key_ref, value_ref, bias_ref, total_ref, grad_ref, query_grad, key_grad, value_grad
):
    keys = upright(key_ref)
    values = upright(value_ref)
    length = key_ref.shape[3]
    for head in range(query_ref.shape[1]):
        queries = query_ref[0, head]
        grads = grad_ref[0, head]
        scores = product(keys, queries) * HEAD_SIZE ** (-0.5) + bias_ref[...]
        probability = jnp.exp(scores - total_ref[0, head : head + 1])
        weighted = probability * product(values, grads)
        grad_scores = weighted - probability * jnp.sum(weighted, axis=0, keepdims=True)
        grad_scores = grad_scores.astype(jnp.bfloat16)
        probability = probability.astype(jnp.bfloat16)
        from_keys = 0.0
        for m in range(key_ref.shape[0]):
            part = slice(m * length, (m + 1) * length)
            from_keys += product(key_ref[m, 0], grad_scores[part])
            from_queries = product(queries, grad_scores[part], TRANSPOSED) * HEAD_SIZE ** (-0.5)
            from_grads = product(grads, probability[part], TRANSPOSED)
            if head == 0:
                key_grad[m, 0] = from_queries
                value_grad[m, 0] = from_grads
            else:
                key_grad[m, 0] += from_queries
                value_grad[m, 0] += from_grads
        query_grad[0, head] = from_keys * HEAD_SIZE ** (-0.5)


def group_block(array):
    zeros = (0,) * (array.ndim - 1)
    return pl.BlockSpec((1,) + array.shape[1:], lambda g: (g,) + zeros)


def piece_block(pieces, first):
    block = (pieces.shape[0], 1) + pieces.shape[2:]
    return pl.BlockSpec(block, lambda g: (0, first + g, 0, 0))


def attend(queries, keys_values, bias):
    groups, heads, _, length = queries.shape
    totals = jax.ShapeDtypeStruct((groups, heads, length), jnp.float32)
    return pl.pallas_call(
        attend_kernel,
        grid=(groups,),
        in_specs=[
            group_block(queries),
            piece_block(keys_values, 0),
            piece_block(keys_values, groups),
            pl.BlockSpec(bias.shape, lambda g: (0, 0)),
        ],
        out_specs=[group_block(queries), group_block(totals)],
        out_shape=[jax.ShapeDtypeStruct(queries.shape, queries.dtype), totals],
        compiler_params=pltpu.CompilerParams(vmem_limit_bytes=40 << 20),
        cost_estimate=pl.CostEstimate(flops=1 << 28, bytes_accessed=1 << 20, transcendentals=0),
    )(queries, keys_values, keys_values, bias)


def attend_back(queries, keys_values, bias, totals, grads):
    groups = queries.shape[0]
    from_queries = jax.ShapeDtypeStruct(queries.shape, jnp.float32)
    from_keys = jax.ShapeDtypeStruct(
        (keys_values.shape[0], groups) + keys_values.shape[2:], jnp.float32
    )
    return pl.pallas_call(
        attend_back_kernel,
        grid=(groups,),
        in_specs=[
            group_block(queries),
            piece_block(keys_values, 0),
            piece_block(keys_values, groups),
            pl.BlockSpec(bias.shape, lambda g: (0, 0)),
            group_block(totals),
            group_block(grads),
        ],
        out_specs=[group_block(from_queries), piece_block(from_keys, 0), piece_block(from_keys, 0)],
        out_shape=[from_queries, from_keys, from_keys],
        compiler_params=pltpu.CompilerParams(vmem_limit_bytes=40 << 20),
        cost_estimate=pl.CostEstimate(flops=1 << 28, bytes_accessed=1 << 20, transcendentals=0),
    )(queries, keys_values, keys_values, bias, totals, grads)


class Slice:

    def __init__(self, dp_size, grp_size):
        self.dp_size = dp_size
        self.grp_size = grp_size
        dp_bits = bits_of(dp_size)
        grp_bits = bits_of(grp_size)
        x_count = min(max(grp_bits - 1, 0), dp_bits)
        z_bits = [("dp", bit) for bit in range(dp_bits - 1, x_count - 1, -1)]
        self.far = z_bits[:1]
        self.near = z_bits[1:]
        self.x = [("dp", bit) for bit in range(x_count - 1, -1, -1)]
        self.y = [("grp", bit) for bit in range(1, grp_bits)]
        self.core = [("grp", 0)]
        self.clock = None

    def size(self, axis):
        return self.dp_size if axis == "dp" else self.grp_size

    def own(self, axis, bit):
        return (lax.axis_index(axis) >> bit) & 1

    def swap(self, array, step):
        axis, bit = step
        size = self.size(axis)
        return lax.ppermute(array, axis, [(k, k ^ (1 << bit)) for k in range(size)])

    def in_turn(self, value):
        if self.clock is None:
            return value
        return tie(value, self.clock)

    def to_masks(self, rows):
        blocks = rows.reshape(self.grp_size, -1, rows.shape[1])
        own = lax.axis_index("grp")
        return [
            lax.dynamic_index_in_dim(blocks, own ^ m, 0, keepdims=False)
            for m in range(self.grp_size)
        ]

    def from_masks(self, blocks):
        for bit in range(bits_of(self.grp_size)):
            own = self.own("grp", bit)
            blocks = [
                jnp.where(own == 0, block, blocks[k ^ (1 << bit)]) for k, block in enumerate(blocks)
            ]
        return jnp.concatenate(blocks, axis=0)

    def pair(self, array):
        return jnp.concatenate([array, self.swap(array, self.core[0])], axis=1)

    def pair_blocks(self, blocks):
        own = range(0, self.grp_size, 2)
        came = self.swap(jnp.stack([blocks[m ^ 1] for m in own]), self.core[0])
        return {m: jnp.concatenate([blocks[m], came[n]], axis=1) for n, m in enumerate(own)}


class Gather:

    def __init__(self, net, chunks, bits=()):
        self.net = net
        self.chunks = chunks
        self.bits = list(bits)
        self.sent = None

    def send(self, steps):
        for step in steps:
            self.land()
            self.sent = (step, [self.net.swap(array, step) for _, array in self.chunks])
        return self

    def land(self, join=True, in_turn=False):
        if self.sent is None:
            return self
        (axis, bit), came = self.sent
        self.sent = None
        if in_turn:
            came = self.net.in_turn(came)
        chunks = []
        if axis == "grp":
            for (masks, array), other in zip(self.chunks, came):
                other_masks = [m ^ (1 << bit) for m in masks]
                if join:
                    chunks.append((masks + other_masks, jnp.concatenate([array, other])))
                else:
                    chunks += [(masks, array), (other_masks, other)]
        else:
            own = self.net.own(axis, bit)
            self.bits = sorted(self.bits + [bit], reverse=True)
            place = 1 + self.bits.index(bit)
            for (masks, array), other in zip(self.chunks, came):
                low = jnp.where(own == 0, array, other)
                high = jnp.where(own == 0, other, array)
                chunks.append((masks, jnp.stack([low, high], axis=place)))
        self.chunks = chunks
        if in_turn:
            self.net.clock = came if axis == "grp" and not join else [a for _, a in chunks]
        return self

    def land_next(self, steps, join=True):
        return self.land(join, True).send(steps)

    def rows(self, low, high):
        chunks = [(masks, array[..., low:high, :]) for masks, array in self.chunks]
        return Gather(self.net, chunks, self.bits)

    def pieces(self):
        return {
            mask: array[n].reshape(-1, array.shape[-1])
            for masks, array in self.chunks
            for n, mask in enumerate(masks)
        }


class Sum:

    def __init__(self, net, pieces, low=0, high=None):
        self.net = net
        self.bits = list(range(bits_of(net.dp_size) - 1, -1, -1))
        self.pieces = {
            mask: piece.reshape((2,) * len(self.bits) + (-1, piece.shape[1]))[..., low:high, :]
            for mask, piece in pieces.items()
        }

    def split(self, step):
        axis, bit = step
        kept, sent = {}, {}
        if axis == "grp":
            for mask, piece in self.pieces.items():
                if mask & (1 << bit):
                    sent[mask ^ (1 << bit)] = piece
                else:
                    kept[mask] = piece
        else:
            own = self.net.own(axis, bit)
            place = self.bits.index(bit)
            self.bits = self.bits[:place] + self.bits[place + 1 :]
            for mask, piece in self.pieces.items():
                low = lax.index_in_dim(piece, 0, place, keepdims=False)
                high = lax.index_in_dim(piece, 1, place, keepdims=False)
                kept[mask] = jnp.where(own == 0, low, high)
                sent[mask] = jnp.where(own == 0, high, low)
        self.pieces = kept
        return sent

    def owned(self):
        return self.pieces[0]


class Bundle:

    def __init__(self, net, *sums):
        self.net = net
        self.sums = sums
        self.sent = None

    def send(self, steps):
        for step in steps[::-1]:
            self.land()
            places, packed = [], []
            for part in self.sums:
                for mask, piece in part.split(step).items():
                    places.append((part, mask, piece.shape))
                    packed.append(piece.astype(jnp.bfloat16).reshape(-1, piece.shape[-1]))
            self.outgoing = jnp.concatenate(packed)
            self.sent = (places, self.net.swap(self.outgoing, step))
        return self

    def land(self, in_turn=False):
        if self.sent is None:
            return self
        places, came = self.sent
        self.sent = None
        if in_turn:
            came = self.net.in_turn(came)
        at = 0
        for part, mask, shape in places:
            rows = came[at : at + math.prod(shape[:-1])]
            at += rows.shape[0]
            part.pieces[mask] = part.pieces[mask].astype(jnp.float32) + rows.reshape(
                shape
            ).astype(jnp.float32)
        if in_turn:
            self.net.clock = [part.pieces for part in self.sums]
        return self

    def land_next(self, steps):
        return self.land(True).send(steps)


def forward_product(blocks, pieces):
    total = None
    for mask, piece in pieces.items():
        term = product(piece, blocks[mask])
        total = term if total is None else total + term
    return total


def backward_product(grad_rows, pieces):
    return [product(pieces[mask], grad_rows, (((0,), (0,)), ((), ()))) for mask in sorted(pieces)]


def weight_gradient(grad_rows, blocks):
    return {mask: product(grad_rows, block, TRANSPOSED) for mask, block in blocks.items()}


def local(
    dp_size,
    grp_size,
    tokens,
    cotangent,
    segments,
    positions,
    w_qkv,
    m_qkv,
    v_qkv,
    w_out,
    m_out,
    v_out,
    w_in,
    m_in,
    v_in,
    w_down,
    m_down,
    v_down,
    gains,
    m_gains,
    v_gains,
):
    net = Slice(dp_size, grp_size)
    low = jnp.bfloat16
    qkv_width = w_qkv.shape[1]
    qkv_out = jnp.concatenate([w_qkv.astype(low).T, w_out.astype(low).T])
    qkv_out = Gather(net, [([0], qkv_out[None])]).send(net.far)
    gate = Gather(net, [([0], w_in[0].astype(low).T[None])]).send(net.y)
    up = Gather(net, [([0], w_in[1].astype(low).T[None])]).send(net.x)
    down_low = w_down.astype(low).T[None]
    upstream_low = cotangent[0].T
    upstream_pair = net.pair(upstream_low)
    qkv_out.land_next(net.near)
    down = Gather(net, [([0], net.in_turn(down_low))]).send(net.far)
    upstream_pair = net.in_turn(upstream_pair)
    net.clock = upstream_pair
    qkv_out.land(True, True)
    qkv = qkv_out.rows(0, qkv_width).send(net.x)
    out = qkv_out.rows(qkv_width, None).send(net.y)
    gate.land_next(net.far)
    down.land_next(net.near)
    out.land_next(net.x)
    down.land_next(net.y)
    qkv.land_next(net.y)
    up.land_next(net.far)
    gate.land_next(net.near)
    out.land_next(net.core)
    up.land_next(net.near)
    gate.land_next(net.x)
    qkv.land_next(net.core)
    qkv.land(False)
    down.land_next(net.x)

    inputs = tokens[0].T.astype(jnp.float32)
    token_length = inputs.shape[1]
    query_width = QUERY_HEADS * HEAD_SIZE
    key_end = query_width + KEY_VALUE_HEADS * HEAD_SIZE
    head_shape = (KEY_VALUE_HEADS, -1, HEAD_SIZE, token_length)
    own_piece = lax.axis_index("grp")
    query_places = own_piece * token_length + jnp.arange(token_length)
    segment_pieces = segments[0].reshape(grp_size, token_length)
    own_segments = lax.dynamic_index_in_dim(segment_pieces, own_piece, 0, keepdims=False)
    key_masks = [0]
    for axis, bit in net.y + net.core:
        key_masks = key_masks + [m ^ (1 << bit) for m in key_masks]
    key_segments = jnp.concatenate(
        [
            lax.dynamic_index_in_dim(segment_pieces, own_piece ^ m, 0, keepdims=False)
            for m in key_masks
        ]
    )
    key_places = jnp.concatenate(
        [(own_piece ^ m) * token_length + jnp.arange(token_length) for m in key_masks]
    )
    allowed = (key_places[:, None] <= query_places[None, :]) & (
        key_segments[:, None] == own_segments[None, :]
    )
    bias = jnp.where(allowed, 0.0, MASKED)
    rotary_cosine, rotary_sine = rotation(positions[0])
    factor_one = lax.rsqrt(jnp.mean(inputs * inputs, axis=0, keepdims=True) + NORM_EPS)
    plain_one = inputs * factor_one
    normed = (plain_one * gains[0][:, None]).astype(low)
    normed_blocks = net.to_masks(normed)
    normed_pair = net.pair_blocks(normed_blocks)
    blended = forward_product(normed_blocks, qkv.pieces())
    rotated = apply_rotary(blended[:key_end], rotary_cosine, rotary_sine).astype(low)
    keys_values = jnp.concatenate([rotated[query_width:], blended[key_end:].astype(low)])[None]
    up.land(True, True)
    up.chunks = [(masks, tie(array, keys_values)) for masks, array in up.chunks]
    up.send(net.y)
    for step in net.y + net.core:
        keys_values = jnp.concatenate([keys_values, net.swap(keys_values, step)], axis=0)

    keys_values = keys_values.reshape(grp_size, -1, HEAD_SIZE, token_length)
    queries = rotated[:query_width].reshape(head_shape)
    attended, log_totals = attend(queries, keys_values, bias)
    attended_low = attended.reshape(query_width, token_length)
    attended_blocks = net.to_masks(attended_low)
    net.clock = attended_low
    gate.land_next(net.core)
    up.land_next(net.core, False)
    down.land_next(net.core)
    gate, up, down, out = [part.land(False).pieces() for part in (gate, up, down, out)]
    middle = inputs + forward_product(attended_blocks, out)
    factor_two = lax.rsqrt(jnp.mean(middle * middle, axis=0, keepdims=True) + NORM_EPS)
    plain_two = middle * factor_two
    normed_two = (plain_two * gains[1][:, None]).astype(low)
    normed_two_blocks = net.to_masks(normed_two)
    gate_pre = forward_product(normed_two_blocks, gate)
    up_proj = forward_product(normed_two_blocks, up)
    sigmoid_gate = jax.nn.sigmoid(gate_pre)
    activated = gate_pre * sigmoid_gate
    hidden = (activated * up_proj).astype(low)
    hidden_blocks = net.to_masks(hidden)
    layer_out = middle + forward_product(hidden_blocks, down)

    upstream = upstream_low.astype(jnp.float32)
    grad_down = weight_gradient(upstream_pair, net.pair_blocks(hidden_blocks))
    down_cut = w_down.shape[1] // 16 * 8
    sum_down = (Sum(net, grad_down, 0, down_cut), Sum(net, grad_down, down_cut))
    first_down = Bundle(net, sum_down[0]).send(net.x)
    second_down = Bundle(net, sum_down[1]).send(net.y)
    grad_hidden = net.from_masks(backward_product(upstream_low, down))
    grad_gate = (
        grad_hidden * up_proj * sigmoid_gate * (1.0 + gate_pre * (1.0 - sigmoid_gate))
    ).astype(low)
    grad_up = (grad_hidden * activated).astype(low)
    normed_two_pair = net.pair_blocks(normed_two_blocks)
    sum_gate = Sum(net, weight_gradient(net.pair(grad_gate), normed_two_pair))
    sum_up = Sum(net, weight_gradient(net.pair(grad_up), normed_two_pair))
    grad_in_gate = Bundle(net, sum_gate).send(net.x)
    grad_in_up = Bundle(net, sum_up).send(net.y)
    grad_normed_two = net.from_masks(
        [
            one + two
            for one, two in zip(
                backward_product(grad_gate, gate), backward_product(grad_up, up)
            )
        ]
    )
    back_two, gain_two = norm_back(grad_normed_two, plain_two, factor_two, gains[1])
    grad_middle = upstream + back_two
    middle_low = grad_middle.astype(low)
    attended_gradient = net.from_masks(backward_product(middle_low, out))
    outgoing = [part.outgoing for part in (first_down, second_down, grad_in_up, grad_in_gate)]
    attended_gradient = tie(attended_gradient.astype(low).reshape(head_shape), outgoing)
    grad_queries, grad_keys, grad_values = attend_back(
        queries, keys_values, bias, log_totals, attended_gradient
    )
    grad_keys_values = jnp.concatenate([grad_keys, grad_values], axis=1).reshape(
        grp_size, -1, token_length
    )
    net.clock = grad_keys_values
    for step in net.core + net.y[::-1]:
        half = grad_keys_values.shape[0] // 2
        came = net.swap(grad_keys_values[half:].astype(low), step)
        if step == net.y[-1]:
            first_down.land(True)
            second_down.land(True)
            both_down = Bundle(net, *sum_down).send(net.near)
            middle_pair = tie(net.pair(middle_low), net.clock)
            attended_pair = net.pair_blocks(attended_blocks)
            sum_out = Sum(net, weight_gradient(middle_pair, attended_pair))
            grad_out = Bundle(net, sum_out).send(net.x)
            grad_in_up.land_next(net.x)
            grad_in_gate.land_next(net.y)
        came = net.in_turn(came)
        grad_keys_values = grad_keys_values[:half] + came.astype(jnp.float32)
        net.clock = grad_keys_values
    grad_queries = grad_queries.reshape(query_width, token_length)
    grad_keys_values = grad_keys_values[0]
    key_width = key_end - query_width
    grad_mixed = jnp.concatenate(
        [
            inverse_rotary(grad_queries, rotary_cosine, rotary_sine),
            inverse_rotary(grad_keys_values[:key_width], rotary_cosine, rotary_sine),
            grad_keys_values[key_width:],
        ]
    ).astype(low)
    net.clock = grad_mixed
    both_down.land_next(net.far)
    grad_out.land(True)
    mixed_pair = net.in_turn(net.pair(grad_mixed))
    grad_qkv = weight_gradient(mixed_pair, normed_pair)
    cut = qkv_width // 16 * 8
    sum_qkv = (Sum(net, grad_qkv, 0, cut), Sum(net, grad_qkv, cut))
    first_qkv = Bundle(net, sum_qkv[0]).send(net.y)
    second_qkv = Bundle(net, sum_qkv[1]).send(net.x)
    net.clock = (first_qkv.outgoing, second_qkv.outgoing)
    grad_normed = net.from_masks(backward_product(tie(grad_mixed, net.clock), qkv.pieces()))
    back_one, gain_one = norm_back(grad_normed, plain_one, factor_one, gains[0])
    tokens_grad = grad_middle + back_one
    gain_grads = jnp.stack([gain_one, gain_two])

    def gain_steps(gain_grads, steps):
        for step in steps:
            gain_grads = gain_grads + net.in_turn(net.swap(gain_grads, step))
            net.clock = gain_grads
        return gain_grads

    grad_in_up.land(True)
    grad_in_gate.land(True)
    both_in = Bundle(net, sum_up, sum_gate).send(net.near)
    grad_out.send(net.y)
    gain_grads = gain_steps(gain_grads, net.core)
    first_qkv.land_next(net.x)
    second_qkv.land_next(net.y)
    gain_grads = gain_steps(gain_grads, net.y)
    both_down.land(True)
    first_down.send(net.y)
    second_down.send(net.x)
    grad_out.land(True)
    gain_grads = gain_steps(gain_grads, net.x)
    both_in.land_next(net.far)
    first_qkv.land(True)
    second_qkv.land(True)
    rest = Bundle(net, sum_out, *sum_qkv).send(net.near)
    gain_grads = gain_steps(gain_grads, net.near)
    first_down.land(True)
    second_down.land(True)
    both_in.land(True)
    rest.land_next(net.far)
    gain_grads = gain_steps(gain_grads, net.far)
    rest.land(True)
    owned_down = jnp.concatenate([part.owned() for part in sum_down])
    owned_in = jnp.stack([sum_gate.owned(), sum_up.owned()])
    owned_out = sum_out.owned()
    owned_qkv = jnp.concatenate([part.owned() for part in sum_qkv])
    new_qkv, mom_qkv, sq_qkv = adamw_update(
        w_qkv, m_qkv, v_qkv, owned_qkv.T, RATE_MATRIX, WEIGHT_DECAY
    )
    new_out, mom_out, sq_out = adamw_update(
        w_out, m_out, v_out, owned_out.T, RATE_MATRIX, WEIGHT_DECAY
    )
    new_in, mom_in, sq_in = adamw_update(
        w_in, m_in, v_in, owned_in.transpose(0, 2, 1), RATE_MATRIX, WEIGHT_DECAY
    )
    new_down, mom_down, sq_down = adamw_update(
        w_down, m_down, v_down, owned_down.T, RATE_MATRIX, WEIGHT_DECAY
    )
    new_gains, mom_gains, sq_gains = adamw_update(
        gains, m_gains, v_gains, gain_grads, RATE_GAIN, 0.0
    )
    return (
        layer_out.T[None],
        tokens_grad.T[None],
        new_qkv,
        mom_qkv,
        sq_qkv,
        new_out,
        mom_out,
        sq_out,
        new_in,
        mom_in,
        sq_in,
        new_down,
        mom_down,
        sq_down,
        new_gains,
        mom_gains,
        sq_gains,
    )


def solution(mesh):
    return jax.shard_map(
        partial(local, mesh.shape["dp"], mesh.shape["grp"]),
        mesh=mesh,
        in_specs=(
            P("dp", "grp", None),
            P("dp", "grp", None),
            P("dp", None),
            P("dp", "grp"),
            P("grp", "dp"),
            P("grp", "dp"),
            P("grp", "dp"),
            P("grp", "dp"),
            P("grp", "dp"),
            P("grp", "dp"),
            P(None, "grp", "dp"),
            P(None, "grp", "dp"),
            P(None, "grp", "dp"),
            P("grp", "dp"),
            P("grp", "dp"),
            P("grp", "dp"),
            P(),
            P(),
            P(),
        ),
        out_specs=(
            P("dp", "grp", None),
            P("dp", "grp", None),
            P("grp", "dp"),
            P("grp", "dp"),
            P("grp", "dp"),
            P("grp", "dp"),
            P("grp", "dp"),
            P("grp", "dp"),
            P(None, "grp", "dp"),
            P(None, "grp", "dp"),
            P(None, "grp", "dp"),
            P("grp", "dp"),
            P("grp", "dp"),
            P("grp", "dp"),
            P(),
            P(),
            P(),
        ),
        check_vma=False,
    )
```

```python
import math
from functools import partial

import jax
import jax.numpy as jnp
from jax import lax
from jax.experimental import pallas as pl
from jax.experimental.layout import Layout, with_layout_constraint
from jax.experimental.pallas import tpu as pltpu
from jax.sharding import PartitionSpec as P

QUERY_HEADS = 15
KEY_VALUE_HEADS = 5
HEAD_SIZE = 64
STEP = 10


NORM_EPS = 1e-05
ROPE_BASE = 10000.0
MASKED = -1e30
BETA_FIRST = 0.9
BETA_SECOND = 0.95
ADAM_EPS = 1e-08
WEIGHT_DECAY = 0.1
RATE_MATRIX = 0.05
RATE_GAIN = 0.3


def rotation(places_in_doc):
    frequency = ROPE_BASE ** (-(jnp.arange(HEAD_SIZE // 2).astype(jnp.float32) * 2.0 / HEAD_SIZE))
    angles = frequency[:, None] * places_in_doc.astype(jnp.float32)[None, :]
    return (jnp.cos(angles), jnp.sin(angles))


def halves_of(head_rows):
    halves = head_rows.reshape(-1, 2, HEAD_SIZE // 2, head_rows.shape[-1])
    return halves[:, 0], halves[:, 1]


def apply_rotary(head_rows, rotary_cosine, rotary_sine):
    front_half, back_half = halves_of(head_rows)
    return jnp.stack(
        [
            front_half * rotary_cosine - back_half * rotary_sine,
            back_half * rotary_cosine + front_half * rotary_sine,
        ],
        axis=1,
    ).reshape(-1, head_rows.shape[-1])


def inverse_rotary(grad_rows, rotary_cosine, rotary_sine):
    return apply_rotary(grad_rows, rotary_cosine, -rotary_sine)


def norm_back(grad_output, plain_rows, factor, gain_row):
    scaled = grad_output * gain_row[:, None]
    grad_input = factor * (
        scaled - plain_rows * jnp.mean(scaled * plain_rows, axis=0, keepdims=True)
    )
    gain_gradient = jnp.sum(grad_output * plain_rows, axis=1)
    return (grad_input, gain_gradient)


def adamw_update(weight, moment_one, moment_two, gradient, step_rate, decay_rate):
    first_new = BETA_FIRST * moment_one + (1.0 - BETA_FIRST) * gradient
    second_new = BETA_SECOND * moment_two + (1.0 - BETA_SECOND) * gradient * gradient
    first_hat = first_new / (1.0 - BETA_FIRST**STEP)
    second_hat = second_new / (1.0 - BETA_SECOND**STEP)
    weight_new = weight - step_rate * (
        first_hat / (jnp.sqrt(second_hat) + ADAM_EPS) + decay_rate * weight
    )
    return (weight_new, first_new, second_new)


def bits_of(count):
    return count.bit_length() - 1


def tie(value, *others):
    return lax.optimization_barrier((value, others))[0]


TRANSPOSED = (((1,), (1,)), ((), ()))
FLAT = (((1,), (0,)), ((), ()))


def product(left, right, dims=FLAT):
    return lax.dot_general(left, right, dims, preferred_element_type=jnp.float32)


def upright(pieces_ref):
    return jnp.concatenate([pieces_ref[m, 0].T for m in range(pieces_ref.shape[0])], axis=0)


def attend_kernel(query_ref, key_ref, value_ref, bias_ref, out_ref, total_ref):
    keys = upright(key_ref)
    length = key_ref.shape[3]
    for head in range(query_ref.shape[1]):
        scores = product(keys, query_ref[0, head]) * HEAD_SIZE ** (-0.5) + bias_ref[...]
        peak = jnp.max(scores, axis=0, keepdims=True)
        exponent = jnp.exp(scores - peak)
        total = jnp.sum(exponent, axis=0, keepdims=True)
        probability = (exponent * (1.0 / total)).astype(jnp.bfloat16)
        attended = 0.0
        for m in range(key_ref.shape[0]):
            attended += product(value_ref[m, 0], probability[m * length : (m + 1) * length])
        out_ref[0, head] = attended.astype(jnp.bfloat16)
        total_ref[0, head : head + 1] = peak + jnp.log(total)


def attend_back_kernel(
    query_ref, key_ref, value_ref, bias_ref, total_ref, grad_ref, query_grad, key_grad, value_grad
):
    keys = upright(key_ref)
    values = upright(value_ref)
    length = key_ref.shape[3]
    for head in range(query_ref.shape[1]):
        queries = query_ref[0, head]
        grads = grad_ref[0, head]
        scores = product(keys, queries) * HEAD_SIZE ** (-0.5) + bias_ref[...]
        probability = jnp.exp(scores - total_ref[0, head : head + 1])
        weighted = probability * product(values, grads)
        grad_scores = weighted - probability * jnp.sum(weighted, axis=0, keepdims=True)
        grad_scores = grad_scores.astype(jnp.bfloat16)
        probability = probability.astype(jnp.bfloat16)
        from_keys = 0.0
        for m in range(key_ref.shape[0]):
            part = slice(m * length, (m + 1) * length)
            from_keys += product(key_ref[m, 0], grad_scores[part])
            from_queries = product(queries, grad_scores[part], TRANSPOSED) * HEAD_SIZE ** (-0.5)
            from_grads = product(grads, probability[part], TRANSPOSED)
            if head == 0:
                key_grad[m, 0] = from_queries
                value_grad[m, 0] = from_grads
            else:
                key_grad[m, 0] += from_queries
                value_grad[m, 0] += from_grads
        query_grad[0, head] = from_keys * HEAD_SIZE ** (-0.5)


def group_block(array):
    zeros = (0,) * (array.ndim - 1)
    return pl.BlockSpec((1,) + array.shape[1:], lambda g: (g,) + zeros)


def piece_block(pieces, first):
    block = (pieces.shape[0], 1) + pieces.shape[2:]
    return pl.BlockSpec(block, lambda g: (0, first + g, 0, 0))


def attend(queries, keys_values, bias):
    groups, heads, _, length = queries.shape
    totals = jax.ShapeDtypeStruct((groups, heads, length), jnp.float32)
    return pl.pallas_call(
        attend_kernel,
        grid=(groups,),
        in_specs=[
            group_block(queries),
            piece_block(keys_values, 0),
            piece_block(keys_values, groups),
            pl.BlockSpec(bias.shape, lambda g: (0, 0)),
        ],
        out_specs=[group_block(queries), group_block(totals)],
        out_shape=[jax.ShapeDtypeStruct(queries.shape, queries.dtype), totals],
        compiler_params=pltpu.CompilerParams(vmem_limit_bytes=40 << 20),
        cost_estimate=pl.CostEstimate(flops=1 << 28, bytes_accessed=1 << 20, transcendentals=0),
    )(queries, keys_values, keys_values, bias)


def attend_back(queries, keys_values, bias, totals, grads):
    groups = queries.shape[0]
    from_queries = jax.ShapeDtypeStruct(queries.shape, jnp.float32)
    from_keys = jax.ShapeDtypeStruct(
        (keys_values.shape[0], groups) + keys_values.shape[2:], jnp.float32
    )
    return pl.pallas_call(
        attend_back_kernel,
        grid=(groups,),
        in_specs=[
            group_block(queries),
            piece_block(keys_values, 0),
            piece_block(keys_values, groups),
            pl.BlockSpec(bias.shape, lambda g: (0, 0)),
            group_block(totals),
            group_block(grads),
        ],
        out_specs=[group_block(from_queries), piece_block(from_keys, 0), piece_block(from_keys, 0)],
        out_shape=[from_queries, from_keys, from_keys],
        compiler_params=pltpu.CompilerParams(vmem_limit_bytes=40 << 20),
        cost_estimate=pl.CostEstimate(flops=1 << 28, bytes_accessed=1 << 20, transcendentals=0),
    )(queries, keys_values, keys_values, bias, totals, grads)


def row_major(array):
    return with_layout_constraint(array, Layout(tuple(range(array.ndim))))


class Slice:

    def __init__(self, dp_size, grp_size):
        self.dp_size = dp_size
        self.grp_size = grp_size
        dp_bits = bits_of(dp_size)
        grp_bits = bits_of(grp_size)
        x_count = min(max(grp_bits - 1, 0), dp_bits)
        z_bits = [("dp", bit) for bit in range(dp_bits - 1, x_count - 1, -1)]
        self.far = z_bits[:1]
        self.near = z_bits[1:]
        self.x = [("dp", bit) for bit in range(x_count - 1, -1, -1)]
        self.y = [("grp", bit) for bit in range(1, grp_bits)]
        self.core = [("grp", 0)]
        self.clock = None

    def size(self, axis):
        return self.dp_size if axis == "dp" else self.grp_size

    def own(self, axis, bit):
        return (lax.axis_index(axis) >> bit) & 1

    def swap(self, array, step):
        axis, bit = step
        size = self.size(axis)
        pairs = [(k, k ^ (1 << bit)) for k in range(size)]
        return row_major(lax.ppermute(row_major(array), axis, pairs))

    def in_turn(self, value):
        if self.clock is None:
            return value
        return tie(value, self.clock)

    def to_masks(self, rows):
        blocks = rows.reshape(self.grp_size, -1, rows.shape[1])
        own = lax.axis_index("grp")
        return [
            lax.dynamic_index_in_dim(blocks, own ^ m, 0, keepdims=False)
            for m in range(self.grp_size)
        ]

    def from_masks(self, blocks):
        for bit in range(bits_of(self.grp_size)):
            own = self.own("grp", bit)
            blocks = [
                jnp.where(own == 0, block, blocks[k ^ (1 << bit)]) for k, block in enumerate(blocks)
            ]
        return jnp.concatenate(blocks, axis=0)

    def pair(self, array):
        return jnp.concatenate([array, self.swap(array, self.core[0])], axis=1)

    def pair_blocks(self, blocks):
        own = range(0, self.grp_size, 2)
        came = self.swap(jnp.stack([blocks[m ^ 1] for m in own]), self.core[0])
        return {m: jnp.concatenate([blocks[m], came[n]], axis=1) for n, m in enumerate(own)}


class Gather:

    def __init__(self, net, chunks, bits=()):
        self.net = net
        self.chunks = chunks
        self.bits = list(bits)
        self.sent = None

    def send(self, steps):
        for step in steps:
            self.land()
            self.sent = (step, [self.net.swap(array, step) for _, array in self.chunks])
        return self

    def land(self, join=True, in_turn=False):
        if self.sent is None:
            return self
        (axis, bit), came = self.sent
        self.sent = None
        if in_turn:
            came = self.net.in_turn(came)
        chunks = []
        if axis == "grp":
            for (masks, array), other in zip(self.chunks, came):
                other_masks = [m ^ (1 << bit) for m in masks]
                if join:
                    chunks.append((masks + other_masks, jnp.concatenate([array, other])))
                else:
                    chunks += [(masks, array), (other_masks, other)]
        else:
            own = self.net.own(axis, bit)
            self.bits = sorted(self.bits + [bit], reverse=True)
            place = 1 + self.bits.index(bit)
            for (masks, array), other in zip(self.chunks, came):
                low = jnp.where(own == 0, array, other)
                high = jnp.where(own == 0, other, array)
                chunks.append((masks, jnp.stack([low, high], axis=place)))
        self.chunks = chunks
        if in_turn:
            self.net.clock = came if axis == "grp" and not join else [a for _, a in chunks]
        return self

    def land_next(self, steps, join=True):
        return self.land(join, True).send(steps)

    def rows(self, low, high):
        chunks = [(masks, array[..., low:high, :]) for masks, array in self.chunks]
        return Gather(self.net, chunks, self.bits)

    def pieces(self):
        return {
            mask: array[n].reshape(-1, array.shape[-1])
            for masks, array in self.chunks
            for n, mask in enumerate(masks)
        }


class Sum:

    def __init__(self, net, pieces, low=0, high=None):
        self.net = net
        self.bits = list(range(bits_of(net.dp_size) - 1, -1, -1))
        self.pieces = {
            mask: piece.reshape((2,) * len(self.bits) + (-1, piece.shape[1]))[..., low:high, :]
            for mask, piece in pieces.items()
        }

    def split(self, step):
        axis, bit = step
        kept, sent = {}, {}
        if axis == "grp":
            for mask, piece in self.pieces.items():
                if mask & (1 << bit):
                    sent[mask ^ (1 << bit)] = piece
                else:
                    kept[mask] = piece
        else:
            own = self.net.own(axis, bit)
            place = self.bits.index(bit)
            self.bits = self.bits[:place] + self.bits[place + 1 :]
            for mask, piece in self.pieces.items():
                kept[mask] = lax.dynamic_index_in_dim(piece, own, place, keepdims=False)
                sent[mask] = lax.dynamic_index_in_dim(piece, 1 - own, place, keepdims=False)
        self.pieces = kept
        return sent

    def owned(self):
        return row_major(self.pieces[0])


class Bundle:

    def __init__(self, net, *sums):
        self.net = net
        self.sums = sums
        self.sent = None

    def send(self, steps):
        for step in steps[::-1]:
            self.land()
            places, packed = [], []
            for part in self.sums:
                for mask, piece in part.split(step).items():
                    places.append((part, mask, piece.shape))
                    packed.append(piece.astype(jnp.bfloat16).reshape(-1, piece.shape[-1]))
            self.outgoing = jnp.concatenate(packed)
            self.sent = (places, self.net.swap(self.outgoing, step))
        return self

    def land(self, in_turn=False):
        if self.sent is None:
            return self
        places, came = self.sent
        self.sent = None
        if in_turn:
            came = self.net.in_turn(came)
        at = 0
        for part, mask, shape in places:
            rows = came[at : at + math.prod(shape[:-1])]
            at += rows.shape[0]
            part.pieces[mask] = part.pieces[mask].astype(jnp.float32) + rows.reshape(
                shape
            ).astype(jnp.float32)
        if in_turn:
            self.net.clock = [part.pieces for part in self.sums]
        return self

    def land_next(self, steps):
        return self.land(True).send(steps)


def forward_product(blocks, pieces):
    total = None
    for mask, piece in pieces.items():
        term = product(piece, blocks[mask])
        total = term if total is None else total + term
    return total


def backward_product(grad_rows, pieces):
    return [product(pieces[mask], grad_rows, (((0,), (0,)), ((), ()))) for mask in sorted(pieces)]


def weight_gradient(grad_rows, blocks):
    return {
        mask: row_major(product(grad_rows, block, TRANSPOSED)) for mask, block in blocks.items()
    }


def local(
    dp_size,
    grp_size,
    tokens,
    cotangent,
    segments,
    positions,
    w_qkv,
    m_qkv,
    v_qkv,
    w_out,
    m_out,
    v_out,
    w_in,
    m_in,
    v_in,
    w_down,
    m_down,
    v_down,
    gains,
    m_gains,
    v_gains,
):
    net = Slice(dp_size, grp_size)
    low = jnp.bfloat16
    qkv_width = w_qkv.shape[1]
    qkv_out = jnp.concatenate([w_qkv.astype(low).T, w_out.astype(low).T])
    qkv_out = Gather(net, [([0], qkv_out[None])]).send(net.far)
    gate = Gather(net, [([0], w_in[0].astype(low).T[None])]).send(net.y)
    up = Gather(net, [([0], w_in[1].astype(low).T[None])]).send(net.x)
    down_low = w_down.astype(low).T[None]
    upstream_low = cotangent[0].T
    upstream_pair = net.pair(upstream_low)
    qkv_out.land_next(net.near)
    down = Gather(net, [([0], net.in_turn(down_low))]).send(net.far)
    gate.land(True, True)
    up.land(True, True)
    upstream_pair = net.in_turn(upstream_pair)
    net.clock = upstream_pair
    inputs = tokens[0].T.astype(jnp.float32)
    token_length = inputs.shape[1]
    query_width = QUERY_HEADS * HEAD_SIZE
    key_end = query_width + KEY_VALUE_HEADS * HEAD_SIZE
    head_shape = (KEY_VALUE_HEADS, -1, HEAD_SIZE, token_length)
    own_piece = lax.axis_index("grp")
    query_places = own_piece * token_length + jnp.arange(token_length)
    segment_pieces = segments[0].reshape(grp_size, token_length)
    own_segments = lax.dynamic_index_in_dim(segment_pieces, own_piece, 0, keepdims=False)
    key_masks = [0]
    for axis, bit in net.y + net.core:
        key_masks = key_masks + [m ^ (1 << bit) for m in key_masks]
    key_segments = jnp.concatenate(
        [
            lax.dynamic_index_in_dim(segment_pieces, own_piece ^ m, 0, keepdims=False)
            for m in key_masks
        ]
    )
    key_places = jnp.concatenate(
        [(own_piece ^ m) * token_length + jnp.arange(token_length) for m in key_masks]
    )
    allowed = (key_places[:, None] <= query_places[None, :]) & (
        key_segments[:, None] == own_segments[None, :]
    )
    bias = jnp.where(allowed, 0.0, MASKED)
    rotary_cosine, rotary_sine = rotation(positions[0])
    factor_one = lax.rsqrt(jnp.mean(inputs * inputs, axis=0, keepdims=True) + NORM_EPS)
    plain_one = inputs * factor_one
    normed = (plain_one * gains[0][:, None]).astype(low)
    normed_blocks = net.to_masks(normed)
    normed_pair = net.in_turn(net.pair_blocks(normed_blocks))
    net.clock = normed_pair
    qkv_out.land(True, True)
    qkv = qkv_out.rows(0, qkv_width).send(net.x)
    out = qkv_out.rows(qkv_width, None).send(net.y)
    gate.send(net.far)
    down.land_next(net.near)
    out.land_next(net.x)
    down.land_next(net.y)
    qkv.land_next(net.y)
    gate.land_next(net.near)
    out.land(True, True)
    up.chunks = [(masks, net.in_turn(array)) for masks, array in up.chunks]
    up.send(net.far)
    gate.land_next(net.x)
    qkv.land_next(net.core)
    up.land_next(net.near)
    down.land_next(net.x)
    qkv.land(False, True)
    blended = forward_product(normed_blocks, qkv.pieces())
    rotated = apply_rotary(blended[:key_end], rotary_cosine, rotary_sine).astype(low)
    keys_values = jnp.concatenate([rotated[query_width:], blended[key_end:].astype(low)])[None]
    up.land_next(net.y)
    out.send(net.core)
    for step in net.y + net.core:
        keys_values = jnp.concatenate([keys_values, net.swap(keys_values, step)], axis=0)

    keys_values = keys_values.reshape(grp_size, -1, HEAD_SIZE, token_length)
    queries = rotated[:query_width].reshape(head_shape)
    attended, log_totals = attend(queries, keys_values, bias)
    attended_low = attended.reshape(query_width, token_length)
    attended_blocks = net.to_masks(attended_low)
    net.clock = attended_low
    gate.land_next(net.core)
    up.land_next(net.core, False)
    down.land_next(net.core)
    gate, up, down, out = [part.land(False).pieces() for part in (gate, up, down, out)]
    middle = inputs + forward_product(attended_blocks, out)
    factor_two = lax.rsqrt(jnp.mean(middle * middle, axis=0, keepdims=True) + NORM_EPS)
    plain_two = middle * factor_two
    normed_two = (plain_two * gains[1][:, None]).astype(low)
    normed_two_blocks = net.to_masks(normed_two)
    gate_pre = forward_product(normed_two_blocks, gate)
    up_proj = forward_product(normed_two_blocks, up)
    sigmoid_gate = jax.nn.sigmoid(gate_pre)
    activated = gate_pre * sigmoid_gate
    hidden = (activated * up_proj).astype(low)
    hidden_blocks = net.to_masks(hidden)
    layer_out = middle + forward_product(hidden_blocks, down)

    upstream = upstream_low.astype(jnp.float32)
    grad_down = weight_gradient(upstream_pair, net.pair_blocks(hidden_blocks))
    sum_down = Sum(net, grad_down)
    grad_down = Bundle(net, sum_down).send(net.x)
    grad_hidden = net.from_masks(backward_product(upstream_low, down))
    grad_gate = (
        grad_hidden * up_proj * sigmoid_gate * (1.0 + gate_pre * (1.0 - sigmoid_gate))
    ).astype(low)
    grad_up = (grad_hidden * activated).astype(low)
    normed_two_pair = net.pair_blocks(normed_two_blocks)
    sum_gate = Sum(net, weight_gradient(net.pair(grad_gate), normed_two_pair))
    sum_up = Sum(net, weight_gradient(net.pair(grad_up), normed_two_pair))
    grad_in_gate = Bundle(net, sum_gate).send(net.x)
    grad_in_up = Bundle(net, sum_up).send(net.y)
    grad_normed_two = net.from_masks(
        [
            one + two
            for one, two in zip(
                backward_product(grad_gate, gate), backward_product(grad_up, up)
            )
        ]
    )
    back_two, gain_two = norm_back(grad_normed_two, plain_two, factor_two, gains[1])
    grad_middle = upstream + back_two
    middle_low = grad_middle.astype(low)
    attended_gradient = net.from_masks(backward_product(middle_low, out))
    outgoing = [part.outgoing for part in (grad_down, grad_in_up, grad_in_gate)]
    attended_gradient = tie(attended_gradient.astype(low).reshape(head_shape), outgoing)
    grad_queries, grad_keys, grad_values = attend_back(
        queries, keys_values, bias, log_totals, attended_gradient
    )
    grad_keys_values = jnp.concatenate([grad_keys, grad_values], axis=1).reshape(
        grp_size, -1, token_length
    )
    net.clock = grad_keys_values
    for step in net.core + net.y[::-1]:
        half = grad_keys_values.shape[0] // 2
        came = net.swap(grad_keys_values[half:].astype(low), step)
        if step == net.core[0]:
            grad_in_up.land_next(net.x)
        elif step == net.y[-1]:
            middle_pair = tie(net.pair(middle_low), net.clock)
            attended_pair = net.pair_blocks(attended_blocks)
            sum_out = Sum(net, weight_gradient(middle_pair, attended_pair))
            grad_out = Bundle(net, sum_out).send(net.y)
            grad_down.land_next(net.near)
            grad_in_gate.land_next(net.y)
        came = net.in_turn(came)
        grad_keys_values = grad_keys_values[:half] + came.astype(jnp.float32)
        net.clock = grad_keys_values
    grad_queries = grad_queries.reshape(query_width, token_length)
    grad_keys_values = grad_keys_values[0]
    key_width = key_end - query_width
    grad_mixed = jnp.concatenate(
        [
            inverse_rotary(grad_queries, rotary_cosine, rotary_sine),
            inverse_rotary(grad_keys_values[:key_width], rotary_cosine, rotary_sine),
            grad_keys_values[key_width:],
        ]
    ).astype(low)
    net.clock = grad_mixed
    grad_down.land_next(net.far)
    grad_out.land(True)
    mixed_pair = net.in_turn(net.pair(grad_mixed))
    grad_qkv = weight_gradient(mixed_pair, normed_pair)
    cut = qkv_width // 16 * 8
    sum_qkv = (Sum(net, grad_qkv, 0, cut), Sum(net, grad_qkv, cut))
    first_qkv = Bundle(net, sum_qkv[0]).send(net.y)
    second_qkv = Bundle(net, sum_qkv[1]).send(net.x)
    net.clock = (first_qkv.outgoing, second_qkv.outgoing)
    grad_in_up.land(True)
    grad_in_gate.land(True)
    both_in = Bundle(net, sum_up, sum_gate).send(net.near)
    grad_out.send(net.x)
    grad_normed = net.from_masks(backward_product(tie(grad_mixed, net.clock), qkv.pieces()))
    back_one, gain_one = norm_back(grad_normed, plain_one, factor_one, gains[0])
    tokens_grad = grad_middle + back_one
    gain_grads = jnp.stack([gain_one, gain_two])

    def gain_steps(gain_grads, steps):
        for step in steps:
            gain_grads = gain_grads + net.in_turn(net.swap(gain_grads, step))
            net.clock = gain_grads
        return gain_grads

    gain_grads = gain_steps(gain_grads, net.core)
    first_qkv.land_next(net.x)
    second_qkv.land_next(net.y)
    gain_grads = gain_steps(gain_grads, net.y)
    grad_down.land_next(net.y)
    grad_out.land(True)
    gain_grads = gain_steps(gain_grads, net.x)
    both_in.land_next(net.far)
    first_qkv.land(True)
    second_qkv.land(True)
    rest = Bundle(net, sum_out, *sum_qkv).send(net.near)
    gain_grads = gain_steps(gain_grads, net.near)
    grad_down.land(True)
    both_in.land(True)
    rest.land_next(net.far)
    gain_grads = gain_steps(gain_grads, net.far)
    rest.land(True)
    owned_down = sum_down.owned()
    owned_in = jnp.stack([sum_gate.owned(), sum_up.owned()])
    owned_out = sum_out.owned()
    owned_qkv = jnp.concatenate([part.owned() for part in sum_qkv])
    new_qkv, mom_qkv, sq_qkv = adamw_update(
        w_qkv, m_qkv, v_qkv, owned_qkv.T, RATE_MATRIX, WEIGHT_DECAY
    )
    new_out, mom_out, sq_out = adamw_update(
        w_out, m_out, v_out, owned_out.T, RATE_MATRIX, WEIGHT_DECAY
    )
    new_in, mom_in, sq_in = adamw_update(
        w_in, m_in, v_in, owned_in.transpose(0, 2, 1), RATE_MATRIX, WEIGHT_DECAY
    )
    new_down, mom_down, sq_down = adamw_update(
        w_down, m_down, v_down, owned_down.T, RATE_MATRIX, WEIGHT_DECAY
    )
    new_gains, mom_gains, sq_gains = adamw_update(
        gains, m_gains, v_gains, gain_grads, RATE_GAIN, 0.0
    )
    return (
        layer_out.T[None],
        tokens_grad.T[None],
        new_qkv,
        mom_qkv,
        sq_qkv,
        new_out,
        mom_out,
        sq_out,
        new_in,
        mom_in,
        sq_in,
        new_down,
        mom_down,
        sq_down,
        new_gains,
        mom_gains,
        sq_gains,
    )


def solution(mesh):
    return jax.shard_map(
        partial(local, mesh.shape["dp"], mesh.shape["grp"]),
        mesh=mesh,
        in_specs=(
            P("dp", "grp", None),
            P("dp", "grp", None),
            P("dp", None),
            P("dp", "grp"),
            P("grp", "dp"),
            P("grp", "dp"),
            P("grp", "dp"),
            P("grp", "dp"),
            P("grp", "dp"),
            P("grp", "dp"),
            P(None, "grp", "dp"),
            P(None, "grp", "dp"),
            P(None, "grp", "dp"),
            P("grp", "dp"),
            P("grp", "dp"),
            P("grp", "dp"),
            P(),
            P(),
            P(),
        ),
        out_specs=(
            P("dp", "grp", None),
            P("dp", "grp", None),
            P("grp", "dp"),
            P("grp", "dp"),
            P("grp", "dp"),
            P("grp", "dp"),
            P("grp", "dp"),
            P("grp", "dp"),
            P(None, "grp", "dp"),
            P(None, "grp", "dp"),
            P(None, "grp", "dp"),
            P("grp", "dp"),
            P("grp", "dp"),
            P("grp", "dp"),
            P(),
            P(),
            P(),
        ),
        check_vma=False,
    )
```

```python
from functools import partial

import jax
import jax.numpy as jnp
from jax import lax
from jax.experimental import pallas as pl
from jax.experimental.pallas import tpu as pltpu
from jax.sharding import PartitionSpec as P

QUERY_HEADS = 15
KEY_VALUE_HEADS = 5
HEAD_SIZE = 64
STEP = 10


NORM_EPS = 1e-05
ROPE_BASE = 10000.0
MASKED = -1e30
BETA_FIRST = 0.9
BETA_SECOND = 0.95
ADAM_EPS = 1e-08
WEIGHT_DECAY = 0.1
RATE_MATRIX = 0.05
RATE_GAIN = 0.3


def rotation(places_in_doc):
    frequency = ROPE_BASE ** (-(jnp.arange(HEAD_SIZE // 2).astype(jnp.float32) * 2.0 / HEAD_SIZE))
    angles = frequency[:, None] * places_in_doc.astype(jnp.float32)[None, :]
    return (jnp.cos(angles), jnp.sin(angles))


def halves_of(head_rows):
    halves = head_rows.reshape(-1, 2, HEAD_SIZE // 2, head_rows.shape[-1])
    return halves[:, 0], halves[:, 1]


def apply_rotary(head_rows, rotary_cosine, rotary_sine):
    front_half, back_half = halves_of(head_rows)
    return jnp.stack(
        [
            front_half * rotary_cosine - back_half * rotary_sine,
            back_half * rotary_cosine + front_half * rotary_sine,
        ],
        axis=1,
    ).reshape(-1, head_rows.shape[-1])


def inverse_rotary(grad_rows, rotary_cosine, rotary_sine):
    return apply_rotary(grad_rows, rotary_cosine, -rotary_sine)


def norm_back(grad_output, plain_rows, factor, gain_row):
    scaled = grad_output * gain_row[:, None]
    grad_input = factor * (
        scaled - plain_rows * jnp.mean(scaled * plain_rows, axis=0, keepdims=True)
    )
    gain_gradient = jnp.sum(grad_output * plain_rows, axis=1)
    return (grad_input, gain_gradient)


def adamw_update(weight, moment_one, moment_two, gradient, step_rate, decay_rate):
    first_new = BETA_FIRST * moment_one + (1.0 - BETA_FIRST) * gradient
    second_new = BETA_SECOND * moment_two + (1.0 - BETA_SECOND) * gradient * gradient
    first_hat = first_new / (1.0 - BETA_FIRST**STEP)
    second_hat = second_new / (1.0 - BETA_SECOND**STEP)
    weight_new = weight - step_rate * (
        first_hat / (jnp.sqrt(second_hat) + ADAM_EPS) + decay_rate * weight
    )
    return (weight_new, first_new, second_new)


def bits_of(count):
    return count.bit_length() - 1


def tie(value, *others):
    return lax.optimization_barrier((value, others))[0]


TRANSPOSED = (((1,), (1,)), ((), ()))
FLAT = (((1,), (0,)), ((), ()))


def product(left, right, dims=FLAT):
    return lax.dot_general(left, right, dims, preferred_element_type=jnp.float32)


def upright(pieces_ref):
    return jnp.concatenate([pieces_ref[m, 0].T for m in range(pieces_ref.shape[0])], axis=0)


def attend_kernel(query_ref, key_ref, value_ref, bias_ref, out_ref, total_ref):
    keys = upright(key_ref)
    length = key_ref.shape[3]
    for head in range(query_ref.shape[1]):
        scores = product(keys, query_ref[0, head]) * HEAD_SIZE ** (-0.5) + bias_ref[...]
        peak = jnp.max(scores, axis=0, keepdims=True)
        exponent = jnp.exp(scores - peak)
        total = jnp.sum(exponent, axis=0, keepdims=True)
        probability = (exponent * (1.0 / total)).astype(jnp.bfloat16)
        attended = 0.0
        for m in range(key_ref.shape[0]):
            attended += product(value_ref[m, 0], probability[m * length : (m + 1) * length])
        out_ref[0, head] = attended.astype(jnp.bfloat16)
        total_ref[0, head : head + 1] = peak + jnp.log(total)


def attend_back_kernel(
    query_ref, key_ref, value_ref, bias_ref, total_ref, grad_ref, query_grad, key_grad, value_grad
):
    keys = upright(key_ref)
    values = upright(value_ref)
    length = key_ref.shape[3]
    for head in range(query_ref.shape[1]):
        queries = query_ref[0, head]
        grads = grad_ref[0, head]
        scores = product(keys, queries) * HEAD_SIZE ** (-0.5) + bias_ref[...]
        probability = jnp.exp(scores - total_ref[0, head : head + 1])
        weighted = probability * product(values, grads)
        grad_scores = weighted - probability * jnp.sum(weighted, axis=0, keepdims=True)
        grad_scores = grad_scores.astype(jnp.bfloat16)
        probability = probability.astype(jnp.bfloat16)
        from_keys = 0.0
        for m in range(key_ref.shape[0]):
            part = slice(m * length, (m + 1) * length)
            from_keys += product(key_ref[m, 0], grad_scores[part])
            from_queries = product(queries, grad_scores[part], TRANSPOSED) * HEAD_SIZE ** (-0.5)
            from_grads = product(grads, probability[part], TRANSPOSED)
            if head == 0:
                key_grad[m, 0] = from_queries
                value_grad[m, 0] = from_grads
            else:
                key_grad[m, 0] += from_queries
                value_grad[m, 0] += from_grads
        query_grad[0, head] = from_keys * HEAD_SIZE ** (-0.5)


def group_block(array):
    zeros = (0,) * (array.ndim - 1)
    return pl.BlockSpec((1,) + array.shape[1:], lambda g: (g,) + zeros)


def piece_block(pieces, first):
    block = (pieces.shape[0], 1) + pieces.shape[2:]
    return pl.BlockSpec(block, lambda g: (0, first + g, 0, 0))


def attend(queries, keys_values, bias):
    groups, heads, _, length = queries.shape
    totals = jax.ShapeDtypeStruct((groups, heads, length), jnp.float32)
    return pl.pallas_call(
        attend_kernel,
        grid=(groups,),
        in_specs=[
            group_block(queries),
            piece_block(keys_values, 0),
            piece_block(keys_values, groups),
            pl.BlockSpec(bias.shape, lambda g: (0, 0)),
        ],
        out_specs=[group_block(queries), group_block(totals)],
        out_shape=[jax.ShapeDtypeStruct(queries.shape, queries.dtype), totals],
        compiler_params=pltpu.CompilerParams(vmem_limit_bytes=40 << 20),
        cost_estimate=pl.CostEstimate(flops=1 << 28, bytes_accessed=1 << 20, transcendentals=0),
    )(queries, keys_values, keys_values, bias)


def attend_back(queries, keys_values, bias, totals, grads):
    groups = queries.shape[0]
    from_queries = jax.ShapeDtypeStruct(queries.shape, jnp.float32)
    from_keys = jax.ShapeDtypeStruct(
        (keys_values.shape[0], groups) + keys_values.shape[2:], jnp.float32
    )
    return pl.pallas_call(
        attend_back_kernel,
        grid=(groups,),
        in_specs=[
            group_block(queries),
            piece_block(keys_values, 0),
            piece_block(keys_values, groups),
            pl.BlockSpec(bias.shape, lambda g: (0, 0)),
            group_block(totals),
            group_block(grads),
        ],
        out_specs=[group_block(from_queries), piece_block(from_keys, 0), piece_block(from_keys, 0)],
        out_shape=[from_queries, from_keys, from_keys],
        compiler_params=pltpu.CompilerParams(vmem_limit_bytes=40 << 20),
        cost_estimate=pl.CostEstimate(flops=1 << 28, bytes_accessed=1 << 20, transcendentals=0),
    )(queries, keys_values, keys_values, bias, totals, grads)


class Slice:

    def __init__(self, dp_size, grp_size):
        self.dp_size = dp_size
        self.grp_size = grp_size
        dp_bits = bits_of(dp_size)
        grp_bits = bits_of(grp_size)
        x_count = min(max(grp_bits - 1, 0), dp_bits)
        z_bits = [("dp", bit) for bit in range(dp_bits - 1, x_count - 1, -1)]
        self.far = z_bits[:1]
        self.near = z_bits[1:]
        self.x = [("dp", bit) for bit in range(x_count - 1, -1, -1)]
        self.y = [("grp", bit) for bit in range(1, grp_bits)]
        self.core = [("grp", 0)]
        self.clock = None

    def size(self, axis):
        return self.dp_size if axis == "dp" else self.grp_size

    def own(self, axis, bit):
        return (lax.axis_index(axis) >> bit) & 1

    def swap(self, array, step):
        axis, bit = step
        size = self.size(axis)
        return lax.ppermute(array, axis, [(k, k ^ (1 << bit)) for k in range(size)])

    def in_turn(self, value):
        if self.clock is None:
            return value
        return tie(value, self.clock)

    def to_masks(self, rows):
        blocks = rows.reshape(self.grp_size, -1, rows.shape[1])
        own = lax.axis_index("grp")
        return [
            lax.dynamic_index_in_dim(blocks, own ^ m, 0, keepdims=False)
            for m in range(self.grp_size)
        ]

    def from_masks(self, blocks):
        for bit in range(bits_of(self.grp_size)):
            own = self.own("grp", bit)
            blocks = [
                jnp.where(own == 0, block, blocks[k ^ (1 << bit)]) for k, block in enumerate(blocks)
            ]
        return jnp.concatenate(blocks, axis=0)

    def pair(self, array):
        return jnp.concatenate([array, self.swap(array, self.core[0])], axis=1)

    def pair_blocks(self, blocks):
        own = range(0, self.grp_size, 2)
        came = self.swap(jnp.stack([blocks[m ^ 1] for m in own]), self.core[0])
        return {m: jnp.concatenate([blocks[m], came[n]], axis=1) for n, m in enumerate(own)}


class Gather:

    def __init__(self, net, chunks, bits=()):
        self.net = net
        self.chunks = chunks
        self.bits = list(bits)
        self.sent = None

    def send(self, steps):
        for step in steps:
            self.land()
            self.sent = (step, [self.net.swap(array, step) for _, array in self.chunks])
        return self

    def land(self, join=True, in_turn=False):
        if self.sent is None:
            return self
        (axis, bit), came = self.sent
        self.sent = None
        if in_turn:
            came = self.net.in_turn(came)
        chunks = []
        if axis == "grp":
            for (masks, array), other in zip(self.chunks, came):
                other_masks = [m ^ (1 << bit) for m in masks]
                if join:
                    chunks.append((masks + other_masks, jnp.concatenate([array, other])))
                else:
                    chunks += [(masks, array), (other_masks, other)]
        else:
            own = self.net.own(axis, bit)
            self.bits = sorted(self.bits + [bit], reverse=True)
            place = 1 + self.bits.index(bit)
            for (masks, array), other in zip(self.chunks, came):
                low = jnp.where(own == 0, array, other)
                high = jnp.where(own == 0, other, array)
                chunks.append((masks, jnp.stack([low, high], axis=place)))
        self.chunks = chunks
        if in_turn:
            self.net.clock = came if axis == "grp" and not join else [a for _, a in chunks]
        return self

    def land_next(self, steps, join=True):
        return self.land(join, True).send(steps)

    def rows(self, low, high):
        chunks = [(masks, array[..., low:high, :]) for masks, array in self.chunks]
        return Gather(self.net, chunks, self.bits)

    def pieces(self):
        return {
            mask: array[n].reshape(-1, array.shape[-1])
            for masks, array in self.chunks
            for n, mask in enumerate(masks)
        }


def gradient_kernel(own_ref, kept_rows, sent_rows, kept_blocks, sent_blocks, kept_ref, sent_ref):
    for rows, blocks, out in (
        (kept_rows, kept_blocks, kept_ref),
        (sent_rows, sent_blocks, sent_ref),
    ):
        for p in range(blocks.shape[0]):
            out[p, 0, 0] = product(rows[0, 0, 0], blocks[p], TRANSPOSED).astype(out.dtype)


def landing_kernel(own_ref, kept_in, sent_in, kept_came, sent_came, kept_ref, sent_ref):
    kept_ref[0, 0] = kept_in[0, 0, 0] + kept_came[0, 0, 0].astype(jnp.float32)
    sent = sent_in[0, 0, 0] + sent_came[0, 0, 0].astype(jnp.float32)
    sent_ref[0, 0] = sent.astype(sent_ref.dtype)


def whole(array):
    zeros = (0,) * array.ndim
    return pl.BlockSpec(array.shape, lambda a, m, own: zeros)


def half(array, other):
    block = (1, 1, 1) + array.shape[3:]
    if array.shape[1] == 1:
        return pl.BlockSpec(block, lambda a, m, own: (a, 0, m, 0, 0))
    if other:
        return pl.BlockSpec(block, lambda a, m, own: (a, 1 - own[0], m, 0, 0))
    return pl.BlockSpec(block, lambda a, m, own: (a, own[0], m, 0, 0))


def halves_call(kernel, grid, specs, out_blocks, out_shape, args):
    return pl.pallas_call(
        kernel,
        grid_spec=pltpu.PrefetchScalarGridSpec(
            num_scalar_prefetch=1, grid=grid, in_specs=specs, out_specs=out_blocks
        ),
        out_shape=[
            jax.ShapeDtypeStruct(out_shape[0], jnp.float32),
            jax.ShapeDtypeStruct(out_shape[1], jnp.bfloat16),
        ],
        compiler_params=pltpu.CompilerParams(vmem_limit_bytes=40 << 20),
        cost_estimate=pl.CostEstimate(flops=1 << 28, bytes_accessed=1 << 20, transcendentals=0),
    )(*args)


class Sum:

    def __init__(self, net, grad_rows, blocks, steps, low=0, high=None):
        self.net = net
        self.bits = list(range(bits_of(net.dp_size) - 1, -1, -1))
        self.masks = sorted(blocks)
        rows = grad_rows.reshape(net.dp_size, -1, grad_rows.shape[1])[:, low:high]
        axis, bit = steps[-1]
        own = jnp.zeros((1,), jnp.int32)
        kept = sent = jnp.stack([blocks[m] for m in self.masks])
        if axis == "grp":
            kept = jnp.stack([blocks[m] for m in self.masks if not m & (1 << bit)])
            sent = jnp.stack([blocks[m] for m in self.masks if m & (1 << bit)])
            self.masks = [m for m in self.masks if not m & (1 << bit)]
            rows = rows[:, None, None]
        else:
            own = net.own(axis, bit).astype(jnp.int32).reshape(1)
            self.bits.remove(bit)
            rows = rows.reshape((-1, 2, 1 << bit) + rows.shape[1:])
        grid = (rows.shape[0], rows.shape[2])
        pieces, width = kept.shape[:2]
        shape = (pieces,) + grid + (rows.shape[3], width)
        block = pl.BlockSpec(
            (pieces, 1, 1) + shape[3:], lambda a, m, own: (0, a, m, 0, 0)
        )
        self.held, self.outgoing = halves_call(
            gradient_kernel,
            grid,
            [half(rows, False), half(rows, True), whole(kept), whole(sent)],
            [block, block],
            (shape, shape),
            (own, rows, rows, kept, sent),
        )
        self.held = self.held.reshape((pieces, -1) + shape[3:])
        self.came = net.swap(self.outgoing, steps[-1])
        for step in steps[-2::-1]:
            self.step(step)

    def step(self, step):
        axis, bit = step
        pieces, blocks, rows, width = self.held.shape
        own = jnp.zeros((1,), jnp.int32)
        if axis == "grp":
            high = len({m >> (bit + 1) for m in self.masks})
            self.masks = [m for m in self.masks if not m & (1 << bit)]
            view = (high, 2, -1, rows, width)
        else:
            own = self.net.own(axis, bit).astype(jnp.int32).reshape(1)
            place = self.bits.index(bit)
            self.bits.remove(bit)
            view = (pieces << place, 2, -1, rows, width)
        held = self.held.reshape(view)
        came = self.came.reshape(view)
        grid = (held.shape[0], held.shape[2])
        shape = grid + (rows, width)
        block = pl.BlockSpec((1, 1, rows, width), lambda a, m, own: (a, m, 0, 0))
        self.held, self.outgoing = halves_call(
            landing_kernel,
            grid,
            [half(held, False), half(held, True), half(came, False), half(came, True)],
            [block, block],
            (shape, shape),
            (own, held, held, came, came),
        )
        self.held = self.held.reshape((len(self.masks), -1, rows, width))
        self.came = self.net.swap(self.outgoing, step)

    def land_next(self, steps):
        self.came = self.net.in_turn(self.came)
        for step in steps[::-1]:
            self.step(step)
        if steps:
            self.net.clock = (self.held, self.outgoing)
        return self

    def owned(self):
        came = self.came.reshape(self.held.shape)
        return (self.held + came.astype(jnp.float32))[0, 0]


def forward_product(blocks, pieces):
    total = None
    for mask, piece in pieces.items():
        term = product(piece, blocks[mask])
        total = term if total is None else total + term
    return total


def backward_product(grad_rows, pieces):
    return [product(pieces[mask], grad_rows, (((0,), (0,)), ((), ()))) for mask in sorted(pieces)]


def local(
    dp_size,
    grp_size,
    tokens,
    cotangent,
    segments,
    positions,
    w_qkv,
    m_qkv,
    v_qkv,
    w_out,
    m_out,
    v_out,
    w_in,
    m_in,
    v_in,
    w_down,
    m_down,
    v_down,
    gains,
    m_gains,
    v_gains,
):
    net = Slice(dp_size, grp_size)
    low = jnp.bfloat16
    qkv_width = w_qkv.shape[1]
    qkv_out = jnp.concatenate([w_qkv.astype(low).T, w_out.astype(low).T])
    qkv_out = Gather(net, [([0], qkv_out[None])]).send(net.far)
    gate = Gather(net, [([0], w_in[0].astype(low).T[None])]).send(net.y)
    up = Gather(net, [([0], w_in[1].astype(low).T[None])]).send(net.x)
    down_low = w_down.astype(low).T[None]
    upstream_low = cotangent[0].T
    upstream_pair = net.pair(upstream_low)
    qkv_out.land_next(net.near)
    down = Gather(net, [([0], net.in_turn(down_low))]).send(net.far)
    upstream_pair = net.in_turn(upstream_pair)
    net.clock = upstream_pair
    qkv_out.land(True, True)
    qkv = qkv_out.rows(0, qkv_width).send(net.x)
    out = qkv_out.rows(qkv_width, None).send(net.y)
    gate.land_next(net.far)
    down.land_next(net.near)
    out.land_next(net.x)
    down.land_next(net.y)
    qkv.land_next(net.y)
    up.land_next(net.far)
    gate.land_next(net.near)
    out.land_next(net.core)
    up.land_next(net.near)
    gate.land_next(net.x)
    qkv.land_next(net.core)
    qkv.land(False)
    down.land_next(net.x)

    inputs = tokens[0].T.astype(jnp.float32)
    token_length = inputs.shape[1]
    query_width = QUERY_HEADS * HEAD_SIZE
    key_end = query_width + KEY_VALUE_HEADS * HEAD_SIZE
    head_shape = (KEY_VALUE_HEADS, -1, HEAD_SIZE, token_length)
    own_piece = lax.axis_index("grp")
    query_places = own_piece * token_length + jnp.arange(token_length)
    segment_pieces = segments[0].reshape(grp_size, token_length)
    own_segments = lax.dynamic_index_in_dim(segment_pieces, own_piece, 0, keepdims=False)
    key_masks = [0]
    for axis, bit in net.y + net.core:
        key_masks = key_masks + [m ^ (1 << bit) for m in key_masks]
    key_segments = jnp.concatenate(
        [
            lax.dynamic_index_in_dim(segment_pieces, own_piece ^ m, 0, keepdims=False)
            for m in key_masks
        ]
    )
    key_places = jnp.concatenate(
        [(own_piece ^ m) * token_length + jnp.arange(token_length) for m in key_masks]
    )
    allowed = (key_places[:, None] <= query_places[None, :]) & (
        key_segments[:, None] == own_segments[None, :]
    )
    bias = jnp.where(allowed, 0.0, MASKED)
    rotary_cosine, rotary_sine = rotation(positions[0])
    factor_one = lax.rsqrt(jnp.mean(inputs * inputs, axis=0, keepdims=True) + NORM_EPS)
    plain_one = inputs * factor_one
    normed = (plain_one * gains[0][:, None]).astype(low)
    normed_blocks = net.to_masks(normed)
    normed_pair = net.pair_blocks(normed_blocks)
    blended = forward_product(normed_blocks, qkv.pieces())
    rotated = apply_rotary(blended[:key_end], rotary_cosine, rotary_sine).astype(low)
    keys_values = jnp.concatenate([rotated[query_width:], blended[key_end:].astype(low)])[None]
    up.land(True, True)
    up.send(net.y)
    for step in net.y + net.core:
        keys_values = jnp.concatenate([keys_values, net.swap(keys_values, step)], axis=0)

    keys_values = keys_values.reshape(grp_size, -1, HEAD_SIZE, token_length)
    queries = rotated[:query_width].reshape(head_shape)
    attended, log_totals = attend(queries, keys_values, bias)
    attended_low = attended.reshape(query_width, token_length)
    attended_blocks = net.to_masks(attended_low)
    net.clock = attended_low
    gate.land_next(net.core)
    up.land_next(net.core, False)
    down.land_next(net.core)
    gate, up, down, out = [part.land(False).pieces() for part in (gate, up, down, out)]
    middle = inputs + forward_product(attended_blocks, out)
    factor_two = lax.rsqrt(jnp.mean(middle * middle, axis=0, keepdims=True) + NORM_EPS)
    plain_two = middle * factor_two
    normed_two = (plain_two * gains[1][:, None]).astype(low)
    normed_two_blocks = net.to_masks(normed_two)
    gate_pre = forward_product(normed_two_blocks, gate)
    up_proj = forward_product(normed_two_blocks, up)
    sigmoid_gate = jax.nn.sigmoid(gate_pre)
    activated = gate_pre * sigmoid_gate
    hidden = (activated * up_proj).astype(low)
    hidden_blocks = net.to_masks(hidden)
    layer_out = middle + forward_product(hidden_blocks, down)

    upstream = upstream_low.astype(jnp.float32)
    grad_down = Sum(net, upstream_pair, net.pair_blocks(hidden_blocks), net.x)
    grad_hidden = net.from_masks(backward_product(upstream_low, down))
    grad_gate = (
        grad_hidden * up_proj * sigmoid_gate * (1.0 + gate_pre * (1.0 - sigmoid_gate))
    ).astype(low)
    grad_up = (grad_hidden * activated).astype(low)
    normed_two_pair = net.pair_blocks(normed_two_blocks)
    grad_in_gate = Sum(net, net.pair(grad_gate), normed_two_pair, net.x)
    grad_in_up = Sum(net, net.pair(grad_up), normed_two_pair, net.y)
    grad_normed_two = net.from_masks(
        [
            one + two
            for one, two in zip(
                backward_product(grad_gate, gate), backward_product(grad_up, up)
            )
        ]
    )
    back_two, gain_two = norm_back(grad_normed_two, plain_two, factor_two, gains[1])
    grad_middle = upstream + back_two
    middle_low = grad_middle.astype(low)
    attended_gradient = net.from_masks(backward_product(middle_low, out))
    outgoing = [part.outgoing for part in (grad_down, grad_in_up, grad_in_gate)]
    attended_gradient = tie(attended_gradient.astype(low).reshape(head_shape), outgoing)
    grad_queries, grad_keys, grad_values = attend_back(
        queries, keys_values, bias, log_totals, attended_gradient
    )
    grad_keys_values = jnp.concatenate([grad_keys, grad_values], axis=1).reshape(
        grp_size, -1, token_length
    )
    net.clock = grad_keys_values
    for step in net.core + net.y[::-1]:
        half = grad_keys_values.shape[0] // 2
        came = net.swap(grad_keys_values[half:].astype(low), step)
        if step == net.core[0]:
            grad_in_up.land_next(net.x)
        elif step == net.y[-1]:
            middle_pair = tie(net.pair(middle_low), net.clock)
            grad_out = Sum(net, middle_pair, net.pair_blocks(attended_blocks), net.y)
            grad_down.land_next(net.near)
            grad_in_gate.land_next(net.y)
        came = net.in_turn(came)
        grad_keys_values = grad_keys_values[:half] + came.astype(jnp.float32)
        net.clock = grad_keys_values
    grad_queries = grad_queries.reshape(query_width, token_length)
    grad_keys_values = grad_keys_values[0]
    key_width = key_end - query_width
    grad_mixed = jnp.concatenate(
        [
            inverse_rotary(grad_queries, rotary_cosine, rotary_sine),
            inverse_rotary(grad_keys_values[:key_width], rotary_cosine, rotary_sine),
            grad_keys_values[key_width:],
        ]
    ).astype(low)
    net.clock = grad_mixed
    grad_down.land_next(net.far)
    grad_out.land_next(net.x)
    mixed_pair = net.in_turn(net.pair(grad_mixed))
    cut = qkv_width // 16 * 8
    first_qkv = Sum(net, mixed_pair, normed_pair, net.y, 0, cut)
    second_qkv = Sum(net, mixed_pair, normed_pair, net.x, cut)
    net.clock = (first_qkv.outgoing, second_qkv.outgoing)
    grad_in_up.land_next(net.near)
    grad_in_gate.land_next(net.near)
    grad_normed = net.from_masks(backward_product(tie(grad_mixed, net.clock), qkv.pieces()))
    back_one, gain_one = norm_back(grad_normed, plain_one, factor_one, gains[0])
    tokens_grad = grad_middle + back_one
    gain_grads = jnp.stack([gain_one, gain_two])

    def gain_steps(gain_grads, steps):
        for step in steps:
            gain_grads = gain_grads + net.in_turn(net.swap(gain_grads, step))
            net.clock = gain_grads
        return gain_grads

    gain_grads = gain_steps(gain_grads, net.core)
    first_qkv.land_next(net.x)
    second_qkv.land_next(net.y)
    gain_grads = gain_steps(gain_grads, net.y)
    grad_down.land_next(net.y)
    grad_out.land_next(net.near)
    gain_grads = gain_steps(gain_grads, net.x)
    grad_in_up.land_next(net.far)
    grad_in_gate.land_next(net.far)
    first_qkv.land_next(net.near)
    second_qkv.land_next(net.near)
    gain_grads = gain_steps(gain_grads, net.near)
    grad_out.land_next(net.far)
    first_qkv.land_next(net.far)
    second_qkv.land_next(net.far)
    gain_grads = gain_steps(gain_grads, net.far)
    owned_down = grad_down.owned()
    owned_out = grad_out.owned()
    owned_qkv = jnp.concatenate([first_qkv.owned(), second_qkv.owned()])
    owned_in = jnp.stack([grad_in_gate.owned(), grad_in_up.owned()])
    new_qkv, mom_qkv, sq_qkv = adamw_update(
        w_qkv, m_qkv, v_qkv, owned_qkv.T, RATE_MATRIX, WEIGHT_DECAY
    )
    new_out, mom_out, sq_out = adamw_update(
        w_out, m_out, v_out, owned_out.T, RATE_MATRIX, WEIGHT_DECAY
    )
    new_in, mom_in, sq_in = adamw_update(
        w_in, m_in, v_in, owned_in.transpose(0, 2, 1), RATE_MATRIX, WEIGHT_DECAY
    )
    new_down, mom_down, sq_down = adamw_update(
        w_down, m_down, v_down, owned_down.T, RATE_MATRIX, WEIGHT_DECAY
    )
    new_gains, mom_gains, sq_gains = adamw_update(
        gains, m_gains, v_gains, gain_grads, RATE_GAIN, 0.0
    )
    return (
        layer_out.T[None],
        tokens_grad.T[None],
        new_qkv,
        mom_qkv,
        sq_qkv,
        new_out,
        mom_out,
        sq_out,
        new_in,
        mom_in,
        sq_in,
        new_down,
        mom_down,
        sq_down,
        new_gains,
        mom_gains,
        sq_gains,
    )


def solution(mesh):
    return jax.shard_map(
        partial(local, mesh.shape["dp"], mesh.shape["grp"]),
        mesh=mesh,
        in_specs=(
            P("dp", "grp", None),
            P("dp", "grp", None),
            P("dp", None),
            P("dp", "grp"),
            P("grp", "dp"),
            P("grp", "dp"),
            P("grp", "dp"),
            P("grp", "dp"),
            P("grp", "dp"),
            P("grp", "dp"),
            P(None, "grp", "dp"),
            P(None, "grp", "dp"),
            P(None, "grp", "dp"),
            P("grp", "dp"),
            P("grp", "dp"),
            P("grp", "dp"),
            P(),
            P(),
            P(),
        ),
        out_specs=(
            P("dp", "grp", None),
            P("dp", "grp", None),
            P("grp", "dp"),
            P("grp", "dp"),
            P("grp", "dp"),
            P("grp", "dp"),
            P("grp", "dp"),
            P("grp", "dp"),
            P(None, "grp", "dp"),
            P(None, "grp", "dp"),
            P(None, "grp", "dp"),
            P("grp", "dp"),
            P("grp", "dp"),
            P("grp", "dp"),
            P(),
            P(),
            P(),
        ),
        check_vma=False,
    )
```

```python
from functools import partial

import jax
import jax.numpy as jnp
from jax import lax
from jax.experimental import pallas as pl
from jax.experimental.pallas import tpu as pltpu
from jax.sharding import PartitionSpec as P

QUERY_HEADS = 15
KEY_VALUE_HEADS = 5
HEAD_SIZE = 64
STEP = 10


NORM_EPS = 1e-05
ROPE_BASE = 10000.0
MASKED = -1e30
BETA_FIRST = 0.9
BETA_SECOND = 0.95
ADAM_EPS = 1e-08
WEIGHT_DECAY = 0.1
RATE_MATRIX = 0.05
RATE_GAIN = 0.3


def rotation(places_in_doc):
    frequency = ROPE_BASE ** (-(jnp.arange(HEAD_SIZE // 2).astype(jnp.float32) * 2.0 / HEAD_SIZE))
    angles = frequency[:, None] * places_in_doc.astype(jnp.float32)[None, :]
    return (jnp.cos(angles), jnp.sin(angles))


def halves_of(head_rows):
    halves = head_rows.reshape(-1, 2, HEAD_SIZE // 2, head_rows.shape[-1])
    return halves[:, 0], halves[:, 1]


def apply_rotary(head_rows, rotary_cosine, rotary_sine):
    front_half, back_half = halves_of(head_rows)
    return jnp.stack(
        [
            front_half * rotary_cosine - back_half * rotary_sine,
            back_half * rotary_cosine + front_half * rotary_sine,
        ],
        axis=1,
    ).reshape(-1, head_rows.shape[-1])


def inverse_rotary(grad_rows, rotary_cosine, rotary_sine):
    return apply_rotary(grad_rows, rotary_cosine, -rotary_sine)


def norm_back(grad_output, plain_rows, factor, gain_row):
    scaled = grad_output * gain_row[:, None]
    grad_input = factor * (
        scaled - plain_rows * jnp.mean(scaled * plain_rows, axis=0, keepdims=True)
    )
    gain_gradient = jnp.sum(grad_output * plain_rows, axis=1)
    return (grad_input, gain_gradient)


def adamw_update(weight, moment_one, moment_two, gradient, step_rate, decay_rate):
    first_new = BETA_FIRST * moment_one + (1.0 - BETA_FIRST) * gradient
    second_new = BETA_SECOND * moment_two + (1.0 - BETA_SECOND) * gradient * gradient
    first_hat = first_new / (1.0 - BETA_FIRST**STEP)
    second_hat = second_new / (1.0 - BETA_SECOND**STEP)
    weight_new = weight - step_rate * (
        first_hat / (jnp.sqrt(second_hat) + ADAM_EPS) + decay_rate * weight
    )
    return (weight_new, first_new, second_new)


def bits_of(count):
    return count.bit_length() - 1


def tie(value, *others):
    return lax.optimization_barrier((value, others))[0]


TRANSPOSED = (((1,), (1,)), ((), ()))
FLAT = (((1,), (0,)), ((), ()))


def product(left, right, dims=FLAT):
    return lax.dot_general(left, right, dims, preferred_element_type=jnp.float32)


def upright(pieces_ref):
    return jnp.concatenate([pieces_ref[m, 0].T for m in range(pieces_ref.shape[0])], axis=0)


def attend_kernel(query_ref, key_ref, value_ref, bias_ref, out_ref, total_ref):
    keys = upright(key_ref)
    length = key_ref.shape[3]
    for head in range(query_ref.shape[1]):
        scores = product(keys, query_ref[0, head]) * HEAD_SIZE ** (-0.5) + bias_ref[...]
        peak = jnp.max(scores, axis=0, keepdims=True)
        exponent = jnp.exp(scores - peak)
        total = jnp.sum(exponent, axis=0, keepdims=True)
        probability = (exponent * (1.0 / total)).astype(jnp.bfloat16)
        attended = 0.0
        for m in range(key_ref.shape[0]):
            attended += product(value_ref[m, 0], probability[m * length : (m + 1) * length])
        out_ref[0, head] = attended.astype(jnp.bfloat16)
        total_ref[0, head : head + 1] = peak + jnp.log(total)


def attend_back_kernel(
    query_ref, key_ref, value_ref, bias_ref, total_ref, grad_ref, query_grad, key_grad, value_grad
):
    keys = upright(key_ref)
    values = upright(value_ref)
    length = key_ref.shape[3]
    for head in range(query_ref.shape[1]):
        queries = query_ref[0, head]
        grads = grad_ref[0, head]
        scores = product(keys, queries) * HEAD_SIZE ** (-0.5) + bias_ref[...]
        probability = jnp.exp(scores - total_ref[0, head : head + 1])
        weighted = probability * product(values, grads)
        grad_scores = weighted - probability * jnp.sum(weighted, axis=0, keepdims=True)
        grad_scores = grad_scores.astype(jnp.bfloat16)
        probability = probability.astype(jnp.bfloat16)
        from_keys = 0.0
        for m in range(key_ref.shape[0]):
            part = slice(m * length, (m + 1) * length)
            from_keys += product(key_ref[m, 0], grad_scores[part])
            from_queries = product(queries, grad_scores[part], TRANSPOSED) * HEAD_SIZE ** (-0.5)
            from_grads = product(grads, probability[part], TRANSPOSED)
            if head == 0:
                key_grad[m, 0] = from_queries
                value_grad[m, 0] = from_grads
            else:
                key_grad[m, 0] += from_queries
                value_grad[m, 0] += from_grads
        query_grad[0, head] = from_keys * HEAD_SIZE ** (-0.5)


def group_block(array):
    zeros = (0,) * (array.ndim - 1)
    return pl.BlockSpec((1,) + array.shape[1:], lambda g: (g,) + zeros)


def piece_block(pieces, first):
    block = (pieces.shape[0], 1) + pieces.shape[2:]
    return pl.BlockSpec(block, lambda g: (0, first + g, 0, 0))


def attend(queries, keys_values, bias):
    groups, heads, _, length = queries.shape
    totals = jax.ShapeDtypeStruct((groups, heads, length), jnp.float32)
    return pl.pallas_call(
        attend_kernel,
        grid=(groups,),
        in_specs=[
            group_block(queries),
            piece_block(keys_values, 0),
            piece_block(keys_values, groups),
            pl.BlockSpec(bias.shape, lambda g: (0, 0)),
        ],
        out_specs=[group_block(queries), group_block(totals)],
        out_shape=[jax.ShapeDtypeStruct(queries.shape, queries.dtype), totals],
        compiler_params=pltpu.CompilerParams(vmem_limit_bytes=40 << 20),
        cost_estimate=pl.CostEstimate(flops=1 << 28, bytes_accessed=1 << 20, transcendentals=0),
    )(queries, keys_values, keys_values, bias)


def attend_back(queries, keys_values, bias, totals, grads, clock):
    groups = queries.shape[0]
    from_queries = jax.ShapeDtypeStruct(queries.shape, jnp.float32)
    from_keys = jax.ShapeDtypeStruct(
        (keys_values.shape[0], groups) + keys_values.shape[2:], jnp.float32
    )
    def after_clock(*refs):
        attend_back_kernel(*refs[len(clock) :])

    return pl.pallas_call(
        after_clock,
        grid=(groups,),
        in_specs=[pl.BlockSpec(memory_space=pl.ANY)] * len(clock)
        + [
            group_block(queries),
            piece_block(keys_values, 0),
            piece_block(keys_values, groups),
            pl.BlockSpec(bias.shape, lambda g: (0, 0)),
            group_block(totals),
            group_block(grads),
        ],
        out_specs=[group_block(from_queries), piece_block(from_keys, 0), piece_block(from_keys, 0)],
        out_shape=[from_queries, from_keys, from_keys],
        compiler_params=pltpu.CompilerParams(vmem_limit_bytes=40 << 20),
        cost_estimate=pl.CostEstimate(flops=1 << 28, bytes_accessed=1 << 20, transcendentals=0),
    )(*clock, queries, keys_values, keys_values, bias, totals, grads)


class Slice:

    def __init__(self, dp_size, grp_size):
        self.dp_size = dp_size
        self.grp_size = grp_size
        dp_bits = bits_of(dp_size)
        grp_bits = bits_of(grp_size)
        x_count = min(max(grp_bits - 1, 0), dp_bits)
        z_bits = [("dp", bit) for bit in range(dp_bits - 1, x_count - 1, -1)]
        self.far = z_bits[:1]
        self.near = z_bits[1:]
        self.x = [("dp", bit) for bit in range(x_count - 1, -1, -1)]
        self.y = [("grp", bit) for bit in range(1, grp_bits)]
        self.core = [("grp", 0)]
        self.clock = None

    def size(self, axis):
        return self.dp_size if axis == "dp" else self.grp_size

    def own(self, axis, bit):
        return (lax.axis_index(axis) >> bit) & 1

    def swap(self, array, step):
        axis, bit = step
        size = self.size(axis)
        return lax.ppermute(array, axis, [(k, k ^ (1 << bit)) for k in range(size)])

    def in_turn(self, value):
        if self.clock is None:
            return value
        return tie(value, self.clock)

    def to_masks(self, rows):
        blocks = rows.reshape(self.grp_size, -1, rows.shape[1])
        own = lax.axis_index("grp")
        return [
            lax.dynamic_index_in_dim(blocks, own ^ m, 0, keepdims=False)
            for m in range(self.grp_size)
        ]

    def from_masks(self, blocks):
        for bit in range(bits_of(self.grp_size)):
            own = self.own("grp", bit)
            blocks = [
                jnp.where(own == 0, block, blocks[k ^ (1 << bit)]) for k, block in enumerate(blocks)
            ]
        return jnp.concatenate(blocks, axis=0)

    def pair(self, array):
        return jnp.concatenate([array, self.swap(array, self.core[0])], axis=1)

    def pair_blocks(self, blocks):
        own = range(0, self.grp_size, 2)
        came = self.swap(jnp.stack([blocks[m ^ 1] for m in own]), self.core[0])
        return {m: jnp.concatenate([blocks[m], came[n]], axis=1) for n, m in enumerate(own)}


class Gather:

    def __init__(self, net, chunks, bits=()):
        self.net = net
        self.chunks = chunks
        self.bits = list(bits)
        self.sent = None

    def send(self, steps):
        for step in steps:
            self.land()
            self.sent = (step, [self.net.swap(array, step) for _, array in self.chunks])
        return self

    def land(self, join=True, in_turn=False):
        if self.sent is None:
            return self
        (axis, bit), came = self.sent
        self.sent = None
        if in_turn:
            came = self.net.in_turn(came)
        chunks = []
        if axis == "grp":
            for (masks, array), other in zip(self.chunks, came):
                other_masks = [m ^ (1 << bit) for m in masks]
                if join:
                    chunks.append((masks + other_masks, jnp.concatenate([array, other])))
                else:
                    chunks += [(masks, array), (other_masks, other)]
        else:
            own = self.net.own(axis, bit)
            self.bits = sorted(self.bits + [bit], reverse=True)
            place = 1 + self.bits.index(bit)
            for (masks, array), other in zip(self.chunks, came):
                low = jnp.where(own == 0, array, other)
                high = jnp.where(own == 0, other, array)
                chunks.append((masks, jnp.stack([low, high], axis=place)))
        self.chunks = chunks
        if in_turn:
            self.net.clock = came if axis == "grp" and not join else [a for _, a in chunks]
        return self

    def land_next(self, steps, join=True):
        return self.land(join, True).send(steps)

    def rows(self, low, high):
        chunks = [(masks, array[..., low:high, :]) for masks, array in self.chunks]
        return Gather(self.net, chunks, self.bits)

    def pieces(self):
        return {
            mask: array[n].reshape(-1, array.shape[-1])
            for masks, array in self.chunks
            for n, mask in enumerate(masks)
        }


def gradient_kernel(own_ref, kept_rows, sent_rows, kept_blocks, sent_blocks, kept_ref, sent_ref):
    for rows, blocks, out in (
        (kept_rows, kept_blocks, kept_ref),
        (sent_rows, sent_blocks, sent_ref),
    ):
        for p in range(blocks.shape[0]):
            out[p, 0, 0] = product(rows[0, 0, 0], blocks[p], TRANSPOSED).astype(out.dtype)


def landing_kernel(own_ref, kept_in, sent_in, kept_came, sent_came, kept_ref, sent_ref):
    kept_ref[0, 0] = kept_in[0, 0, 0] + kept_came[0, 0, 0].astype(jnp.float32)
    sent = sent_in[0, 0, 0] + sent_came[0, 0, 0].astype(jnp.float32)
    sent_ref[0, 0] = sent.astype(sent_ref.dtype)


def whole(array):
    zeros = (0,) * array.ndim
    return pl.BlockSpec(array.shape, lambda a, m, own: zeros)


def half(array, other):
    block = (1, 1, 1) + array.shape[3:]
    if array.shape[1] == 1:
        return pl.BlockSpec(block, lambda a, m, own: (a, 0, m, 0, 0))
    if other:
        return pl.BlockSpec(block, lambda a, m, own: (a, 1 - own[0], m, 0, 0))
    return pl.BlockSpec(block, lambda a, m, own: (a, own[0], m, 0, 0))


def halves_call(kernel, grid, specs, out_blocks, out_shape, args, clock):
    def after_clock(own_ref, *refs):
        kernel(own_ref, *refs[len(clock) :])

    later = pl.BlockSpec(memory_space=pl.ANY)
    args = args[:1] + tuple(clock) + args[1:]
    return pl.pallas_call(
        after_clock,
        grid_spec=pltpu.PrefetchScalarGridSpec(
            num_scalar_prefetch=1,
            grid=grid,
            in_specs=[later] * len(clock) + specs,
            out_specs=out_blocks,
        ),
        out_shape=[
            jax.ShapeDtypeStruct(out_shape[0], jnp.float32),
            jax.ShapeDtypeStruct(out_shape[1], jnp.bfloat16),
        ],
        compiler_params=pltpu.CompilerParams(vmem_limit_bytes=40 << 20),
        cost_estimate=pl.CostEstimate(flops=1 << 28, bytes_accessed=1 << 20, transcendentals=0),
    )(*args)


def add_kernel(kept_ref, came_ref, *refs):
    refs[-1][...] = kept_ref[...] + came_ref[...].astype(jnp.float32)


def add_in_turn(kept, came, clock):
    here = pl.BlockSpec(memory_space=pltpu.VMEM)
    return pl.pallas_call(
        add_kernel,
        in_specs=[here, here] + [pl.BlockSpec(memory_space=pl.ANY)] * len(clock),
        out_specs=here,
        out_shape=jax.ShapeDtypeStruct(kept.shape, jnp.float32),
        compiler_params=pltpu.CompilerParams(vmem_limit_bytes=40 << 20),
        cost_estimate=pl.CostEstimate(flops=1 << 20, bytes_accessed=1 << 20, transcendentals=0),
    )(kept, came, *clock)


class Sum:

    def __init__(self, net, grad_rows, blocks, steps, low=0, high=None, clock=()):
        self.net = net
        self.bits = list(range(bits_of(net.dp_size) - 1, -1, -1))
        self.masks = sorted(blocks)
        rows = grad_rows.reshape(net.dp_size, -1, grad_rows.shape[1])[:, low:high]
        axis, bit = steps[-1]
        own = jnp.zeros((1,), jnp.int32)
        kept = sent = jnp.stack([blocks[m] for m in self.masks])
        if axis == "grp":
            kept = jnp.stack([blocks[m] for m in self.masks if not m & (1 << bit)])
            sent = jnp.stack([blocks[m] for m in self.masks if m & (1 << bit)])
            self.masks = [m for m in self.masks if not m & (1 << bit)]
            rows = rows[:, None, None]
        else:
            own = net.own(axis, bit).astype(jnp.int32).reshape(1)
            self.bits.remove(bit)
            rows = rows.reshape((-1, 2, 1 << bit) + rows.shape[1:])
        grid = (rows.shape[0], rows.shape[2])
        pieces, width = kept.shape[:2]
        shape = (pieces,) + grid + (rows.shape[3], width)
        block = pl.BlockSpec(
            (pieces, 1, 1) + shape[3:], lambda a, m, own: (0, a, m, 0, 0)
        )
        self.held, self.outgoing = halves_call(
            gradient_kernel,
            grid,
            [half(rows, False), half(rows, True), whole(kept), whole(sent)],
            [block, block],
            (shape, shape),
            (own, rows, rows, kept, sent),
            clock,
        )
        self.held = self.held.reshape((pieces, -1) + shape[3:])
        self.came = net.swap(self.outgoing, steps[-1])
        for step in steps[-2::-1]:
            self.step(step)

    def step(self, step, clock=()):
        axis, bit = step
        pieces, blocks, rows, width = self.held.shape
        own = jnp.zeros((1,), jnp.int32)
        if axis == "grp":
            high = len({m >> (bit + 1) for m in self.masks})
            self.masks = [m for m in self.masks if not m & (1 << bit)]
            view = (high, 2, -1, rows, width)
        else:
            own = self.net.own(axis, bit).astype(jnp.int32).reshape(1)
            place = self.bits.index(bit)
            self.bits.remove(bit)
            view = (pieces << place, 2, -1, rows, width)
        held = self.held.reshape(view)
        came = self.came.reshape(view)
        grid = (held.shape[0], held.shape[2])
        shape = grid + (rows, width)
        block = pl.BlockSpec((1, 1, rows, width), lambda a, m, own: (a, m, 0, 0))
        self.held, self.outgoing = halves_call(
            landing_kernel,
            grid,
            [half(held, False), half(held, True), half(came, False), half(came, True)],
            [block, block],
            (shape, shape),
            (own, held, held, came, came),
            clock,
        )
        self.held = self.held.reshape((len(self.masks), -1, rows, width))
        self.came = self.net.swap(self.outgoing, step)

    def land_next(self, steps):
        for step in steps[::-1]:
            self.step(step, self.net.clock)
        if steps:
            self.net.clock = [self.outgoing]
        return self

    def owned(self):
        came = self.came.reshape(self.held.shape)
        return (self.held + came.astype(jnp.float32))[0, 0]


def forward_product(blocks, pieces):
    total = None
    for mask, piece in pieces.items():
        term = product(piece, blocks[mask])
        total = term if total is None else total + term
    return total


def backward_product(grad_rows, pieces):
    return [product(pieces[mask], grad_rows, (((0,), (0,)), ((), ()))) for mask in sorted(pieces)]


def local(
    dp_size,
    grp_size,
    tokens,
    cotangent,
    segments,
    positions,
    w_qkv,
    m_qkv,
    v_qkv,
    w_out,
    m_out,
    v_out,
    w_in,
    m_in,
    v_in,
    w_down,
    m_down,
    v_down,
    gains,
    m_gains,
    v_gains,
):
    net = Slice(dp_size, grp_size)
    low = jnp.bfloat16
    qkv_width = w_qkv.shape[1]
    qkv_out = jnp.concatenate([w_qkv.astype(low).T, w_out.astype(low).T])
    qkv_out = Gather(net, [([0], qkv_out[None])]).send(net.far)
    gate = Gather(net, [([0], w_in[0].astype(low).T[None])]).send(net.y)
    up = Gather(net, [([0], w_in[1].astype(low).T[None])]).send(net.x)
    down_low = w_down.astype(low).T[None]
    upstream_low = cotangent[0].T
    upstream_pair = net.pair(upstream_low)
    qkv_out.land_next(net.near)
    down = Gather(net, [([0], net.in_turn(down_low))]).send(net.far)
    upstream_pair = net.in_turn(upstream_pair)
    net.clock = upstream_pair
    qkv_out.land(True, True)
    qkv = qkv_out.rows(0, qkv_width).send(net.x)
    out = qkv_out.rows(qkv_width, None).send(net.y)
    gate.land_next(net.far)
    down.land_next(net.near)
    out.land_next(net.x)
    down.land_next(net.y)
    qkv.land_next(net.y)
    up.land_next(net.far)
    gate.land_next(net.near)
    out.land_next(net.core)
    up.land_next(net.near)
    gate.land_next(net.x)
    qkv.land_next(net.core)
    qkv.land(False)
    down.land_next(net.x)

    inputs = tokens[0].T.astype(jnp.float32)
    token_length = inputs.shape[1]
    query_width = QUERY_HEADS * HEAD_SIZE
    key_end = query_width + KEY_VALUE_HEADS * HEAD_SIZE
    head_shape = (KEY_VALUE_HEADS, -1, HEAD_SIZE, token_length)
    own_piece = lax.axis_index("grp")
    query_places = own_piece * token_length + jnp.arange(token_length)
    segment_pieces = segments[0].reshape(grp_size, token_length)
    own_segments = lax.dynamic_index_in_dim(segment_pieces, own_piece, 0, keepdims=False)
    key_masks = [0]
    for axis, bit in net.y + net.core:
        key_masks = key_masks + [m ^ (1 << bit) for m in key_masks]
    key_segments = jnp.concatenate(
        [
            lax.dynamic_index_in_dim(segment_pieces, own_piece ^ m, 0, keepdims=False)
            for m in key_masks
        ]
    )
    key_places = jnp.concatenate(
        [(own_piece ^ m) * token_length + jnp.arange(token_length) for m in key_masks]
    )
    allowed = (key_places[:, None] <= query_places[None, :]) & (
        key_segments[:, None] == own_segments[None, :]
    )
    bias = jnp.where(allowed, 0.0, MASKED)
    rotary_cosine, rotary_sine = rotation(positions[0])
    factor_one = lax.rsqrt(jnp.mean(inputs * inputs, axis=0, keepdims=True) + NORM_EPS)
    plain_one = inputs * factor_one
    normed = (plain_one * gains[0][:, None]).astype(low)
    normed_blocks = net.to_masks(normed)
    normed_pair = net.pair_blocks(normed_blocks)
    blended = forward_product(normed_blocks, qkv.pieces())
    rotated = apply_rotary(blended[:key_end], rotary_cosine, rotary_sine).astype(low)
    keys_values = jnp.concatenate([rotated[query_width:], blended[key_end:].astype(low)])[None]
    up.land(True, True)
    up.send(net.y)
    for step in net.y + net.core:
        keys_values = jnp.concatenate([keys_values, net.swap(keys_values, step)], axis=0)

    keys_values = keys_values.reshape(grp_size, -1, HEAD_SIZE, token_length)
    queries = rotated[:query_width].reshape(head_shape)
    attended, log_totals = attend(queries, keys_values, bias)
    attended_low = attended.reshape(query_width, token_length)
    attended_blocks = net.to_masks(attended_low)
    net.clock = attended_blocks
    gate.land_next(net.core)
    up.land_next(net.core, False)
    down.land_next(net.core)
    gate, up, down, out = [part.land(False).pieces() for part in (gate, up, down, out)]
    middle = inputs + forward_product(attended_blocks, out)
    factor_two = lax.rsqrt(jnp.mean(middle * middle, axis=0, keepdims=True) + NORM_EPS)
    plain_two = middle * factor_two
    normed_two = (plain_two * gains[1][:, None]).astype(low)
    normed_two_blocks = net.to_masks(normed_two)
    gate_pre = forward_product(normed_two_blocks, gate)
    up_proj = forward_product(normed_two_blocks, up)
    sigmoid_gate = jax.nn.sigmoid(gate_pre)
    activated = gate_pre * sigmoid_gate
    hidden = (activated * up_proj).astype(low)
    hidden_blocks = net.to_masks(hidden)
    layer_out = middle + forward_product(hidden_blocks, down)

    upstream = upstream_low.astype(jnp.float32)
    grad_down = Sum(net, upstream_pair, net.pair_blocks(hidden_blocks), net.x)
    grad_hidden = net.from_masks(backward_product(upstream_low, down))
    grad_gate = (
        grad_hidden * up_proj * sigmoid_gate * (1.0 + gate_pre * (1.0 - sigmoid_gate))
    ).astype(low)
    grad_up = (grad_hidden * activated).astype(low)
    normed_two_pair = net.pair_blocks(normed_two_blocks)
    grad_in_gate = Sum(net, net.pair(grad_gate), normed_two_pair, net.x)
    grad_in_up = Sum(net, net.pair(grad_up), normed_two_pair, net.y)
    grad_normed_two = net.from_masks(
        [
            one + two
            for one, two in zip(
                backward_product(grad_gate, gate), backward_product(grad_up, up)
            )
        ]
    )
    back_two, gain_two = norm_back(grad_normed_two, plain_two, factor_two, gains[1])
    grad_middle = upstream + back_two
    middle_low = grad_middle.astype(low)
    attended_gradient = net.from_masks(backward_product(middle_low, out))
    outgoing = [part.outgoing for part in (grad_down, grad_in_up, grad_in_gate)]
    attended_gradient = attended_gradient.astype(low).reshape(head_shape)
    grad_queries, grad_keys, grad_values = attend_back(
        queries, keys_values, bias, log_totals, attended_gradient, outgoing
    )
    grad_keys_values = jnp.concatenate([grad_keys, grad_values], axis=1).reshape(
        grp_size, -1, token_length
    )
    net.clock = [grad_keys_values]
    for step in net.core + net.y[::-1]:
        half = grad_keys_values.shape[0] // 2
        came = net.swap(grad_keys_values[half:].astype(low), step)
        if step == net.core[0]:
            grad_down.land_next(net.near)
            grad_in_up.land_next(net.x)
        grad_keys_values = add_in_turn(grad_keys_values[:half], came, net.clock)
        net.clock = [grad_keys_values]
    grad_queries = grad_queries.reshape(query_width, token_length)
    grad_keys_values = grad_keys_values[0]
    key_width = key_end - query_width
    grad_mixed = jnp.concatenate(
        [
            inverse_rotary(grad_queries, rotary_cosine, rotary_sine),
            inverse_rotary(grad_keys_values[:key_width], rotary_cosine, rotary_sine),
            grad_keys_values[key_width:],
        ]
    ).astype(low)
    net.clock = [grad_mixed]
    mixed_pair = net.pair(grad_mixed)
    middle_pair = net.pair(middle_low)
    attended_pair = net.pair_blocks(attended_blocks)
    grad_out = Sum(net, middle_pair, attended_pair, net.y, clock=net.clock)
    net.clock = [grad_out.outgoing]
    grad_down.land_next(net.far)
    cut = qkv_width // 16 * 8
    first_qkv = Sum(net, mixed_pair, normed_pair, net.y, 0, cut, net.clock)
    second_qkv = Sum(net, mixed_pair, normed_pair, net.x, cut, None, net.clock)
    net.clock = [first_qkv.outgoing, second_qkv.outgoing]
    grad_in_gate.land_next(net.y)
    grad_normed = net.from_masks(backward_product(grad_mixed, qkv.pieces()))
    back_one, gain_one = norm_back(grad_normed, plain_one, factor_one, gains[0])
    tokens_grad = grad_middle + back_one
    gain_grads = jnp.stack([gain_one, gain_two])

    def gain_steps(gain_grads, steps):
        for step in steps:
            gain_grads = add_in_turn(gain_grads, net.swap(gain_grads, step), net.clock)
            net.clock = [gain_grads]
        return gain_grads

    grad_in_up.land_next(net.near)
    grad_out.land_next(net.x)
    gain_grads = gain_steps(gain_grads, net.core)
    second_qkv.land_next(net.y)
    first_qkv.land_next(net.x)
    grad_down.land_next(net.y)
    grad_in_gate.land_next(net.near)
    grad_in_up.land_next(net.far)
    gain_grads = gain_steps(gain_grads, net.y)
    second_qkv.land_next(net.near)
    first_qkv.land_next(net.near)
    grad_out.land_next(net.near)
    gain_grads = gain_steps(gain_grads, net.x)
    grad_in_gate.land_next(net.far)
    second_qkv.land_next(net.far)
    first_qkv.land_next(net.far)
    grad_out.land_next(net.far)
    gain_grads = gain_steps(gain_grads, net.near + net.far)
    owned_down = grad_down.owned()
    owned_out = grad_out.owned()
    owned_qkv = jnp.concatenate([first_qkv.owned(), second_qkv.owned()])
    owned_in = jnp.stack([grad_in_gate.owned(), grad_in_up.owned()])
    new_qkv, mom_qkv, sq_qkv = adamw_update(
        w_qkv, m_qkv, v_qkv, owned_qkv.T, RATE_MATRIX, WEIGHT_DECAY
    )
    new_out, mom_out, sq_out = adamw_update(
        w_out, m_out, v_out, owned_out.T, RATE_MATRIX, WEIGHT_DECAY
    )
    new_in, mom_in, sq_in = adamw_update(
        w_in, m_in, v_in, owned_in.transpose(0, 2, 1), RATE_MATRIX, WEIGHT_DECAY
    )
    new_down, mom_down, sq_down = adamw_update(
        w_down, m_down, v_down, owned_down.T, RATE_MATRIX, WEIGHT_DECAY
    )
    new_gains, mom_gains, sq_gains = adamw_update(
        gains, m_gains, v_gains, gain_grads, RATE_GAIN, 0.0
    )
    return (
        layer_out.T[None],
        tokens_grad.T[None],
        new_qkv,
        mom_qkv,
        sq_qkv,
        new_out,
        mom_out,
        sq_out,
        new_in,
        mom_in,
        sq_in,
        new_down,
        mom_down,
        sq_down,
        new_gains,
        mom_gains,
        sq_gains,
    )


def solution(mesh):
    return jax.shard_map(
        partial(local, mesh.shape["dp"], mesh.shape["grp"]),
        mesh=mesh,
        in_specs=(
            P("dp", "grp", None),
            P("dp", "grp", None),
            P("dp", None),
            P("dp", "grp"),
            P("grp", "dp"),
            P("grp", "dp"),
            P("grp", "dp"),
            P("grp", "dp"),
            P("grp", "dp"),
            P("grp", "dp"),
            P(None, "grp", "dp"),
            P(None, "grp", "dp"),
            P(None, "grp", "dp"),
            P("grp", "dp"),
            P("grp", "dp"),
            P("grp", "dp"),
            P(),
            P(),
            P(),
        ),
        out_specs=(
            P("dp", "grp", None),
            P("dp", "grp", None),
            P("grp", "dp"),
            P("grp", "dp"),
            P("grp", "dp"),
            P("grp", "dp"),
            P("grp", "dp"),
            P("grp", "dp"),
            P(None, "grp", "dp"),
            P(None, "grp", "dp"),
            P(None, "grp", "dp"),
            P("grp", "dp"),
            P("grp", "dp"),
            P("grp", "dp"),
            P(),
            P(),
            P(),
        ),
        check_vma=False,
    )
```

```python
from functools import partial

import jax
import jax.numpy as jnp
from jax import lax
from jax.experimental import pallas as pl
from jax.experimental.pallas import tpu as pltpu
from jax.sharding import PartitionSpec as P

QUERY_HEADS = 15
KEY_VALUE_HEADS = 5
HEAD_SIZE = 64
STEP = 10


NORM_EPS = 1e-05
ROPE_BASE = 10000.0
MASKED = -1e30
BETA_FIRST = 0.9
BETA_SECOND = 0.95
ADAM_EPS = 1e-08
WEIGHT_DECAY = 0.1
RATE_MATRIX = 0.05
RATE_GAIN = 0.3


def rotation(places_in_doc):
    frequency = ROPE_BASE ** (-(jnp.arange(HEAD_SIZE // 2).astype(jnp.float32) * 2.0 / HEAD_SIZE))
    angles = frequency[:, None] * places_in_doc.astype(jnp.float32)[None, :]
    return (jnp.cos(angles), jnp.sin(angles))


def halves_of(head_rows):
    halves = head_rows.reshape(-1, 2, HEAD_SIZE // 2, head_rows.shape[-1])
    return halves[:, 0], halves[:, 1]


def apply_rotary(head_rows, rotary_cosine, rotary_sine):
    front_half, back_half = halves_of(head_rows)
    return jnp.stack(
        [
            front_half * rotary_cosine - back_half * rotary_sine,
            back_half * rotary_cosine + front_half * rotary_sine,
        ],
        axis=1,
    ).reshape(-1, head_rows.shape[-1])


def inverse_rotary(grad_rows, rotary_cosine, rotary_sine):
    return apply_rotary(grad_rows, rotary_cosine, -rotary_sine)


def norm_back(grad_output, plain_rows, factor, gain_row):
    scaled = grad_output * gain_row[:, None]
    grad_input = factor * (
        scaled - plain_rows * jnp.mean(scaled * plain_rows, axis=0, keepdims=True)
    )
    gain_gradient = jnp.sum(grad_output * plain_rows, axis=1)
    return (grad_input, gain_gradient)


def adamw_update(weight, moment_one, moment_two, gradient, step_rate, decay_rate):
    first_new = BETA_FIRST * moment_one + (1.0 - BETA_FIRST) * gradient
    second_new = BETA_SECOND * moment_two + (1.0 - BETA_SECOND) * gradient * gradient
    first_hat = first_new / (1.0 - BETA_FIRST**STEP)
    second_hat = second_new / (1.0 - BETA_SECOND**STEP)
    weight_new = weight - step_rate * (
        first_hat / (jnp.sqrt(second_hat) + ADAM_EPS) + decay_rate * weight
    )
    return (weight_new, first_new, second_new)


def bits_of(count):
    return count.bit_length() - 1


def tie(value, *others):
    return lax.optimization_barrier((value, others))[0]


TRANSPOSED = (((1,), (1,)), ((), ()))
FLAT = (((1,), (0,)), ((), ()))


def product(left, right, dims=FLAT):
    return lax.dot_general(left, right, dims, preferred_element_type=jnp.float32)


def upright(pieces_ref):
    return jnp.concatenate([pieces_ref[m, 0].T for m in range(pieces_ref.shape[0])], axis=0)


def attend_kernel(query_ref, key_ref, value_ref, bias_ref, out_ref, total_ref):
    keys = upright(key_ref)
    length = key_ref.shape[3]
    for head in range(query_ref.shape[1]):
        scores = product(keys, query_ref[0, head]) * HEAD_SIZE ** (-0.5) + bias_ref[...]
        peak = jnp.max(scores, axis=0, keepdims=True)
        exponent = jnp.exp(scores - peak)
        total = jnp.sum(exponent, axis=0, keepdims=True)
        probability = (exponent * (1.0 / total)).astype(jnp.bfloat16)
        attended = 0.0
        for m in range(key_ref.shape[0]):
            attended += product(value_ref[m, 0], probability[m * length : (m + 1) * length])
        out_ref[0, head] = attended.astype(jnp.bfloat16)
        total_ref[0, head : head + 1] = peak + jnp.log(total)


def attend_back_kernel(
    query_ref, key_ref, value_ref, bias_ref, total_ref, grad_ref, query_grad, key_grad, value_grad
):
    keys = upright(key_ref)
    values = upright(value_ref)
    length = key_ref.shape[3]
    for head in range(query_ref.shape[1]):
        queries = query_ref[0, head]
        grads = grad_ref[0, head]
        scores = product(keys, queries) * HEAD_SIZE ** (-0.5) + bias_ref[...]
        probability = jnp.exp(scores - total_ref[0, head : head + 1])
        weighted = probability * product(values, grads)
        grad_scores = weighted - probability * jnp.sum(weighted, axis=0, keepdims=True)
        grad_scores = grad_scores.astype(jnp.bfloat16)
        probability = probability.astype(jnp.bfloat16)
        from_keys = 0.0
        for m in range(key_ref.shape[0]):
            part = slice(m * length, (m + 1) * length)
            from_keys += product(key_ref[m, 0], grad_scores[part])
            from_queries = product(queries, grad_scores[part], TRANSPOSED) * HEAD_SIZE ** (-0.5)
            from_grads = product(grads, probability[part], TRANSPOSED)
            if head == 0:
                key_grad[m, 0] = from_queries
                value_grad[m, 0] = from_grads
            else:
                key_grad[m, 0] += from_queries
                value_grad[m, 0] += from_grads
        query_grad[0, head] = from_keys * HEAD_SIZE ** (-0.5)


def group_block(array):
    zeros = (0,) * (array.ndim - 1)
    return pl.BlockSpec((1,) + array.shape[1:], lambda g: (g,) + zeros)


def piece_block(pieces, first):
    block = (pieces.shape[0], 1) + pieces.shape[2:]
    return pl.BlockSpec(block, lambda g: (0, first + g, 0, 0))


def attend(queries, keys_values, bias):
    groups, heads, _, length = queries.shape
    totals = jax.ShapeDtypeStruct((groups, heads, length), jnp.float32)
    return pl.pallas_call(
        attend_kernel,
        grid=(groups,),
        in_specs=[
            group_block(queries),
            piece_block(keys_values, 0),
            piece_block(keys_values, groups),
            pl.BlockSpec(bias.shape, lambda g: (0, 0)),
        ],
        out_specs=[group_block(queries), group_block(totals)],
        out_shape=[jax.ShapeDtypeStruct(queries.shape, queries.dtype), totals],
        compiler_params=pltpu.CompilerParams(vmem_limit_bytes=40 << 20),
        cost_estimate=pl.CostEstimate(flops=1 << 28, bytes_accessed=1 << 20, transcendentals=0),
    )(queries, keys_values, keys_values, bias)


def attend_back(queries, keys_values, bias, totals, grads, clock):
    groups = queries.shape[0]
    from_queries = jax.ShapeDtypeStruct(queries.shape, jnp.float32)
    from_keys = jax.ShapeDtypeStruct(
        (keys_values.shape[0], groups) + keys_values.shape[2:], jnp.float32
    )
    def after_clock(*refs):
        attend_back_kernel(*refs[len(clock) :])

    return pl.pallas_call(
        after_clock,
        grid=(groups,),
        in_specs=[pl.BlockSpec(memory_space=pl.ANY)] * len(clock)
        + [
            group_block(queries),
            piece_block(keys_values, 0),
            piece_block(keys_values, groups),
            pl.BlockSpec(bias.shape, lambda g: (0, 0)),
            group_block(totals),
            group_block(grads),
        ],
        out_specs=[group_block(from_queries), piece_block(from_keys, 0), piece_block(from_keys, 0)],
        out_shape=[from_queries, from_keys, from_keys],
        compiler_params=pltpu.CompilerParams(vmem_limit_bytes=40 << 20),
        cost_estimate=pl.CostEstimate(flops=1 << 28, bytes_accessed=1 << 20, transcendentals=0),
    )(*clock, queries, keys_values, keys_values, bias, totals, grads)


class Slice:

    def __init__(self, dp_size, grp_size):
        self.dp_size = dp_size
        self.grp_size = grp_size
        dp_bits = bits_of(dp_size)
        grp_bits = bits_of(grp_size)
        x_count = min(max(grp_bits - 1, 0), dp_bits)
        z_bits = [("dp", bit) for bit in range(dp_bits - 1, x_count - 1, -1)]
        self.far = z_bits[:1]
        self.near = z_bits[1:]
        self.x = [("dp", bit) for bit in range(x_count - 1, -1, -1)]
        self.y = [("grp", bit) for bit in range(1, grp_bits)]
        self.core = [("grp", 0)]
        self.clock = None

    def size(self, axis):
        return self.dp_size if axis == "dp" else self.grp_size

    def own(self, axis, bit):
        return (lax.axis_index(axis) >> bit) & 1

    def swap(self, array, step):
        axis, bit = step
        size = self.size(axis)
        return lax.ppermute(array, axis, [(k, k ^ (1 << bit)) for k in range(size)])

    def in_turn(self, value):
        if self.clock is None:
            return value
        return tie(value, self.clock)

    def to_masks(self, rows):
        blocks = rows.reshape(self.grp_size, -1, rows.shape[1])
        own = lax.axis_index("grp")
        return [
            lax.dynamic_index_in_dim(blocks, own ^ m, 0, keepdims=False)
            for m in range(self.grp_size)
        ]

    def from_masks(self, blocks):
        for bit in range(bits_of(self.grp_size)):
            own = self.own("grp", bit)
            blocks = [
                jnp.where(own == 0, block, blocks[k ^ (1 << bit)]) for k, block in enumerate(blocks)
            ]
        return jnp.concatenate(blocks, axis=0)

    def pair(self, array):
        return jnp.concatenate([array, self.swap(array, self.core[0])], axis=1)

    def pair_blocks(self, blocks):
        own = range(0, self.grp_size, 2)
        came = self.swap(jnp.stack([blocks[m ^ 1] for m in own]), self.core[0])
        return {m: jnp.concatenate([blocks[m], came[n]], axis=1) for n, m in enumerate(own)}


class Gather:

    def __init__(self, net, chunks, bits=()):
        self.net = net
        self.chunks = chunks
        self.bits = list(bits)
        self.sent = None

    def send(self, steps):
        for step in steps:
            self.land()
            self.sent = (step, [self.net.swap(array, step) for _, array in self.chunks])
        return self

    def land(self, join=True, in_turn=False):
        if self.sent is None:
            return self
        (axis, bit), came = self.sent
        self.sent = None
        if in_turn:
            came = self.net.in_turn(came)
        chunks = []
        if axis == "grp":
            for (masks, array), other in zip(self.chunks, came):
                other_masks = [m ^ (1 << bit) for m in masks]
                if join:
                    chunks.append((masks + other_masks, jnp.concatenate([array, other])))
                else:
                    chunks += [(masks, array), (other_masks, other)]
        else:
            own = self.net.own(axis, bit)
            self.bits = sorted(self.bits + [bit], reverse=True)
            place = 1 + self.bits.index(bit)
            for (masks, array), other in zip(self.chunks, came):
                low = jnp.where(own == 0, array, other)
                high = jnp.where(own == 0, other, array)
                chunks.append((masks, jnp.stack([low, high], axis=place)))
        self.chunks = chunks
        if in_turn:
            self.net.clock = came if axis == "grp" and not join else [a for _, a in chunks]
        return self

    def land_next(self, steps, join=True):
        return self.land(join, True).send(steps)

    def rows(self, low, high):
        chunks = [(masks, array[..., low:high, :]) for masks, array in self.chunks]
        return Gather(self.net, chunks, self.bits)

    def pieces(self):
        return {
            mask: array[n].reshape(-1, array.shape[-1])
            for masks, array in self.chunks
            for n, mask in enumerate(masks)
        }


def gradient_kernel(own_ref, kept_rows, sent_rows, kept_blocks, sent_blocks, kept_ref, sent_ref):
    for rows, blocks, out in (
        (kept_rows, kept_blocks, kept_ref),
        (sent_rows, sent_blocks, sent_ref),
    ):
        for p in range(blocks.shape[0]):
            out[p, 0, 0] = product(rows[0, 0, 0], blocks[p], TRANSPOSED).astype(out.dtype)


def landing_kernel(own_ref, kept_in, sent_in, kept_came, sent_came, kept_ref, sent_ref):
    kept_ref[0, 0] = kept_in[0, 0, 0] + kept_came[0, 0, 0].astype(jnp.float32)
    sent = sent_in[0, 0, 0] + sent_came[0, 0, 0].astype(jnp.float32)
    sent_ref[0, 0] = sent.astype(sent_ref.dtype)


def whole(array):
    zeros = (0,) * array.ndim
    return pl.BlockSpec(array.shape, lambda a, m, own: zeros)


def half(array, other):
    block = (1, 1, 1) + array.shape[3:]
    if array.shape[1] == 1:
        return pl.BlockSpec(block, lambda a, m, own: (a, 0, m, 0, 0))
    if other:
        return pl.BlockSpec(block, lambda a, m, own: (a, 1 - own[0], m, 0, 0))
    return pl.BlockSpec(block, lambda a, m, own: (a, own[0], m, 0, 0))


def halves_call(kernel, grid, specs, out_blocks, out_shape, args, clock):
    def after_clock(own_ref, *refs):
        kernel(own_ref, *refs[len(clock) :])

    later = pl.BlockSpec(memory_space=pl.ANY)
    args = args[:1] + tuple(clock) + args[1:]
    return pl.pallas_call(
        after_clock,
        grid_spec=pltpu.PrefetchScalarGridSpec(
            num_scalar_prefetch=1,
            grid=grid,
            in_specs=[later] * len(clock) + specs,
            out_specs=out_blocks,
        ),
        out_shape=[
            jax.ShapeDtypeStruct(out_shape[0], jnp.float32),
            jax.ShapeDtypeStruct(out_shape[1], jnp.bfloat16),
        ],
        compiler_params=pltpu.CompilerParams(vmem_limit_bytes=40 << 20),
        cost_estimate=pl.CostEstimate(flops=1 << 28, bytes_accessed=1 << 20, transcendentals=0),
    )(*args)


def add_kernel(kept_ref, came_ref, *refs):
    refs[-1][...] = kept_ref[...] + came_ref[...].astype(jnp.float32)


def add_in_turn(kept, came, clock):
    here = pl.BlockSpec(memory_space=pltpu.VMEM)
    return pl.pallas_call(
        add_kernel,
        in_specs=[here, here] + [pl.BlockSpec(memory_space=pl.ANY)] * len(clock),
        out_specs=here,
        out_shape=jax.ShapeDtypeStruct(kept.shape, jnp.float32),
        compiler_params=pltpu.CompilerParams(vmem_limit_bytes=40 << 20),
        cost_estimate=pl.CostEstimate(flops=1 << 20, bytes_accessed=1 << 20, transcendentals=0),
    )(kept, came, *clock)


class Sum:

    def __init__(self, net, grad_rows, blocks, steps, low=0, high=None, clock=()):
        self.net = net
        self.bits = list(range(bits_of(net.dp_size) - 1, -1, -1))
        self.masks = sorted(blocks)
        rows = grad_rows.reshape(net.dp_size, -1, grad_rows.shape[1])[:, low:high]
        axis, bit = steps[-1]
        own = jnp.zeros((1,), jnp.int32)
        kept = sent = jnp.stack([blocks[m] for m in self.masks])
        if axis == "grp":
            kept = jnp.stack([blocks[m] for m in self.masks if not m & (1 << bit)])
            sent = jnp.stack([blocks[m] for m in self.masks if m & (1 << bit)])
            self.masks = [m for m in self.masks if not m & (1 << bit)]
            rows = rows[:, None, None]
        else:
            own = net.own(axis, bit).astype(jnp.int32).reshape(1)
            self.bits.remove(bit)
            rows = rows.reshape((-1, 2, 1 << bit) + rows.shape[1:])
        grid = (rows.shape[0], rows.shape[2])
        pieces, width = kept.shape[:2]
        shape = (pieces,) + grid + (rows.shape[3], width)
        block = pl.BlockSpec(
            (pieces, 1, 1) + shape[3:], lambda a, m, own: (0, a, m, 0, 0)
        )
        self.held, self.outgoing = halves_call(
            gradient_kernel,
            grid,
            [half(rows, False), half(rows, True), whole(kept), whole(sent)],
            [block, block],
            (shape, shape),
            (own, rows, rows, kept, sent),
            clock,
        )
        self.held = self.held.reshape((pieces, -1) + shape[3:])
        self.came = net.swap(self.outgoing, steps[-1])
        for step in steps[-2::-1]:
            self.step(step)

    def step(self, step, clock=()):
        axis, bit = step
        pieces, blocks, rows, width = self.held.shape
        own = jnp.zeros((1,), jnp.int32)
        if axis == "grp":
            high = len({m >> (bit + 1) for m in self.masks})
            self.masks = [m for m in self.masks if not m & (1 << bit)]
            view = (high, 2, -1, rows, width)
        else:
            own = self.net.own(axis, bit).astype(jnp.int32).reshape(1)
            place = self.bits.index(bit)
            self.bits.remove(bit)
            view = (pieces << place, 2, -1, rows, width)
        held = self.held.reshape(view)
        came = self.came.reshape(view)
        grid = (held.shape[0], held.shape[2])
        shape = grid + (rows, width)
        block = pl.BlockSpec((1, 1, rows, width), lambda a, m, own: (a, m, 0, 0))
        self.held, self.outgoing = halves_call(
            landing_kernel,
            grid,
            [half(held, False), half(held, True), half(came, False), half(came, True)],
            [block, block],
            (shape, shape),
            (own, held, held, came, came),
            clock,
        )
        self.held = self.held.reshape((len(self.masks), -1, rows, width))
        self.came = self.net.swap(self.outgoing, step)

    def land_next(self, steps):
        for step in steps[::-1]:
            self.step(step, self.net.clock)
        if steps:
            self.net.clock = [self.outgoing]
        return self

    def owned(self):
        came = self.came.reshape(self.held.shape)
        return (self.held + came.astype(jnp.float32))[0, 0]


def forward_product(blocks, pieces):
    total = None
    for mask, piece in pieces.items():
        term = product(piece, blocks[mask])
        total = term if total is None else total + term
    return total


def backward_product(grad_rows, pieces):
    return [product(pieces[mask], grad_rows, (((0,), (0,)), ((), ()))) for mask in sorted(pieces)]


def local(
    dp_size,
    grp_size,
    tokens,
    cotangent,
    segments,
    positions,
    w_qkv,
    m_qkv,
    v_qkv,
    w_out,
    m_out,
    v_out,
    w_in,
    m_in,
    v_in,
    w_down,
    m_down,
    v_down,
    gains,
    m_gains,
    v_gains,
):
    net = Slice(dp_size, grp_size)
    low = jnp.bfloat16
    qkv_width = w_qkv.shape[1]
    qkv_out = jnp.concatenate([w_qkv.astype(low).T, w_out.astype(low).T])
    qkv_out = Gather(net, [([0], qkv_out[None])]).send(net.far)
    gate = Gather(net, [([0], w_in[0].astype(low).T[None])]).send(net.y)
    up = Gather(net, [([0], w_in[1].astype(low).T[None])]).send(net.x)
    down_low = w_down.astype(low).T[None]
    upstream_low = cotangent[0].T
    upstream_pair = net.pair(upstream_low)

    inputs = tokens[0].T.astype(jnp.float32)
    token_length = inputs.shape[1]
    query_width = QUERY_HEADS * HEAD_SIZE
    key_end = query_width + KEY_VALUE_HEADS * HEAD_SIZE
    head_shape = (KEY_VALUE_HEADS, -1, HEAD_SIZE, token_length)
    own_piece = lax.axis_index("grp")
    query_places = own_piece * token_length + jnp.arange(token_length)
    segment_pieces = segments[0].reshape(grp_size, token_length)
    own_segments = lax.dynamic_index_in_dim(segment_pieces, own_piece, 0, keepdims=False)
    key_masks = [0]
    for axis, bit in net.y + net.core:
        key_masks = key_masks + [m ^ (1 << bit) for m in key_masks]
    key_segments = jnp.concatenate(
        [
            lax.dynamic_index_in_dim(segment_pieces, own_piece ^ m, 0, keepdims=False)
            for m in key_masks
        ]
    )
    key_places = jnp.concatenate(
        [(own_piece ^ m) * token_length + jnp.arange(token_length) for m in key_masks]
    )
    allowed = (key_places[:, None] <= query_places[None, :]) & (
        key_segments[:, None] == own_segments[None, :]
    )
    bias = jnp.where(allowed, 0.0, MASKED)
    rotary_cosine, rotary_sine = rotation(positions[0])
    factor_one = lax.rsqrt(jnp.mean(inputs * inputs, axis=0, keepdims=True) + NORM_EPS)
    plain_one = inputs * factor_one
    normed = (plain_one * gains[0][:, None]).astype(low)
    normed_blocks = net.to_masks(normed)
    normed_pair = net.pair_blocks(normed_blocks)
    qkv_out.land_next(net.near)
    down = Gather(net, [([0], net.in_turn(down_low))]).send(net.far)
    gate.land(True, True)
    up.land(True, True)
    normed_pair = net.in_turn(normed_pair)
    upstream_pair = tie(upstream_pair, normed_pair)
    net.clock = (normed_pair, upstream_pair)
    qkv_out.land(True, True)
    qkv = qkv_out.rows(0, qkv_width).send(net.x)
    out = qkv_out.rows(qkv_width, None).send(net.y)
    gate.send(net.far)
    down.land_next(net.near)
    out.land_next(net.x)
    qkv.land_next(net.y)
    up.chunks = [(masks, net.in_turn(array)) for masks, array in up.chunks]
    up.send(net.far)
    gate.land_next(net.near)
    down.land_next(net.y)
    out.land(True, True)
    up.land_next(net.near)
    gate.land_next(net.x)
    qkv.land_next(net.core)
    down.land_next(net.x)
    up.land_next(net.y)
    qkv.land(False)
    blended = forward_product(normed_blocks, qkv.pieces())
    rotated = apply_rotary(blended[:key_end], rotary_cosine, rotary_sine).astype(low)
    keys_values = jnp.concatenate([rotated[query_width:], blended[key_end:].astype(low)])[None]
    gate.land(True, True)
    for step in net.y + net.core:
        came = net.swap(keys_values, step)
        if step == net.core[0]:
            came = net.in_turn(came)
        keys_values = jnp.concatenate([keys_values, came], axis=0)
    out.send(net.core)
    gate.send(net.core)

    keys_values = keys_values.reshape(grp_size, -1, HEAD_SIZE, token_length)
    queries = rotated[:query_width].reshape(head_shape)
    attended, log_totals = attend(queries, keys_values, bias)
    attended_low = attended.reshape(query_width, token_length)
    attended_blocks = net.to_masks(attended_low)
    net.clock = attended_blocks
    up.land_next(net.core, False)
    down.land_next(net.core)
    gate, up, down, out = [part.land(False).pieces() for part in (gate, up, down, out)]
    middle = inputs + forward_product(attended_blocks, out)
    factor_two = lax.rsqrt(jnp.mean(middle * middle, axis=0, keepdims=True) + NORM_EPS)
    plain_two = middle * factor_two
    normed_two = (plain_two * gains[1][:, None]).astype(low)
    normed_two_blocks = net.to_masks(normed_two)
    gate_pre = forward_product(normed_two_blocks, gate)
    up_proj = forward_product(normed_two_blocks, up)
    sigmoid_gate = jax.nn.sigmoid(gate_pre)
    activated = gate_pre * sigmoid_gate
    hidden = (activated * up_proj).astype(low)
    hidden_blocks = net.to_masks(hidden)
    layer_out = middle + forward_product(hidden_blocks, down)

    upstream = upstream_low.astype(jnp.float32)
    grad_down = Sum(net, upstream_pair, net.pair_blocks(hidden_blocks), net.x)
    grad_hidden = net.from_masks(backward_product(upstream_low, down))
    grad_gate = (
        grad_hidden * up_proj * sigmoid_gate * (1.0 + gate_pre * (1.0 - sigmoid_gate))
    ).astype(low)
    grad_up = (grad_hidden * activated).astype(low)
    normed_two_pair = net.pair_blocks(normed_two_blocks)
    grad_in_gate = Sum(net, net.pair(grad_gate), normed_two_pair, net.x)
    grad_in_up = Sum(net, net.pair(grad_up), normed_two_pair, net.y)
    grad_normed_two = net.from_masks(
        [
            one + two
            for one, two in zip(
                backward_product(grad_gate, gate), backward_product(grad_up, up)
            )
        ]
    )
    back_two, gain_two = norm_back(grad_normed_two, plain_two, factor_two, gains[1])
    grad_middle = upstream + back_two
    middle_low = grad_middle.astype(low)
    attended_gradient = net.from_masks(backward_product(middle_low, out))
    outgoing = [part.outgoing for part in (grad_down, grad_in_up, grad_in_gate)]
    attended_gradient = attended_gradient.astype(low).reshape(head_shape)
    grad_queries, grad_keys, grad_values = attend_back(
        queries, keys_values, bias, log_totals, attended_gradient, outgoing
    )
    grad_keys_values = jnp.concatenate([grad_keys, grad_values], axis=1).reshape(
        grp_size, -1, token_length
    )
    net.clock = [grad_keys_values]
    for step in net.core + net.y[::-1]:
        half = grad_keys_values.shape[0] // 2
        came = net.swap(grad_keys_values[half:].astype(low), step)
        if step == net.core[0]:
            grad_down.land_next(net.near)
            grad_in_up.land_next(net.near)
        grad_keys_values = add_in_turn(grad_keys_values[:half], came, net.clock)
        net.clock = [grad_keys_values]
    grad_queries = grad_queries.reshape(query_width, token_length)
    grad_keys_values = grad_keys_values[0]
    key_width = key_end - query_width
    grad_mixed = jnp.concatenate(
        [
            inverse_rotary(grad_queries, rotary_cosine, rotary_sine),
            inverse_rotary(grad_keys_values[:key_width], rotary_cosine, rotary_sine),
            grad_keys_values[key_width:],
        ]
    ).astype(low)
    net.clock = [grad_mixed]
    mixed_pair = net.pair(grad_mixed)
    middle_pair = net.pair(middle_low)
    attended_pair = net.pair_blocks(attended_blocks)
    grad_out = Sum(net, middle_pair, attended_pair, net.y, clock=net.clock)
    net.clock = [grad_out.outgoing]
    grad_down.land_next(net.far)
    cut = qkv_width // 16 * 8
    first_qkv = Sum(net, mixed_pair, normed_pair, net.y, 0, cut, net.clock)
    second_qkv = Sum(net, mixed_pair, normed_pair, net.x, cut, None, net.clock)
    net.clock = [first_qkv.outgoing, second_qkv.outgoing]
    grad_in_gate.land_next(net.y)
    grad_normed = net.from_masks(backward_product(grad_mixed, qkv.pieces()))
    back_one, gain_one = norm_back(grad_normed, plain_one, factor_one, gains[0])
    tokens_grad = grad_middle + back_one
    gain_grads = jnp.stack([gain_one, gain_two])

    def gain_steps(gain_grads, steps):
        for step in steps:
            gain_grads = add_in_turn(gain_grads, net.swap(gain_grads, step), net.clock)
            net.clock = [gain_grads]
        return gain_grads

    grad_in_up.land_next(net.far)
    grad_out.land_next(net.x)
    gain_grads = gain_steps(gain_grads, net.core)
    second_qkv.land_next(net.y)
    first_qkv.land_next(net.x)
    grad_down.land_next(net.y)
    grad_in_gate.land_next(net.near)
    grad_in_up.land_next(net.x)
    gain_grads = gain_steps(gain_grads, net.y)
    second_qkv.land_next(net.near)
    first_qkv.land_next(net.near)
    grad_out.land_next(net.near)
    gain_grads = gain_steps(gain_grads, net.x)
    grad_in_gate.land_next(net.far)
    second_qkv.land_next(net.far)
    first_qkv.land_next(net.far)
    grad_out.land_next(net.far)
    gain_grads = gain_steps(gain_grads, net.near + net.far)
    owned_down = grad_down.owned()
    owned_out = grad_out.owned()
    owned_qkv = jnp.concatenate([first_qkv.owned(), second_qkv.owned()])
    owned_in = jnp.stack([grad_in_gate.owned(), grad_in_up.owned()])
    new_qkv, mom_qkv, sq_qkv = adamw_update(
        w_qkv, m_qkv, v_qkv, owned_qkv.T, RATE_MATRIX, WEIGHT_DECAY
    )
    new_out, mom_out, sq_out = adamw_update(
        w_out, m_out, v_out, owned_out.T, RATE_MATRIX, WEIGHT_DECAY
    )
    new_in, mom_in, sq_in = adamw_update(
        w_in, m_in, v_in, owned_in.transpose(0, 2, 1), RATE_MATRIX, WEIGHT_DECAY
    )
    new_down, mom_down, sq_down = adamw_update(
        w_down, m_down, v_down, owned_down.T, RATE_MATRIX, WEIGHT_DECAY
    )
    new_gains, mom_gains, sq_gains = adamw_update(
        gains, m_gains, v_gains, gain_grads, RATE_GAIN, 0.0
    )
    return (
        layer_out.T[None],
        tokens_grad.T[None],
        new_qkv,
        mom_qkv,
        sq_qkv,
        new_out,
        mom_out,
        sq_out,
        new_in,
        mom_in,
        sq_in,
        new_down,
        mom_down,
        sq_down,
        new_gains,
        mom_gains,
        sq_gains,
    )


def solution(mesh):
    return jax.shard_map(
        partial(local, mesh.shape["dp"], mesh.shape["grp"]),
        mesh=mesh,
        in_specs=(
            P("dp", "grp", None),
            P("dp", "grp", None),
            P("dp", None),
            P("dp", "grp"),
            P("grp", "dp"),
            P("grp", "dp"),
            P("grp", "dp"),
            P("grp", "dp"),
            P("grp", "dp"),
            P("grp", "dp"),
            P(None, "grp", "dp"),
            P(None, "grp", "dp"),
            P(None, "grp", "dp"),
            P("grp", "dp"),
            P("grp", "dp"),
            P("grp", "dp"),
            P(),
            P(),
            P(),
        ),
        out_specs=(
            P("dp", "grp", None),
            P("dp", "grp", None),
            P("grp", "dp"),
            P("grp", "dp"),
            P("grp", "dp"),
            P("grp", "dp"),
            P("grp", "dp"),
            P("grp", "dp"),
            P(None, "grp", "dp"),
            P(None, "grp", "dp"),
            P(None, "grp", "dp"),
            P("grp", "dp"),
            P("grp", "dp"),
            P("grp", "dp"),
            P(),
            P(),
            P(),
        ),
        check_vma=False,
    )
```

```python
from functools import partial

import jax
import jax.numpy as jnp
from jax import lax
from jax.experimental import pallas as pl
from jax.experimental.pallas import tpu as pltpu
from jax.sharding import PartitionSpec as P

QUERY_HEADS = 15
KEY_VALUE_HEADS = 5
HEAD_SIZE = 64
STEP = 10


NORM_EPS = 1e-05
ROPE_BASE = 10000.0
MASKED = -1e30
BETA_FIRST = 0.9
BETA_SECOND = 0.95
ADAM_EPS = 1e-08
WEIGHT_DECAY = 0.1
RATE_MATRIX = 0.05
RATE_GAIN = 0.3


def rotation(places_in_doc):
    frequency = ROPE_BASE ** (-(jnp.arange(HEAD_SIZE // 2).astype(jnp.float32) * 2.0 / HEAD_SIZE))
    angles = frequency[:, None] * places_in_doc.astype(jnp.float32)[None, :]
    return (jnp.cos(angles), jnp.sin(angles))


def halves_of(head_rows):
    halves = head_rows.reshape(-1, 2, HEAD_SIZE // 2, head_rows.shape[-1])
    return halves[:, 0], halves[:, 1]


def apply_rotary(head_rows, rotary_cosine, rotary_sine):
    front_half, back_half = halves_of(head_rows)
    return jnp.stack(
        [
            front_half * rotary_cosine - back_half * rotary_sine,
            back_half * rotary_cosine + front_half * rotary_sine,
        ],
        axis=1,
    ).reshape(-1, head_rows.shape[-1])


def inverse_rotary(grad_rows, rotary_cosine, rotary_sine):
    return apply_rotary(grad_rows, rotary_cosine, -rotary_sine)


def norm_back(grad_output, plain_rows, factor, gain_row):
    scaled = grad_output * gain_row[:, None]
    grad_input = factor * (
        scaled - plain_rows * jnp.mean(scaled * plain_rows, axis=0, keepdims=True)
    )
    gain_gradient = jnp.sum(grad_output * plain_rows, axis=1)
    return (grad_input, gain_gradient)


def adamw_update(weight, moment_one, moment_two, gradient, step_rate, decay_rate):
    first_new = BETA_FIRST * moment_one + (1.0 - BETA_FIRST) * gradient
    second_new = BETA_SECOND * moment_two + (1.0 - BETA_SECOND) * gradient * gradient
    first_hat = first_new / (1.0 - BETA_FIRST**STEP)
    second_hat = second_new / (1.0 - BETA_SECOND**STEP)
    weight_new = weight - step_rate * (
        first_hat / (jnp.sqrt(second_hat) + ADAM_EPS) + decay_rate * weight
    )
    return (weight_new, first_new, second_new)


def bits_of(count):
    return count.bit_length() - 1


def tie(value, *others):
    return lax.optimization_barrier((value, others))[0]


TRANSPOSED = (((1,), (1,)), ((), ()))
FLAT = (((1,), (0,)), ((), ()))


def product(left, right, dims=FLAT):
    return lax.dot_general(left, right, dims, preferred_element_type=jnp.float32)


def upright(pieces_ref):
    return jnp.concatenate([pieces_ref[m, 0].T for m in range(pieces_ref.shape[0])], axis=0)


def attend_kernel(query_ref, key_ref, value_ref, bias_ref, out_ref, total_ref):
    keys = upright(key_ref)
    length = key_ref.shape[3]
    for head in range(query_ref.shape[1]):
        scores = product(keys, query_ref[0, head]) * HEAD_SIZE ** (-0.5) + bias_ref[...]
        peak = jnp.max(scores, axis=0, keepdims=True)
        exponent = jnp.exp(scores - peak)
        total = jnp.sum(exponent, axis=0, keepdims=True)
        probability = (exponent * (1.0 / total)).astype(jnp.bfloat16)
        attended = 0.0
        for m in range(key_ref.shape[0]):
            attended += product(value_ref[m, 0], probability[m * length : (m + 1) * length])
        out_ref[0, head] = attended.astype(jnp.bfloat16)
        total_ref[0, head : head + 1] = peak + jnp.log(total)


def attend_back_kernel(
    query_ref, key_ref, value_ref, bias_ref, total_ref, grad_ref, query_grad, key_grad, value_grad
):
    keys = upright(key_ref)
    values = upright(value_ref)
    length = key_ref.shape[3]
    for head in range(query_ref.shape[1]):
        queries = query_ref[0, head]
        grads = grad_ref[0, head]
        scores = product(keys, queries) * HEAD_SIZE ** (-0.5) + bias_ref[...]
        probability = jnp.exp(scores - total_ref[0, head : head + 1])
        weighted = probability * product(values, grads)
        grad_scores = weighted - probability * jnp.sum(weighted, axis=0, keepdims=True)
        grad_scores = grad_scores.astype(jnp.bfloat16)
        probability = probability.astype(jnp.bfloat16)
        from_keys = 0.0
        for m in range(key_ref.shape[0]):
            part = slice(m * length, (m + 1) * length)
            from_keys += product(key_ref[m, 0], grad_scores[part])
            from_queries = product(queries, grad_scores[part], TRANSPOSED) * HEAD_SIZE ** (-0.5)
            from_grads = product(grads, probability[part], TRANSPOSED)
            if head == 0:
                key_grad[m, 0] = from_queries
                value_grad[m, 0] = from_grads
            else:
                key_grad[m, 0] += from_queries
                value_grad[m, 0] += from_grads
        query_grad[0, head] = from_keys * HEAD_SIZE ** (-0.5)


def group_block(array):
    zeros = (0,) * (array.ndim - 1)
    return pl.BlockSpec((1,) + array.shape[1:], lambda g: (g,) + zeros)


def piece_block(pieces, first):
    block = (pieces.shape[0], 1) + pieces.shape[2:]
    return pl.BlockSpec(block, lambda g: (0, first + g, 0, 0))


def attend(queries, keys_values, bias):
    groups, heads, _, length = queries.shape
    totals = jax.ShapeDtypeStruct((groups, heads, length), jnp.float32)
    return pl.pallas_call(
        attend_kernel,
        grid=(groups,),
        in_specs=[
            group_block(queries),
            piece_block(keys_values, 0),
            piece_block(keys_values, groups),
            pl.BlockSpec(bias.shape, lambda g: (0, 0)),
        ],
        out_specs=[group_block(queries), group_block(totals)],
        out_shape=[jax.ShapeDtypeStruct(queries.shape, queries.dtype), totals],
        compiler_params=pltpu.CompilerParams(vmem_limit_bytes=40 << 20),
        cost_estimate=pl.CostEstimate(flops=1 << 28, bytes_accessed=1 << 20, transcendentals=0),
    )(queries, keys_values, keys_values, bias)


def attend_back(queries, keys_values, bias, totals, grads, clock):
    groups = queries.shape[0]
    from_queries = jax.ShapeDtypeStruct(queries.shape, jnp.float32)
    from_keys = jax.ShapeDtypeStruct(
        (keys_values.shape[0], groups) + keys_values.shape[2:], jnp.float32
    )
    def after_clock(*refs):
        attend_back_kernel(*refs[len(clock) :])

    return pl.pallas_call(
        after_clock,
        grid=(groups,),
        in_specs=[pl.BlockSpec(memory_space=pl.ANY)] * len(clock)
        + [
            group_block(queries),
            piece_block(keys_values, 0),
            piece_block(keys_values, groups),
            pl.BlockSpec(bias.shape, lambda g: (0, 0)),
            group_block(totals),
            group_block(grads),
        ],
        out_specs=[group_block(from_queries), piece_block(from_keys, 0), piece_block(from_keys, 0)],
        out_shape=[from_queries, from_keys, from_keys],
        compiler_params=pltpu.CompilerParams(vmem_limit_bytes=40 << 20),
        cost_estimate=pl.CostEstimate(flops=1 << 28, bytes_accessed=1 << 20, transcendentals=0),
    )(*clock, queries, keys_values, keys_values, bias, totals, grads)


class Slice:

    def __init__(self, dp_size, grp_size):
        self.dp_size = dp_size
        self.grp_size = grp_size
        dp_bits = bits_of(dp_size)
        grp_bits = bits_of(grp_size)
        x_count = min(max(grp_bits - 1, 0), dp_bits)
        z_bits = [("dp", bit) for bit in range(dp_bits - 1, x_count - 1, -1)]
        self.far = z_bits[:1]
        self.near = z_bits[1:]
        self.x = [("dp", bit) for bit in range(x_count - 1, -1, -1)]
        self.y = [("grp", bit) for bit in range(1, grp_bits)]
        self.core = [("grp", 0)]
        self.clock = None

    def size(self, axis):
        return self.dp_size if axis == "dp" else self.grp_size

    def own(self, axis, bit):
        return (lax.axis_index(axis) >> bit) & 1

    def swap(self, array, step):
        axis, bit = step
        size = self.size(axis)
        return lax.ppermute(array, axis, [(k, k ^ (1 << bit)) for k in range(size)])

    def in_turn(self, value):
        if self.clock is None:
            return value
        return tie(value, self.clock)

    def to_masks(self, rows):
        blocks = rows.reshape(self.grp_size, -1, rows.shape[1])
        own = lax.axis_index("grp")
        return [
            lax.dynamic_index_in_dim(blocks, own ^ m, 0, keepdims=False)
            for m in range(self.grp_size)
        ]

    def from_masks(self, blocks):
        for bit in range(bits_of(self.grp_size)):
            own = self.own("grp", bit)
            blocks = [
                jnp.where(own == 0, block, blocks[k ^ (1 << bit)]) for k, block in enumerate(blocks)
            ]
        return jnp.concatenate(blocks, axis=0)

    def pair(self, array):
        return jnp.concatenate([array, self.swap(array, self.core[0])], axis=1)

    def pair_blocks(self, blocks):
        own = range(0, self.grp_size, 2)
        came = self.swap(jnp.stack([blocks[m ^ 1] for m in own]), self.core[0])
        return {m: jnp.concatenate([blocks[m], came[n]], axis=1) for n, m in enumerate(own)}


class Gather:

    def __init__(self, net, chunks, bits=()):
        self.net = net
        self.chunks = chunks
        self.bits = list(bits)
        self.sent = None

    def send(self, steps):
        for step in steps:
            self.land()
            self.sent = (step, [self.net.swap(array, step) for _, array in self.chunks])
        return self

    def land(self, join=True, in_turn=False):
        if self.sent is None:
            return self
        (axis, bit), came = self.sent
        self.sent = None
        if in_turn:
            came = self.net.in_turn(came)
        chunks = []
        if axis == "grp":
            for (masks, array), other in zip(self.chunks, came):
                other_masks = [m ^ (1 << bit) for m in masks]
                if join:
                    chunks.append((masks + other_masks, jnp.concatenate([array, other])))
                else:
                    chunks += [(masks, array), (other_masks, other)]
        else:
            own = self.net.own(axis, bit)
            self.bits = sorted(self.bits + [bit], reverse=True)
            place = 1 + self.bits.index(bit)
            for (masks, array), other in zip(self.chunks, came):
                low = jnp.where(own == 0, array, other)
                high = jnp.where(own == 0, other, array)
                chunks.append((masks, jnp.stack([low, high], axis=place)))
        self.chunks = chunks
        if in_turn:
            self.net.clock = came if axis == "grp" and not join else [a for _, a in chunks]
        return self

    def land_next(self, steps, join=True):
        return self.land(join, True).send(steps)

    def rows(self, low, high):
        chunks = [(masks, array[..., low:high, :]) for masks, array in self.chunks]
        return Gather(self.net, chunks, self.bits)

    def pieces(self):
        return {
            mask: array[n].reshape(-1, array.shape[-1])
            for masks, array in self.chunks
            for n, mask in enumerate(masks)
        }


def gradient_kernel(own_ref, kept_rows, sent_rows, kept_blocks, sent_blocks, kept_ref, sent_ref):
    for rows, blocks, out in (
        (kept_rows, kept_blocks, kept_ref),
        (sent_rows, sent_blocks, sent_ref),
    ):
        for p in range(blocks.shape[0]):
            out[p, 0, 0] = product(rows[0, 0, 0], blocks[p], TRANSPOSED).astype(out.dtype)


def landing_kernel(own_ref, kept_in, sent_in, kept_came, sent_came, kept_ref, sent_ref):
    kept_ref[0, 0] = kept_in[0, 0, 0] + kept_came[0, 0, 0].astype(jnp.float32)
    sent = sent_in[0, 0, 0] + sent_came[0, 0, 0].astype(jnp.float32)
    sent_ref[0, 0] = sent.astype(sent_ref.dtype)


def whole(array):
    zeros = (0,) * array.ndim
    return pl.BlockSpec(array.shape, lambda a, m, own: zeros)


def half(array, other):
    block = (1, 1, 1) + array.shape[3:]
    if array.shape[1] == 1:
        return pl.BlockSpec(block, lambda a, m, own: (a, 0, m, 0, 0))
    if other:
        return pl.BlockSpec(block, lambda a, m, own: (a, 1 - own[0], m, 0, 0))
    return pl.BlockSpec(block, lambda a, m, own: (a, own[0], m, 0, 0))


def halves_call(kernel, grid, specs, out_blocks, out_shape, args, clock):
    def after_clock(own_ref, *refs):
        kernel(own_ref, *refs[len(clock) :])

    later = pl.BlockSpec(memory_space=pl.ANY)
    args = args[:1] + tuple(clock) + args[1:]
    return pl.pallas_call(
        after_clock,
        grid_spec=pltpu.PrefetchScalarGridSpec(
            num_scalar_prefetch=1,
            grid=grid,
            in_specs=[later] * len(clock) + specs,
            out_specs=out_blocks,
        ),
        out_shape=[
            jax.ShapeDtypeStruct(out_shape[0], jnp.float32),
            jax.ShapeDtypeStruct(out_shape[1], jnp.bfloat16),
        ],
        compiler_params=pltpu.CompilerParams(vmem_limit_bytes=40 << 20),
        cost_estimate=pl.CostEstimate(flops=1 << 28, bytes_accessed=1 << 20, transcendentals=0),
    )(*args)


def add_kernel(kept_ref, came_ref, *refs):
    refs[-1][...] = kept_ref[...] + came_ref[...].astype(jnp.float32)


def add_in_turn(kept, came, clock):
    here = pl.BlockSpec(memory_space=pltpu.VMEM)
    return pl.pallas_call(
        add_kernel,
        in_specs=[here, here] + [pl.BlockSpec(memory_space=pl.ANY)] * len(clock),
        out_specs=here,
        out_shape=jax.ShapeDtypeStruct(kept.shape, jnp.float32),
        compiler_params=pltpu.CompilerParams(vmem_limit_bytes=40 << 20),
        cost_estimate=pl.CostEstimate(flops=1 << 20, bytes_accessed=1 << 20, transcendentals=0),
    )(kept, came, *clock)


class Sum:

    def __init__(self, net, grad_rows, blocks, steps, low=0, high=None, clock=()):
        self.net = net
        self.bits = list(range(bits_of(net.dp_size) - 1, -1, -1))
        self.masks = sorted(blocks)
        rows = grad_rows.reshape(net.dp_size, -1, grad_rows.shape[1])[:, low:high]
        axis, bit = steps[-1]
        own = jnp.zeros((1,), jnp.int32)
        kept = sent = jnp.stack([blocks[m] for m in self.masks])
        if axis == "grp":
            kept = jnp.stack([blocks[m] for m in self.masks if not m & (1 << bit)])
            sent = jnp.stack([blocks[m] for m in self.masks if m & (1 << bit)])
            self.masks = [m for m in self.masks if not m & (1 << bit)]
            rows = rows[:, None, None]
        else:
            own = net.own(axis, bit).astype(jnp.int32).reshape(1)
            self.bits.remove(bit)
            rows = rows.reshape((-1, 2, 1 << bit) + rows.shape[1:])
        grid = (rows.shape[0], rows.shape[2])
        pieces, width = kept.shape[:2]
        shape = (pieces,) + grid + (rows.shape[3], width)
        block = pl.BlockSpec(
            (pieces, 1, 1) + shape[3:], lambda a, m, own: (0, a, m, 0, 0)
        )
        self.held, self.outgoing = halves_call(
            gradient_kernel,
            grid,
            [half(rows, False), half(rows, True), whole(kept), whole(sent)],
            [block, block],
            (shape, shape),
            (own, rows, rows, kept, sent),
            clock,
        )
        self.held = self.held.reshape((pieces, -1) + shape[3:])
        self.came = net.swap(self.outgoing, steps[-1])
        for step in steps[-2::-1]:
            self.step(step)

    def step(self, step, clock=()):
        axis, bit = step
        pieces, blocks, rows, width = self.held.shape
        own = jnp.zeros((1,), jnp.int32)
        if axis == "grp":
            high = len({m >> (bit + 1) for m in self.masks})
            self.masks = [m for m in self.masks if not m & (1 << bit)]
            view = (high, 2, -1, rows, width)
        else:
            own = self.net.own(axis, bit).astype(jnp.int32).reshape(1)
            place = self.bits.index(bit)
            self.bits.remove(bit)
            view = (pieces << place, 2, -1, rows, width)
        held = self.held.reshape(view)
        came = self.came.reshape(view)
        grid = (held.shape[0], held.shape[2])
        shape = grid + (rows, width)
        block = pl.BlockSpec((1, 1, rows, width), lambda a, m, own: (a, m, 0, 0))
        self.held, self.outgoing = halves_call(
            landing_kernel,
            grid,
            [half(held, False), half(held, True), half(came, False), half(came, True)],
            [block, block],
            (shape, shape),
            (own, held, held, came, came),
            clock,
        )
        self.held = self.held.reshape((len(self.masks), -1, rows, width))
        self.came = self.net.swap(self.outgoing, step)

    def land_next(self, steps):
        for step in steps[::-1]:
            self.step(step, self.net.clock)
        if steps:
            self.net.clock = [self.outgoing]
        return self

    def owned(self):
        came = self.came.reshape(self.held.shape)
        return (self.held + came.astype(jnp.float32))[0, 0]


def forward_product(blocks, pieces):
    total = None
    for mask, piece in pieces.items():
        term = product(piece, blocks[mask])
        total = term if total is None else total + term
    return total


def backward_product(grad_rows, pieces):
    return [product(pieces[mask], grad_rows, (((0,), (0,)), ((), ()))) for mask in sorted(pieces)]


def local(
    dp_size,
    grp_size,
    tokens,
    cotangent,
    segments,
    positions,
    w_qkv,
    m_qkv,
    v_qkv,
    w_out,
    m_out,
    v_out,
    w_in,
    m_in,
    v_in,
    w_down,
    m_down,
    v_down,
    gains,
    m_gains,
    v_gains,
):
    net = Slice(dp_size, grp_size)
    low = jnp.bfloat16
    qkv_width = w_qkv.shape[1]
    qkv_out = jnp.concatenate([w_qkv.astype(low).T, w_out.astype(low).T])
    qkv_out = Gather(net, [([0], qkv_out[None])]).send(net.far)
    gate = Gather(net, [([0], w_in[0].astype(low).T[None])]).send(net.y)
    up = Gather(net, [([0], w_in[1].astype(low).T[None])]).send(net.x)
    down_low = w_down.astype(low).T[None]
    upstream_low = cotangent[0].T
    upstream_pair = net.pair(upstream_low)

    inputs = tokens[0].T.astype(jnp.float32)
    token_length = inputs.shape[1]
    query_width = QUERY_HEADS * HEAD_SIZE
    key_end = query_width + KEY_VALUE_HEADS * HEAD_SIZE
    head_shape = (KEY_VALUE_HEADS, -1, HEAD_SIZE, token_length)
    own_piece = lax.axis_index("grp")
    query_places = own_piece * token_length + jnp.arange(token_length)
    segment_pieces = segments[0].reshape(grp_size, token_length)
    own_segments = lax.dynamic_index_in_dim(segment_pieces, own_piece, 0, keepdims=False)
    key_masks = [0]
    for axis, bit in net.y + net.core:
        key_masks = key_masks + [m ^ (1 << bit) for m in key_masks]
    key_segments = jnp.concatenate(
        [
            lax.dynamic_index_in_dim(segment_pieces, own_piece ^ m, 0, keepdims=False)
            for m in key_masks
        ]
    )
    key_places = jnp.concatenate(
        [(own_piece ^ m) * token_length + jnp.arange(token_length) for m in key_masks]
    )
    allowed = (key_places[:, None] <= query_places[None, :]) & (
        key_segments[:, None] == own_segments[None, :]
    )
    bias = jnp.where(allowed, 0.0, MASKED)
    rotary_cosine, rotary_sine = rotation(positions[0])
    factor_one = lax.rsqrt(jnp.mean(inputs * inputs, axis=0, keepdims=True) + NORM_EPS)
    plain_one = inputs * factor_one
    normed = (plain_one * gains[0][:, None]).astype(low)
    normed_blocks = net.to_masks(normed)
    normed_pair = net.pair_blocks(normed_blocks)
    qkv_out.land_next(net.near)
    down = Gather(net, [([0], net.in_turn(down_low))]).send(net.far)
    gate.land(True, True)
    up.land(True, True)
    normed_pair = net.in_turn(normed_pair)
    upstream_pair = tie(upstream_pair, normed_pair)
    net.clock = (normed_pair, upstream_pair)
    qkv_out.land(True, True)
    qkv = qkv_out.rows(0, qkv_width).send(net.x)
    out = qkv_out.rows(qkv_width, None).send(net.y)
    gate.chunks = [(masks, net.in_turn(array)) for masks, array in gate.chunks]
    gate.send(net.far)
    down.land_next(net.near)
    out.land_next(net.x)
    qkv.land_next(net.y)
    up.chunks = [(masks, net.in_turn(array)) for masks, array in up.chunks]
    up.send(net.far)
    gate.land_next(net.near)
    down.land_next(net.y)
    out.land(True, True)
    up.land_next(net.near)
    gate.land_next(net.x)
    qkv.land_next(net.core)
    down.land_next(net.x)
    up.land_next(net.y)
    qkv.land(False)
    blended = forward_product(normed_blocks, qkv.pieces())
    rotated = apply_rotary(blended[:key_end], rotary_cosine, rotary_sine).astype(low)
    keys_values = jnp.concatenate([rotated[query_width:], blended[key_end:].astype(low)])[None]
    gate.land(True, True)
    for step in net.y + net.core:
        came = net.swap(keys_values, step)
        if step == net.core[0]:
            came = net.in_turn(came)
        keys_values = jnp.concatenate([keys_values, came], axis=0)
    out.send(net.core)
    gate.send(net.core)

    keys_values = keys_values.reshape(grp_size, -1, HEAD_SIZE, token_length)
    queries = rotated[:query_width].reshape(head_shape)
    attended, log_totals = attend(queries, keys_values, bias)
    attended_low = attended.reshape(query_width, token_length)
    attended_blocks = net.to_masks(attended_low)
    net.clock = attended_blocks
    up.land_next(net.core, False)
    down.land_next(net.core)
    gate, up, down, out = [part.land(False).pieces() for part in (gate, up, down, out)]
    middle = inputs + forward_product(attended_blocks, out)
    factor_two = lax.rsqrt(jnp.mean(middle * middle, axis=0, keepdims=True) + NORM_EPS)
    plain_two = middle * factor_two
    normed_two = (plain_two * gains[1][:, None]).astype(low)
    normed_two_blocks = net.to_masks(normed_two)
    gate_pre = forward_product(normed_two_blocks, gate)
    up_proj = forward_product(normed_two_blocks, up)
    sigmoid_gate = jax.nn.sigmoid(gate_pre)
    activated = gate_pre * sigmoid_gate
    hidden = (activated * up_proj).astype(low)
    hidden_blocks = net.to_masks(hidden)
    layer_out = middle + forward_product(hidden_blocks, down)

    upstream = upstream_low.astype(jnp.float32)
    grad_down = Sum(net, upstream_pair, net.pair_blocks(hidden_blocks), net.x)
    grad_hidden = net.from_masks(backward_product(upstream_low, down))
    grad_gate = (
        grad_hidden * up_proj * sigmoid_gate * (1.0 + gate_pre * (1.0 - sigmoid_gate))
    ).astype(low)
    grad_up = (grad_hidden * activated).astype(low)
    normed_two_pair = net.pair_blocks(normed_two_blocks)
    gate_pair = net.pair(grad_gate)
    up_pair = net.pair(grad_up)
    grad_normed_two = net.from_masks(
        [
            one + two
            for one, two in zip(
                backward_product(grad_gate, gate), backward_product(grad_up, up)
            )
        ]
    )
    back_two, gain_two = norm_back(grad_normed_two, plain_two, factor_two, gains[1])
    grad_middle = upstream + back_two
    middle_low = grad_middle.astype(low)
    attended_gradient = net.from_masks(backward_product(middle_low, out))
    outgoing = [grad_down.outgoing]
    attended_gradient = attended_gradient.astype(low).reshape(head_shape)
    grad_queries, grad_keys, grad_values = attend_back(
        queries, keys_values, bias, log_totals, attended_gradient, outgoing
    )
    grad_keys_values = jnp.concatenate([grad_keys, grad_values], axis=1).reshape(
        grp_size, -1, token_length
    )
    net.clock = [grad_keys_values]
    for step in net.core + net.y[::-1]:
        half = grad_keys_values.shape[0] // 2
        came = net.swap(grad_keys_values[half:].astype(low), step)
        if step == net.y[-1]:
            grad_in_up = Sum(net, up_pair, normed_two_pair, net.y, clock=net.clock)
            net.clock = [grad_in_up.outgoing]
            grad_in_gate = Sum(net, gate_pair, normed_two_pair, net.x, clock=net.clock)
            net.clock = [grad_in_gate.outgoing]
            grad_down.land_next(net.near)
        grad_keys_values = add_in_turn(grad_keys_values[:half], came, net.clock)
        net.clock = [grad_keys_values]
    grad_queries = grad_queries.reshape(query_width, token_length)
    grad_keys_values = grad_keys_values[0]
    key_width = key_end - query_width
    grad_mixed = jnp.concatenate(
        [
            inverse_rotary(grad_queries, rotary_cosine, rotary_sine),
            inverse_rotary(grad_keys_values[:key_width], rotary_cosine, rotary_sine),
            grad_keys_values[key_width:],
        ]
    ).astype(low)
    net.clock = [grad_mixed]
    mixed_pair = net.pair(grad_mixed)
    middle_pair = net.pair(middle_low)
    attended_pair = net.pair_blocks(attended_blocks)
    cut = qkv_width // 16 * 8
    first_qkv = Sum(net, mixed_pair, normed_pair, net.y, 0, cut, net.clock)
    second_qkv = Sum(net, mixed_pair, normed_pair, net.x, cut, None, net.clock)
    net.clock = [first_qkv.outgoing, second_qkv.outgoing]
    grad_down.land_next(net.far)
    grad_in_up.land_next(net.near)
    grad_normed = net.from_masks(backward_product(grad_mixed, qkv.pieces()))
    back_one, gain_one = norm_back(grad_normed, plain_one, factor_one, gains[0])
    tokens_grad = grad_middle + back_one
    gain_grads = jnp.stack([gain_one, gain_two])

    def gain_steps(gain_grads, steps):
        for step in steps:
            gain_grads = add_in_turn(gain_grads, net.swap(gain_grads, step), net.clock)
            net.clock = [gain_grads]
        return gain_grads

    second_qkv.land_next(net.y)
    first_qkv.land_next(net.x)
    grad_out = Sum(net, middle_pair, attended_pair, net.y, clock=net.clock)
    net.clock = [grad_out.outgoing]
    grad_in_gate.land_next(net.y)
    grad_down.land_next(net.y)
    grad_in_up.land_next(net.far)
    gain_grads = gain_steps(gain_grads, net.core)
    second_qkv.land_next(net.near)
    first_qkv.land_next(net.near)
    grad_out.land_next(net.x)
    grad_in_gate.land_next(net.near)
    grad_in_up.land_next(net.x)
    gain_grads = gain_steps(gain_grads, net.y)
    second_qkv.land_next(net.far)
    first_qkv.land_next(net.far)
    grad_out.land_next(net.near)
    gain_grads = gain_steps(gain_grads, net.x)
    grad_in_gate.land_next(net.far)
    grad_out.land_next(net.far)
    gain_grads = gain_steps(gain_grads, net.near + net.far)
    owned_down = grad_down.owned()
    owned_out = grad_out.owned()
    owned_qkv = jnp.concatenate([first_qkv.owned(), second_qkv.owned()])
    owned_in = jnp.stack([grad_in_gate.owned(), grad_in_up.owned()])
    new_qkv, mom_qkv, sq_qkv = adamw_update(
        w_qkv, m_qkv, v_qkv, owned_qkv.T, RATE_MATRIX, WEIGHT_DECAY
    )
    new_out, mom_out, sq_out = adamw_update(
        w_out, m_out, v_out, owned_out.T, RATE_MATRIX, WEIGHT_DECAY
    )
    new_in, mom_in, sq_in = adamw_update(
        w_in, m_in, v_in, owned_in.transpose(0, 2, 1), RATE_MATRIX, WEIGHT_DECAY
    )
    new_down, mom_down, sq_down = adamw_update(
        w_down, m_down, v_down, owned_down.T, RATE_MATRIX, WEIGHT_DECAY
    )
    new_gains, mom_gains, sq_gains = adamw_update(
        gains, m_gains, v_gains, gain_grads, RATE_GAIN, 0.0
    )
    return (
        layer_out.T[None],
        tokens_grad.T[None],
        new_qkv,
        mom_qkv,
        sq_qkv,
        new_out,
        mom_out,
        sq_out,
        new_in,
        mom_in,
        sq_in,
        new_down,
        mom_down,
        sq_down,
        new_gains,
        mom_gains,
        sq_gains,
    )


def solution(mesh):
    return jax.shard_map(
        partial(local, mesh.shape["dp"], mesh.shape["grp"]),
        mesh=mesh,
        in_specs=(
            P("dp", "grp", None),
            P("dp", "grp", None),
            P("dp", None),
            P("dp", "grp"),
            P("grp", "dp"),
            P("grp", "dp"),
            P("grp", "dp"),
            P("grp", "dp"),
            P("grp", "dp"),
            P("grp", "dp"),
            P(None, "grp", "dp"),
            P(None, "grp", "dp"),
            P(None, "grp", "dp"),
            P("grp", "dp"),
            P("grp", "dp"),
            P("grp", "dp"),
            P(),
            P(),
            P(),
        ),
        out_specs=(
            P("dp", "grp", None),
            P("dp", "grp", None),
            P("grp", "dp"),
            P("grp", "dp"),
            P("grp", "dp"),
            P("grp", "dp"),
            P("grp", "dp"),
            P("grp", "dp"),
            P(None, "grp", "dp"),
            P(None, "grp", "dp"),
            P(None, "grp", "dp"),
            P("grp", "dp"),
            P("grp", "dp"),
            P("grp", "dp"),
            P(),
            P(),
            P(),
        ),
        check_vma=False,
    )
```

```python
from functools import partial

import jax
import jax.numpy as jnp
from jax import lax
from jax.experimental import pallas as pl
from jax.experimental.pallas import tpu as pltpu
from jax.sharding import PartitionSpec as P

QUERY_HEADS = 15
KEY_VALUE_HEADS = 5
HEAD_SIZE = 64
STEP = 10


NORM_EPS = 1e-05
ROPE_BASE = 10000.0
MASKED = -1e30
BETA_FIRST = 0.9
BETA_SECOND = 0.95
ADAM_EPS = 1e-08
WEIGHT_DECAY = 0.1
RATE_MATRIX = 0.05
RATE_GAIN = 0.3


def rotation(places_in_doc):
    frequency = ROPE_BASE ** (-(jnp.arange(HEAD_SIZE // 2).astype(jnp.float32) * 2.0 / HEAD_SIZE))
    angles = frequency[:, None] * places_in_doc.astype(jnp.float32)[None, :]
    return (jnp.cos(angles), jnp.sin(angles))


def halves_of(head_rows):
    halves = head_rows.reshape(-1, 2, HEAD_SIZE // 2, head_rows.shape[-1])
    return halves[:, 0], halves[:, 1]


def apply_rotary(head_rows, rotary_cosine, rotary_sine):
    front_half, back_half = halves_of(head_rows)
    return jnp.stack(
        [
            front_half * rotary_cosine - back_half * rotary_sine,
            back_half * rotary_cosine + front_half * rotary_sine,
        ],
        axis=1,
    ).reshape(-1, head_rows.shape[-1])


def inverse_rotary(grad_rows, rotary_cosine, rotary_sine):
    return apply_rotary(grad_rows, rotary_cosine, -rotary_sine)


def norm_back(grad_output, plain_rows, factor, gain_row):
    scaled = grad_output * gain_row[:, None]
    grad_input = factor * (
        scaled - plain_rows * jnp.mean(scaled * plain_rows, axis=0, keepdims=True)
    )
    gain_gradient = jnp.sum(grad_output * plain_rows, axis=1)
    return (grad_input, gain_gradient)


def adamw_update(weight, moment_one, moment_two, gradient, step_rate, decay_rate):
    first_new = BETA_FIRST * moment_one + (1.0 - BETA_FIRST) * gradient
    second_new = BETA_SECOND * moment_two + (1.0 - BETA_SECOND) * gradient * gradient
    first_hat = first_new / (1.0 - BETA_FIRST**STEP)
    second_hat = second_new / (1.0 - BETA_SECOND**STEP)
    weight_new = weight - step_rate * (
        first_hat / (jnp.sqrt(second_hat) + ADAM_EPS) + decay_rate * weight
    )
    return (weight_new, first_new, second_new)


def bits_of(count):
    return count.bit_length() - 1


def tie(value, *others):
    return lax.optimization_barrier((value, others))[0]


TRANSPOSED = (((1,), (1,)), ((), ()))
FLAT = (((1,), (0,)), ((), ()))


def product(left, right, dims=FLAT):
    return lax.dot_general(left, right, dims, preferred_element_type=jnp.float32)


def upright(pieces_ref):
    return jnp.concatenate([pieces_ref[m, 0].T for m in range(pieces_ref.shape[0])], axis=0)


def attend_kernel(query_ref, key_ref, value_ref, bias_ref, out_ref, total_ref):
    keys = upright(key_ref)
    length = key_ref.shape[3]
    for head in range(query_ref.shape[1]):
        scores = product(keys, query_ref[0, head]) * HEAD_SIZE ** (-0.5) + bias_ref[...]
        peak = jnp.max(scores, axis=0, keepdims=True)
        exponent = jnp.exp(scores - peak)
        total = jnp.sum(exponent, axis=0, keepdims=True)
        probability = (exponent * (1.0 / total)).astype(jnp.bfloat16)
        attended = 0.0
        for m in range(key_ref.shape[0]):
            attended += product(value_ref[m, 0], probability[m * length : (m + 1) * length])
        out_ref[0, head] = attended.astype(jnp.bfloat16)
        total_ref[0, head : head + 1] = peak + jnp.log(total)


def attend_back_kernel(
    query_ref, key_ref, value_ref, bias_ref, total_ref, grad_ref, query_grad, key_grad, value_grad
):
    keys = upright(key_ref)
    values = upright(value_ref)
    length = key_ref.shape[3]
    for head in range(query_ref.shape[1]):
        queries = query_ref[0, head]
        grads = grad_ref[0, head]
        scores = product(keys, queries) * HEAD_SIZE ** (-0.5) + bias_ref[...]
        probability = jnp.exp(scores - total_ref[0, head : head + 1])
        weighted = probability * product(values, grads)
        grad_scores = weighted - probability * jnp.sum(weighted, axis=0, keepdims=True)
        grad_scores = grad_scores.astype(jnp.bfloat16)
        probability = probability.astype(jnp.bfloat16)
        from_keys = 0.0
        for m in range(key_ref.shape[0]):
            part = slice(m * length, (m + 1) * length)
            from_keys += product(key_ref[m, 0], grad_scores[part])
            from_queries = product(queries, grad_scores[part], TRANSPOSED) * HEAD_SIZE ** (-0.5)
            from_grads = product(grads, probability[part], TRANSPOSED)
            if head == 0:
                key_grad[m, 0] = from_queries
                value_grad[m, 0] = from_grads
            else:
                key_grad[m, 0] += from_queries
                value_grad[m, 0] += from_grads
        query_grad[0, head] = from_keys * HEAD_SIZE ** (-0.5)


def group_block(array):
    zeros = (0,) * (array.ndim - 1)
    return pl.BlockSpec((1,) + array.shape[1:], lambda g: (g,) + zeros)


def piece_block(pieces, first):
    block = (pieces.shape[0], 1) + pieces.shape[2:]
    return pl.BlockSpec(block, lambda g: (0, first + g, 0, 0))


def attend(queries, keys_values, bias):
    groups, heads, _, length = queries.shape
    totals = jax.ShapeDtypeStruct((groups, heads, length), jnp.float32)
    return pl.pallas_call(
        attend_kernel,
        grid=(groups,),
        in_specs=[
            group_block(queries),
            piece_block(keys_values, 0),
            piece_block(keys_values, groups),
            pl.BlockSpec(bias.shape, lambda g: (0, 0)),
        ],
        out_specs=[group_block(queries), group_block(totals)],
        out_shape=[jax.ShapeDtypeStruct(queries.shape, queries.dtype), totals],
        compiler_params=pltpu.CompilerParams(vmem_limit_bytes=40 << 20),
        cost_estimate=pl.CostEstimate(flops=1 << 28, bytes_accessed=1 << 20, transcendentals=0),
    )(queries, keys_values, keys_values, bias)


def attend_back(queries, keys_values, bias, totals, grads, clock):
    groups = queries.shape[0]
    from_queries = jax.ShapeDtypeStruct(queries.shape, jnp.float32)
    from_keys = jax.ShapeDtypeStruct(
        (keys_values.shape[0], groups) + keys_values.shape[2:], jnp.float32
    )
    def after_clock(*refs):
        attend_back_kernel(*refs[len(clock) :])

    return pl.pallas_call(
        after_clock,
        grid=(groups,),
        in_specs=[pl.BlockSpec(memory_space=pl.ANY)] * len(clock)
        + [
            group_block(queries),
            piece_block(keys_values, 0),
            piece_block(keys_values, groups),
            pl.BlockSpec(bias.shape, lambda g: (0, 0)),
            group_block(totals),
            group_block(grads),
        ],
        out_specs=[group_block(from_queries), piece_block(from_keys, 0), piece_block(from_keys, 0)],
        out_shape=[from_queries, from_keys, from_keys],
        compiler_params=pltpu.CompilerParams(vmem_limit_bytes=40 << 20),
        cost_estimate=pl.CostEstimate(flops=1 << 28, bytes_accessed=1 << 20, transcendentals=0),
    )(*clock, queries, keys_values, keys_values, bias, totals, grads)


class Slice:

    def __init__(self, dp_size, grp_size):
        self.dp_size = dp_size
        self.grp_size = grp_size
        dp_bits = bits_of(dp_size)
        grp_bits = bits_of(grp_size)
        x_count = min(max(grp_bits - 1, 0), dp_bits)
        z_bits = [("dp", bit) for bit in range(dp_bits - 1, x_count - 1, -1)]
        self.far = z_bits[:1]
        self.near = z_bits[1:]
        self.x = [("dp", bit) for bit in range(x_count - 1, -1, -1)]
        self.y = [("grp", bit) for bit in range(1, grp_bits)]
        self.core = [("grp", 0)]
        self.clock = None

    def size(self, axis):
        return self.dp_size if axis == "dp" else self.grp_size

    def own(self, axis, bit):
        return (lax.axis_index(axis) >> bit) & 1

    def swap(self, array, step):
        axis, bit = step
        size = self.size(axis)
        return lax.ppermute(array, axis, [(k, k ^ (1 << bit)) for k in range(size)])

    def in_turn(self, value):
        if self.clock is None:
            return value
        return tie(value, self.clock)

    def to_masks(self, rows):
        blocks = rows.reshape(self.grp_size, -1, rows.shape[1])
        own = lax.axis_index("grp")
        return [
            lax.dynamic_index_in_dim(blocks, own ^ m, 0, keepdims=False)
            for m in range(self.grp_size)
        ]

    def from_masks(self, blocks):
        for bit in range(bits_of(self.grp_size)):
            own = self.own("grp", bit)
            blocks = [
                jnp.where(own == 0, block, blocks[k ^ (1 << bit)]) for k, block in enumerate(blocks)
            ]
        return jnp.concatenate(blocks, axis=0)

    def pair(self, array):
        return jnp.concatenate([array, self.swap(array, self.core[0])], axis=1)

    def pair_blocks(self, blocks):
        own = range(0, self.grp_size, 2)
        came = self.swap(jnp.stack([blocks[m ^ 1] for m in own]), self.core[0])
        return {m: jnp.concatenate([blocks[m], came[n]], axis=1) for n, m in enumerate(own)}


class Gather:

    def __init__(self, net, chunks, bits=()):
        self.net = net
        self.chunks = chunks
        self.bits = list(bits)
        self.sent = None

    def send(self, steps):
        for step in steps:
            self.land()
            self.sent = (step, [self.net.swap(array, step) for _, array in self.chunks])
        return self

    def land(self, join=True, in_turn=False):
        if self.sent is None:
            return self
        (axis, bit), came = self.sent
        self.sent = None
        if in_turn:
            came = self.net.in_turn(came)
        chunks = []
        if axis == "grp":
            for (masks, array), other in zip(self.chunks, came):
                other_masks = [m ^ (1 << bit) for m in masks]
                if join:
                    chunks.append((masks + other_masks, jnp.concatenate([array, other])))
                else:
                    chunks += [(masks, array), (other_masks, other)]
        else:
            own = self.net.own(axis, bit)
            self.bits = sorted(self.bits + [bit], reverse=True)
            place = 1 + self.bits.index(bit)
            for (masks, array), other in zip(self.chunks, came):
                low = jnp.where(own == 0, array, other)
                high = jnp.where(own == 0, other, array)
                chunks.append((masks, jnp.stack([low, high], axis=place)))
        self.chunks = chunks
        if in_turn:
            self.net.clock = came if axis == "grp" and not join else [a for _, a in chunks]
        return self

    def land_next(self, steps, join=True):
        return self.land(join, True).send(steps)

    def rows(self, low, high):
        chunks = [(masks, array[..., low:high, :]) for masks, array in self.chunks]
        return Gather(self.net, chunks, self.bits)

    def pieces(self):
        return {
            mask: array[n].reshape(-1, array.shape[-1])
            for masks, array in self.chunks
            for n, mask in enumerate(masks)
        }


def gradient_kernel(own_ref, kept_rows, sent_rows, kept_blocks, sent_blocks, kept_ref, sent_ref):
    for rows, blocks, out in (
        (kept_rows, kept_blocks, kept_ref),
        (sent_rows, sent_blocks, sent_ref),
    ):
        for p in range(blocks.shape[0]):
            out[p, 0, 0] = product(rows[0, 0, 0], blocks[p], TRANSPOSED).astype(out.dtype)


def landing_kernel(own_ref, kept_in, sent_in, kept_came, sent_came, kept_ref, sent_ref):
    kept_ref[0, 0] = kept_in[0, 0, 0] + kept_came[0, 0, 0].astype(jnp.float32)
    sent = sent_in[0, 0, 0] + sent_came[0, 0, 0].astype(jnp.float32)
    sent_ref[0, 0] = sent.astype(sent_ref.dtype)


def whole(array):
    zeros = (0,) * array.ndim
    return pl.BlockSpec(array.shape, lambda a, m, own: zeros)


def half(array, other):
    block = (1, 1, 1) + array.shape[3:]
    if array.shape[1] == 1:
        return pl.BlockSpec(block, lambda a, m, own: (a, 0, m, 0, 0))
    if other:
        return pl.BlockSpec(block, lambda a, m, own: (a, 1 - own[0], m, 0, 0))
    return pl.BlockSpec(block, lambda a, m, own: (a, own[0], m, 0, 0))


def halves_call(kernel, grid, specs, out_blocks, out_shape, args, clock):
    def after_clock(own_ref, *refs):
        kernel(own_ref, *refs[len(clock) :])

    later = pl.BlockSpec(memory_space=pl.ANY)
    args = args[:1] + tuple(clock) + args[1:]
    return pl.pallas_call(
        after_clock,
        grid_spec=pltpu.PrefetchScalarGridSpec(
            num_scalar_prefetch=1,
            grid=grid,
            in_specs=[later] * len(clock) + specs,
            out_specs=out_blocks,
        ),
        out_shape=[
            jax.ShapeDtypeStruct(out_shape[0], jnp.float32),
            jax.ShapeDtypeStruct(out_shape[1], jnp.bfloat16),
        ],
        compiler_params=pltpu.CompilerParams(vmem_limit_bytes=40 << 20),
        cost_estimate=pl.CostEstimate(flops=1 << 28, bytes_accessed=1 << 20, transcendentals=0),
    )(*args)


def add_kernel(kept_ref, came_ref, *refs):
    refs[-1][...] = kept_ref[...] + came_ref[...].astype(jnp.float32)


def add_in_turn(kept, came, clock):
    here = pl.BlockSpec(memory_space=pltpu.VMEM)
    return pl.pallas_call(
        add_kernel,
        in_specs=[here, here] + [pl.BlockSpec(memory_space=pl.ANY)] * len(clock),
        out_specs=here,
        out_shape=jax.ShapeDtypeStruct(kept.shape, jnp.float32),
        compiler_params=pltpu.CompilerParams(vmem_limit_bytes=40 << 20),
        cost_estimate=pl.CostEstimate(flops=1 << 20, bytes_accessed=1 << 20, transcendentals=0),
    )(kept, came, *clock)


class Sum:

    def __init__(self, net, grad_rows, blocks, steps, low=0, high=None, clock=()):
        self.net = net
        self.bits = list(range(bits_of(net.dp_size) - 1, -1, -1))
        self.masks = sorted(blocks)
        rows = grad_rows.reshape(net.dp_size, -1, grad_rows.shape[1])[:, low:high]
        axis, bit = steps[-1]
        own = jnp.zeros((1,), jnp.int32)
        kept = sent = jnp.stack([blocks[m] for m in self.masks])
        if axis == "grp":
            kept = jnp.stack([blocks[m] for m in self.masks if not m & (1 << bit)])
            sent = jnp.stack([blocks[m] for m in self.masks if m & (1 << bit)])
            self.masks = [m for m in self.masks if not m & (1 << bit)]
            rows = rows[:, None, None]
        else:
            own = net.own(axis, bit).astype(jnp.int32).reshape(1)
            self.bits.remove(bit)
            rows = rows.reshape((-1, 2, 1 << bit) + rows.shape[1:])
        grid = (rows.shape[0], rows.shape[2])
        pieces, width = kept.shape[:2]
        shape = (pieces,) + grid + (rows.shape[3], width)
        block = pl.BlockSpec(
            (pieces, 1, 1) + shape[3:], lambda a, m, own: (0, a, m, 0, 0)
        )
        self.held, self.outgoing = halves_call(
            gradient_kernel,
            grid,
            [half(rows, False), half(rows, True), whole(kept), whole(sent)],
            [block, block],
            (shape, shape),
            (own, rows, rows, kept, sent),
            clock,
        )
        self.held = self.held.reshape((pieces, -1) + shape[3:])
        self.came = net.swap(self.outgoing, steps[-1])
        for step in steps[-2::-1]:
            self.step(step)

    def step(self, step, clock=()):
        axis, bit = step
        pieces, blocks, rows, width = self.held.shape
        own = jnp.zeros((1,), jnp.int32)
        if axis == "grp":
            high = len({m >> (bit + 1) for m in self.masks})
            self.masks = [m for m in self.masks if not m & (1 << bit)]
            view = (high, 2, -1, rows, width)
        else:
            own = self.net.own(axis, bit).astype(jnp.int32).reshape(1)
            place = self.bits.index(bit)
            self.bits.remove(bit)
            view = (pieces << place, 2, -1, rows, width)
        held = self.held.reshape(view)
        came = self.came.reshape(view)
        grid = (held.shape[0], held.shape[2])
        shape = grid + (rows, width)
        block = pl.BlockSpec((1, 1, rows, width), lambda a, m, own: (a, m, 0, 0))
        self.held, self.outgoing = halves_call(
            landing_kernel,
            grid,
            [half(held, False), half(held, True), half(came, False), half(came, True)],
            [block, block],
            (shape, shape),
            (own, held, held, came, came),
            clock,
        )
        self.held = self.held.reshape((len(self.masks), -1, rows, width))
        self.came = self.net.swap(self.outgoing, step)

    def land_next(self, steps):
        for step in steps[::-1]:
            self.step(step, self.net.clock)
        if steps:
            self.net.clock = [self.outgoing]
        return self

    def owned(self):
        came = self.came.reshape(self.held.shape)
        return (self.held + came.astype(jnp.float32))[0, 0]


def forward_product(blocks, pieces):
    total = None
    for mask, piece in pieces.items():
        term = product(piece, blocks[mask])
        total = term if total is None else total + term
    return total


def backward_product(grad_rows, pieces):
    return [product(pieces[mask], grad_rows, (((0,), (0,)), ((), ()))) for mask in sorted(pieces)]


def local(
    dp_size,
    grp_size,
    tokens,
    cotangent,
    segments,
    positions,
    w_qkv,
    m_qkv,
    v_qkv,
    w_out,
    m_out,
    v_out,
    w_in,
    m_in,
    v_in,
    w_down,
    m_down,
    v_down,
    gains,
    m_gains,
    v_gains,
):
    net = Slice(dp_size, grp_size)
    low = jnp.bfloat16
    qkv_width = w_qkv.shape[1]
    qkv_out = jnp.concatenate([w_qkv.astype(low).T, w_out.astype(low).T])
    qkv_out = Gather(net, [([0], qkv_out[None])]).send(net.far)
    gate = Gather(net, [([0], w_in[0].astype(low).T[None])]).send(net.y)
    up = Gather(net, [([0], w_in[1].astype(low).T[None])]).send(net.x)
    down_low = w_down.astype(low).T[None]
    upstream_low = cotangent[0].T
    upstream_pair = net.pair(upstream_low)

    inputs = tokens[0].T.astype(jnp.float32)
    token_length = inputs.shape[1]
    query_width = QUERY_HEADS * HEAD_SIZE
    key_end = query_width + KEY_VALUE_HEADS * HEAD_SIZE
    head_shape = (KEY_VALUE_HEADS, -1, HEAD_SIZE, token_length)
    own_piece = lax.axis_index("grp")
    query_places = own_piece * token_length + jnp.arange(token_length)
    segment_pieces = segments[0].reshape(grp_size, token_length)
    own_segments = lax.dynamic_index_in_dim(segment_pieces, own_piece, 0, keepdims=False)
    key_masks = [0]
    for axis, bit in net.y + net.core:
        key_masks = key_masks + [m ^ (1 << bit) for m in key_masks]
    key_segments = jnp.concatenate(
        [
            lax.dynamic_index_in_dim(segment_pieces, own_piece ^ m, 0, keepdims=False)
            for m in key_masks
        ]
    )
    key_places = jnp.concatenate(
        [(own_piece ^ m) * token_length + jnp.arange(token_length) for m in key_masks]
    )
    allowed = (key_places[:, None] <= query_places[None, :]) & (
        key_segments[:, None] == own_segments[None, :]
    )
    bias = jnp.where(allowed, 0.0, MASKED)
    rotary_cosine, rotary_sine = rotation(positions[0])
    factor_one = lax.rsqrt(jnp.mean(inputs * inputs, axis=0, keepdims=True) + NORM_EPS)
    plain_one = inputs * factor_one
    normed = (plain_one * gains[0][:, None]).astype(low)
    normed_blocks = net.to_masks(normed)
    normed_pair = net.pair_blocks(normed_blocks)
    qkv_out.land_next(net.near)
    down = Gather(net, [([0], net.in_turn(down_low))]).send(net.far)
    gate.land(True, True)
    up.land(True, True)
    normed_pair = net.in_turn(normed_pair)
    upstream_pair = tie(upstream_pair, normed_pair)
    net.clock = (normed_pair, upstream_pair)
    qkv_out.land(True, True)
    qkv = qkv_out.rows(0, qkv_width).send(net.x)
    out = qkv_out.rows(qkv_width, None).send(net.y)
    gate.chunks = [(masks, net.in_turn(array)) for masks, array in gate.chunks]
    gate.send(net.far)
    down.land_next(net.near)
    out.land_next(net.x)
    qkv.land_next(net.y)
    up.chunks = [(masks, net.in_turn(array)) for masks, array in up.chunks]
    up.send(net.far)
    gate.land_next(net.near)
    down.land_next(net.y)
    out.land(True, True)
    up.land_next(net.near)
    gate.land_next(net.x)
    down.land_next(net.x)
    qkv.land_next(net.core)
    up.land_next(net.y)
    qkv.land(False)
    blended = forward_product(normed_blocks, qkv.pieces())
    rotated = apply_rotary(blended[:key_end], rotary_cosine, rotary_sine).astype(low)
    keys_values = jnp.concatenate([rotated[query_width:], blended[key_end:].astype(low)])[None]
    gate.land(True, True)
    for step in net.y + net.core:
        came = net.swap(keys_values, step)
        if step == net.core[0]:
            came = net.in_turn(came)
        keys_values = jnp.concatenate([keys_values, came], axis=0)
    out.send(net.core)
    gate.send(net.core)

    keys_values = keys_values.reshape(grp_size, -1, HEAD_SIZE, token_length)
    queries = rotated[:query_width].reshape(head_shape)
    attended, log_totals = attend(queries, keys_values, bias)
    attended_low = attended.reshape(query_width, token_length)
    attended_blocks = net.to_masks(attended_low)
    net.clock = attended_blocks
    up.land_next(net.core, False)
    down.land_next(net.core)
    gate, up, down, out = [part.land(False).pieces() for part in (gate, up, down, out)]
    middle = inputs + forward_product(attended_blocks, out)
    factor_two = lax.rsqrt(jnp.mean(middle * middle, axis=0, keepdims=True) + NORM_EPS)
    plain_two = middle * factor_two
    normed_two = (plain_two * gains[1][:, None]).astype(low)
    normed_two_blocks = net.to_masks(normed_two)
    gate_pre = forward_product(normed_two_blocks, gate)
    up_proj = forward_product(normed_two_blocks, up)
    sigmoid_gate = jax.nn.sigmoid(gate_pre)
    activated = gate_pre * sigmoid_gate
    hidden = (activated * up_proj).astype(low)
    hidden_blocks = net.to_masks(hidden)
    layer_out = middle + forward_product(hidden_blocks, down)

    upstream = upstream_low.astype(jnp.float32)
    grad_down = Sum(net, upstream_pair, net.pair_blocks(hidden_blocks), net.x)
    grad_hidden = net.from_masks(backward_product(upstream_low, down))
    grad_gate = (
        grad_hidden * up_proj * sigmoid_gate * (1.0 + gate_pre * (1.0 - sigmoid_gate))
    ).astype(low)
    grad_up = (grad_hidden * activated).astype(low)
    normed_two_pair = net.pair_blocks(normed_two_blocks)
    gate_pair = net.pair(grad_gate)
    up_pair = net.pair(grad_up)
    grad_normed_two = net.from_masks(
        [
            one + two
            for one, two in zip(
                backward_product(grad_gate, gate), backward_product(grad_up, up)
            )
        ]
    )
    back_two, gain_two = norm_back(grad_normed_two, plain_two, factor_two, gains[1])
    grad_middle = upstream + back_two
    middle_low = grad_middle.astype(low)
    attended_gradient = net.from_masks(backward_product(middle_low, out))
    outgoing = [grad_down.outgoing]
    attended_gradient = attended_gradient.astype(low).reshape(head_shape)
    grad_queries, grad_keys, grad_values = attend_back(
        queries, keys_values, bias, log_totals, attended_gradient, outgoing
    )
    grad_keys_values = jnp.concatenate([grad_keys, grad_values], axis=1).reshape(
        grp_size, -1, token_length
    )
    net.clock = [grad_keys_values]
    for step in net.core + net.y[::-1]:
        half = grad_keys_values.shape[0] // 2
        came = net.swap(grad_keys_values[half:].astype(low), step)
        if step == net.y[-1]:
            grad_in_up = Sum(net, up_pair, normed_two_pair, net.y, clock=net.clock)
            net.clock = [grad_in_up.outgoing]
            grad_in_gate = Sum(net, gate_pair, normed_two_pair, net.x, clock=net.clock)
            net.clock = [grad_in_gate.outgoing]
            grad_down.land_next(net.near)
        grad_keys_values = add_in_turn(grad_keys_values[:half], came, net.clock)
        net.clock = [grad_keys_values]
    grad_queries = grad_queries.reshape(query_width, token_length)
    grad_keys_values = grad_keys_values[0]
    key_width = key_end - query_width
    grad_mixed = jnp.concatenate(
        [
            inverse_rotary(grad_queries, rotary_cosine, rotary_sine),
            inverse_rotary(grad_keys_values[:key_width], rotary_cosine, rotary_sine),
            grad_keys_values[key_width:],
        ]
    ).astype(low)
    net.clock = [grad_mixed]
    mixed_pair = net.pair(grad_mixed)
    middle_pair = net.pair(middle_low)
    attended_pair = net.pair_blocks(attended_blocks)
    cut = qkv_width // 16 * 8
    first_qkv = Sum(net, mixed_pair, normed_pair, net.y, 0, cut, net.clock)
    second_qkv = Sum(net, mixed_pair, normed_pair, net.x, cut, None, net.clock)
    net.clock = [first_qkv.outgoing, second_qkv.outgoing]
    grad_down.land_next(net.far)
    grad_in_up.land_next(net.near)
    grad_normed = net.from_masks(backward_product(grad_mixed, qkv.pieces()))
    back_one, gain_one = norm_back(grad_normed, plain_one, factor_one, gains[0])
    tokens_grad = grad_middle + back_one
    gain_grads = jnp.stack([gain_one, gain_two])

    def gain_steps(gain_grads, steps):
        for step in steps:
            gain_grads = add_in_turn(gain_grads, net.swap(gain_grads, step), net.clock)
            net.clock = [gain_grads]
        return gain_grads

    second_qkv.land_next(net.y)
    first_qkv.land_next(net.x)
    grad_out = Sum(net, middle_pair, attended_pair, net.x, clock=net.clock)
    net.clock = [grad_out.outgoing]
    grad_in_gate.land_next(net.y)
    grad_down.land_next(net.y)
    grad_in_up.land_next(net.far)
    gain_grads = gain_steps(gain_grads, net.core)
    second_qkv.land_next(net.near)
    first_qkv.land_next(net.near)
    grad_out.land_next(net.y)
    grad_in_gate.land_next(net.near)
    grad_in_up.land_next(net.x)
    gain_grads = gain_steps(gain_grads, net.y)
    second_qkv.land_next(net.far)
    first_qkv.land_next(net.far)
    grad_out.land_next(net.near)
    gain_grads = gain_steps(gain_grads, net.x)
    grad_in_gate.land_next(net.far)
    grad_out.land_next(net.far)
    gain_grads = gain_steps(gain_grads, net.near + net.far)
    owned_down = grad_down.owned()
    owned_out = grad_out.owned()
    owned_qkv = jnp.concatenate([first_qkv.owned(), second_qkv.owned()])
    owned_in = jnp.stack([grad_in_gate.owned(), grad_in_up.owned()])
    new_qkv, mom_qkv, sq_qkv = adamw_update(
        w_qkv, m_qkv, v_qkv, owned_qkv.T, RATE_MATRIX, WEIGHT_DECAY
    )
    new_out, mom_out, sq_out = adamw_update(
        w_out, m_out, v_out, owned_out.T, RATE_MATRIX, WEIGHT_DECAY
    )
    new_in, mom_in, sq_in = adamw_update(
        w_in, m_in, v_in, owned_in.transpose(0, 2, 1), RATE_MATRIX, WEIGHT_DECAY
    )
    new_down, mom_down, sq_down = adamw_update(
        w_down, m_down, v_down, owned_down.T, RATE_MATRIX, WEIGHT_DECAY
    )
    new_gains, mom_gains, sq_gains = adamw_update(
        gains, m_gains, v_gains, gain_grads, RATE_GAIN, 0.0
    )
    return (
        layer_out.T[None],
        tokens_grad.T[None],
        new_qkv,
        mom_qkv,
        sq_qkv,
        new_out,
        mom_out,
        sq_out,
        new_in,
        mom_in,
        sq_in,
        new_down,
        mom_down,
        sq_down,
        new_gains,
        mom_gains,
        sq_gains,
    )


def solution(mesh):
    return jax.shard_map(
        partial(local, mesh.shape["dp"], mesh.shape["grp"]),
        mesh=mesh,
        in_specs=(
            P("dp", "grp", None),
            P("dp", "grp", None),
            P("dp", None),
            P("dp", "grp"),
            P("grp", "dp"),
            P("grp", "dp"),
            P("grp", "dp"),
            P("grp", "dp"),
            P("grp", "dp"),
            P("grp", "dp"),
            P(None, "grp", "dp"),
            P(None, "grp", "dp"),
            P(None, "grp", "dp"),
            P("grp", "dp"),
            P("grp", "dp"),
            P("grp", "dp"),
            P(),
            P(),
            P(),
        ),
        out_specs=(
            P("dp", "grp", None),
            P("dp", "grp", None),
            P("grp", "dp"),
            P("grp", "dp"),
            P("grp", "dp"),
            P("grp", "dp"),
            P("grp", "dp"),
            P("grp", "dp"),
            P(None, "grp", "dp"),
            P(None, "grp", "dp"),
            P(None, "grp", "dp"),
            P("grp", "dp"),
            P("grp", "dp"),
            P("grp", "dp"),
            P(),
            P(),
            P(),
        ),
        check_vma=False,
    )
```
